128 devices in a mesh: dp: 32 (over x_lo, z, y), tensor: 4 (over x_hi, core).
Axes of the slice: x: 4 (x_hi: 2, x_lo: 2; x = x_hi * 2 + x_lo), y: 4, z: 4, core: 2. Of those that a mesh axis runs over, the one named last changes fastest.
Arguments:
- layer_input: bfloat16 [16384, 2048], P(('dp', 'tensor')), may hold values from -6 to 6
- teacher_out: bfloat16 [16384, 2048], P(('dp', 'tensor')), may hold values from -6 to 6
- lengths: int32 [32, 2], replicated, may hold values from 64 to 448, as said below
- norm1_gain: bfloat16 [2048], P('dp'), may hold values from 0.5 to 1.5
- query_weight: bfloat16 [2048, 1024], P('dp', 'tensor'), may hold values from -0.125 to 0.125
- key_weight: bfloat16 [2048, 1024], P('dp', 'tensor'), may hold values from -0.125 to 0.125
- value_weight: bfloat16 [2048, 2048], P('dp', 'tensor'), may hold values from -0.125 to 0.125
- output_gate: bfloat16 [2048, 2048], P('dp', 'tensor'), may hold values from -0.125 to 0.125
- beta_weight: bfloat16 [2048, 8], P('dp', 'tensor'), may hold values from -0.125 to 0.125
- decay_weight: bfloat16 [2048, 8], P('dp', 'tensor'), may hold values from -0.125 to 0.125
- decay_log: float32 [8], P('tensor'), may hold values from 0 to 2.7
- step_bias: float32 [8], P('tensor'), may hold values from -6 to -1
- query_taps: bfloat16 [4, 1024], P(None, 'tensor'), may hold values from -3 to 3
- key_taps: bfloat16 [4, 1024], P(None, 'tensor'), may hold values from -3 to 3
- value_taps: bfloat16 [4, 2048], P(None, 'tensor'), may hold values from -3 to 3
- mixer_gain: bfloat16 [256], replicated, may hold values from 0.5 to 1.5
- out_weight: bfloat16 [2048, 2048], P('dp', 'tensor'), may hold values from -0.125 to 0.125
- norm2_gain: bfloat16 [2048], P('dp'), may hold values from 0.5 to 1.5
- gate_weight: bfloat16 [2048, 5632], P('dp', 'tensor'), may hold values from -0.125 to 0.125
- up_weight: bfloat16 [2048, 5632], P('dp', 'tensor'), may hold values from -0.125 to 0.125
- down_weight: bfloat16 [2048, 5632], P('dp', 'tensor'), may hold values from -0.078125 to 0.078125
Outputs:
- layer_out: float32 [16384, 2048], P(('dp', 'tensor'))
- grad_input: float32 [16384, 2048], P(('dp', 'tensor'))
- grad_norm1_gain: float32 [2048], P('dp')
- grad_query_weight: float32 [2048, 1024], P('dp', 'tensor')
- grad_key_weight: float32 [2048, 1024], P('dp', 'tensor')
- grad_value_weight: float32 [2048, 2048], P('dp', 'tensor')
- grad_output_gate: float32 [2048, 2048], P('dp', 'tensor')
- grad_beta_weight: float32 [2048, 8], P('dp', 'tensor')
- grad_decay_weight: float32 [2048, 8], P('dp', 'tensor')
- grad_decay_log: float32 [8], P('tensor')
- grad_step_bias: float32 [8], P('tensor')
- grad_query_taps: float32 [4, 1024], P(None, 'tensor')
- grad_key_taps: float32 [4, 1024], P(None, 'tensor')
- grad_value_taps: float32 [4, 2048], P(None, 'tensor')
- grad_mixer_gain: float32 [256], replicated
- grad_out_weight: float32 [2048, 2048], P('dp', 'tensor')
- grad_norm2_gain: float32 [2048], P('dp')
- grad_gate_weight: float32 [2048, 5632], P('dp', 'tensor')
- grad_up_weight: float32 [2048, 5632], P('dp', 'tensor')
- grad_down_weight: float32 [2048, 5632], P('dp', 'tensor')
The draws below stay inside these ranges and needn't reach their ends.
Inputs may be any that keep to these rules, and one draw needn't show every extreme that they name: Each group's lengths sum to at most 512; one of its two sequences, in a place drawn from the seed, starts within the group's first 128 positions and ends within its last 128.
All inputs are finite; a program needn't handle non-finite values.
Results may differ from the reference program's by a relative error of at most 0.025.
Values may be sent and summed in bfloat16 or wider, within the bound.
No kernel may reach another device: no remote copies, remote signals or barrier semaphores. Data moves between devices by JAX's collectives and lax.ppermute only.
A program may use at most 192 MiB of HBM per device.

```python
import jax
import jax.numpy as jnp
from jax import lax

D = 2048
H = 8
DK = 128
DV = 256
FF = 5632
CONV = 4
SPAN = 64
TOK_DEV = 128
KD = 1024
VD = 2048
GROUP = 512
TOKENS = 16384
N_DP = 32


def draw_lengths(key, part):
    key = jax.random.fold_in(key, 7)
    keys_split = jax.random.split(key, 4)
    padding = jax.random.randint(keys_split[0], (N_DP,), 0, max(TOK_DEV // 4, 1))
    shorter = jax.random.randint(keys_split[1], (N_DP,), TOK_DEV // 2, TOK_DEV - padding)
    placed = jax.random.randint(keys_split[2], (N_DP,), 0, 2)
    fullest = jax.random.randint(keys_split[3], (), 0, N_DP)
    picked = jnp.arange(N_DP, dtype=jnp.int32) == fullest
    padding = jnp.where(picked, 0, padding)
    shorter = jnp.where(picked, TOK_DEV // 2, shorter)
    longer = GROUP - padding - shorter
    first = jnp.where(placed == 0, longer, shorter)
    second = jnp.where(placed == 0, shorter, longer)
    return jnp.stack([first, second], axis=1).astype(jnp.int32)


def block_levels(own_key, extent, cuts, low, largest):
    level = 1.0
    for axis_at, parts in cuts:
        draws = jax.random.uniform(jax.random.fold_in(jax.random.fold_in(own_key, 6), axis_at), (parts,), jnp.float32, low / len(cuts), largest / len(cuts))
        level = level * jnp.repeat(jnp.exp(draws), extent[axis_at] // parts).reshape((-1,) + (1,) * (len(extent) - 1 - axis_at))
    return level


def bell_draw(own_key, shape, spread, bound, cuts=(), kind=jnp.bfloat16):
    loudness = block_levels(own_key, shape, cuts, -0.22, 0.18) if cuts else 1.0
    drawn = jax.random.normal(own_key, shape, jnp.float32) * spread * loudness
    return jnp.minimum(jnp.maximum(drawn, -bound), bound).astype(kind)


def setup_inputs(seed: int = 0) -> dict:
    splits = jax.random.split(jax.random.key(seed), 22)
    return {
        "layer_input": bell_draw(splits[0], (TOKENS, D), 1.0, 6.0, ((0, 128),)),
        "teacher_out": bell_draw(splits[1], (TOKENS, D), 1.0, 6.0, ((0, 128),)),
        "lengths": draw_lengths(jax.random.fold_in(splits[21], 71), 0),
        "norm1_gain": jnp.clip(1.0 + 0.1 * jax.random.normal(splits[3], (D,), jnp.float32), 0.5, 1.5).astype(jnp.bfloat16),
        "query_weight": bell_draw(splits[4], (D, KD), D ** -0.5, 0.125, ((0, 32), (1, 4))),
        "key_weight": bell_draw(splits[5], (D, KD), D ** -0.5, 0.125, ((0, 32), (1, 4))),
        "value_weight": bell_draw(splits[6], (D, VD), D ** -0.5, 0.125, ((0, 32), (1, 4))),
        "output_gate": bell_draw(splits[7], (D, VD), D ** -0.5, 0.125, ((0, 32), (1, 4))),
        "beta_weight": bell_draw(splits[8], (D, H), D ** -0.5, 0.125, ((0, 32), (1, 4))),
        "decay_weight": bell_draw(splits[9], (D, H), D ** -0.5, 0.125, ((0, 32), (1, 4))),
        "decay_log": jnp.clip(2.7 * jax.random.uniform(splits[10], (H,), jnp.float32) ** block_levels(splits[10], (H,), ((0, 4),), -0.2, 0.2), 0.0, 2.7),
        "step_bias": jnp.clip(-6.0 + 5.0 * jax.random.uniform(splits[11], (H,), jnp.float32) ** block_levels(splits[11], (H,), ((0, 4),), -0.2, 0.2), -6.0, -1.0),
        "query_taps": bell_draw(splits[12], (CONV, KD), CONV ** -0.5, 3.0, ((1, 4),)),
        "key_taps": bell_draw(splits[13], (CONV, KD), CONV ** -0.5, 3.0, ((1, 4),)),
        "value_taps": bell_draw(splits[14], (CONV, VD), CONV ** -0.5, 3.0, ((1, 4),)),
        "mixer_gain": jnp.clip(1.0 + 0.1 * jax.random.normal(splits[15], (DV,), jnp.float32), 0.5, 1.5).astype(jnp.bfloat16),
        "out_weight": bell_draw(splits[16], (D, VD), VD ** -0.5, 0.125, ((0, 32), (1, 4))),
        "norm2_gain": jnp.clip(1.0 + 0.1 * jax.random.normal(splits[17], (D,), jnp.float32), 0.5, 1.5).astype(jnp.bfloat16),
        "gate_weight": bell_draw(splits[18], (D, FF), D ** -0.5, 0.125, ((0, 32), (1, 4))),
        "up_weight": bell_draw(splits[19], (D, FF), D ** -0.5, 0.125, ((0, 32), (1, 4))),
        "down_weight": bell_draw(splits[20], (D, FF), FF ** -0.5, 0.078125, ((0, 32), (1, 4))),
    }


EPSILON = 1e-06
MIXER_FLOOR = 0.001
HIGHEST = lax.Precision.HIGHEST

@jax.custom_vjp
def low(v):
    return lax.optimization_barrier(v.astype(jnp.bfloat16)).astype(jnp.float32)

@jax.custom_vjp
def low_back(v):
    return v

def low_keep(v):
    return (low(v), None)

def low_pass(kept, grad):
    return (grad,)

def back_keep(v):
    return (v, None)

def back_low(kept, grad):
    return (low(grad),)
low.defvjp(low_keep, low_pass)
low_back.defvjp(back_keep, back_low)

def matmul(left, right):
    return jnp.dot(left, right, precision=HIGHEST, preferred_element_type=jnp.float32)

def causal_conv(values, kernel_taps, seg_ids):
    taps_count = kernel_taps.shape[0]
    columns = values.shape[1]
    summed = values * kernel_taps[taps_count - 1][None, :]
    for offset in range(1, taps_count):
        moved = jnp.concatenate([jnp.zeros((offset, columns), values.dtype), values[:-offset]], axis=0)
        earlier = jnp.concatenate([jnp.full((offset,), -1, jnp.int32), seg_ids[:-offset].astype(jnp.int32)], axis=0)
        matches = (earlier == seg_ids.astype(jnp.int32)).astype(values.dtype)
        summed = summed + kernel_taps[taps_count - 1 - offset][None, :] * moved * matches[:, None]
    return jax.nn.silu(summed)

def unit_rows(values):
    return values * lax.rsqrt(lax.optimization_barrier(jnp.sum(values * values, axis=-1, keepdims=True)) + EPSILON)

def gated_norm(mixed_rows, gain, gate_rows):
    scaled = mixed_rows * lax.rsqrt(lax.optimization_barrier(jnp.mean(mixed_rows * mixed_rows, axis=-1, keepdims=True)) + MIXER_FLOOR)
    return scaled * gain * jax.nn.silu(gate_rows)

def segment_ids(lens, row_count):
    boundary = jnp.cumsum(lens).astype(jnp.int32)
    positions = jnp.arange(row_count, dtype=jnp.int32)
    return lax.optimization_barrier(jnp.sum((positions[:, None] >= boundary[None, :]).astype(jnp.int32), axis=1)).astype(jnp.int32)

def token_step(state_now, inputs):
    query_row, key_row, value_row, beta_row, decay_row, begins = inputs
    keep_rate = jnp.exp(decay_row) * (1.0 - begins)
    recalled = jnp.einsum('hvk,hk->hv', state_now, key_row, precision=HIGHEST)
    written = beta_row[:, None] * (value_row - keep_rate[:, None] * recalled)
    updated = keep_rate[:, None, None] * state_now + written[:, :, None] * key_row[:, None, :]
    output_row = jnp.einsum('hvk,hk->hv', updated, query_row, precision=HIGHEST)
    return (updated, output_row)

def block_scan(state_now, inputs):
    return lax.scan(token_step, state_now, inputs)

def delta_rule(queries, keys_unit, values, beta_rates, decays, begins):
    row_count = queries.shape[0]
    blocks = row_count // SPAN
    shaped = tuple((member.reshape((blocks, SPAN) + member.shape[1:]) for member in (queries, keys_unit, values, beta_rates, decays, begins)))
    initial = jnp.zeros((H, DV, DK), queries.dtype)
    last_state, outputs = lax.scan(jax.checkpoint(block_scan), initial, shaped)
    return outputs.reshape(row_count, H, DV)

def group_forward(params, rows_in, lens):
    norm1_gain, query_weight, key_weight, value_weight, output_gate, beta_weight, decay_weight, decay_log, step_bias, query_taps, key_taps, value_taps, mixer_gain, out_weight, norm2_gain, gate_weight, up_weight, down_weight = params
    row_count = rows_in.shape[0]
    seg_ids = segment_ids(lens, row_count)
    earlier = jnp.concatenate([jnp.full((1,), -1, jnp.int32), seg_ids[:-1]])
    begins = (earlier != seg_ids).astype(rows_in.dtype)
    scale_one = lax.rsqrt(lax.optimization_barrier(jnp.mean(rows_in * rows_in, axis=-1, keepdims=True)) + EPSILON)
    normed_one = low(rows_in * scale_one * norm1_gain)
    query_raw = low_back(matmul(normed_one, query_weight))
    key_raw = low_back(matmul(normed_one, key_weight))
    value_raw = low_back(matmul(normed_one, value_weight))
    gate_raw = low_back(matmul(normed_one, output_gate))
    beta_raw = low_back(matmul(normed_one, beta_weight))
    decay_raw = low_back(matmul(normed_one, decay_weight))
    queries = unit_rows(causal_conv(query_raw, query_taps, seg_ids).reshape(row_count, H, DK)) * DK ** (-0.5)
    keys_unit = unit_rows(causal_conv(key_raw, key_taps, seg_ids).reshape(row_count, H, DK))
    values = causal_conv(value_raw, value_taps, seg_ids).reshape(row_count, H, DV)
    beta_rates = jax.nn.sigmoid(beta_raw)
    decays = -jnp.exp(decay_log)[None, :] * jax.nn.softplus(decay_raw + step_bias[None, :])
    mixed_rows = delta_rule(queries, keys_unit, values, beta_rates, decays, begins)
    gated_rows = gated_norm(mixed_rows, mixer_gain, gate_raw.reshape(row_count, H, DV)).reshape(row_count, H * DV)
    branch_one = low_back(matmul(low(gated_rows), out_weight.T))
    hidden = rows_in + branch_one
    scale_two = lax.rsqrt(lax.optimization_barrier(jnp.mean(hidden * hidden, axis=-1, keepdims=True)) + EPSILON)
    normed_two = low(hidden * scale_two * norm2_gain)
    gate_in = low_back(matmul(normed_two, gate_weight))
    up_in = low_back(matmul(normed_two, up_weight))
    act_low = low(jax.nn.silu(gate_in) * up_in)
    branch_two = low_back(matmul(act_low, down_weight.T))
    return hidden + branch_two

def reference(layer_input, teacher_out, lengths, norm1_gain, query_weight, key_weight, value_weight, output_gate, beta_weight, decay_weight, decay_log, step_bias, query_taps, key_taps, value_taps, mixer_gain, out_weight, norm2_gain, gate_weight, up_weight, down_weight):
    params = tuple((member.astype(jnp.float32) for member in (norm1_gain, query_weight, key_weight, value_weight, output_gate, beta_weight, decay_weight, decay_log, step_bias, query_taps, key_taps, value_taps, mixer_gain, out_weight, norm2_gain, gate_weight, up_weight, down_weight)))
    rows_all = layer_input.astype(jnp.float32).reshape(N_DP, GROUP, D)
    teacher = teacher_out.astype(jnp.float32).reshape(N_DP, GROUP, D)
    positions = jnp.arange(GROUP, dtype=jnp.int32)
    lengths_int = lengths.astype(jnp.int32)
    totals = lax.optimization_barrier(jnp.sum(lengths_int, axis=1)).astype(jnp.int32)
    validity = (positions[None, :] < totals[:, None]).astype(jnp.float32)[:, :, None]
    count = jnp.sum(lengths_int).astype(jnp.float32)

    def objective(weights, inputs):

        def one_group(pair):
            return group_forward(weights, pair[0], pair[1])
        outputs = lax.map(jax.checkpoint(one_group), (inputs, lengths_int))
        error = (outputs - teacher) * validity
        loss = jnp.float32(TOKENS) / count * 0.5 * jnp.sum(error * error)
        return (loss, outputs)
    loss, pullback, outputs = jax.vjp(objective, params, rows_all, has_aux=True)
    grads, grad_rows = pullback(jnp.ones_like(loss))
    return (outputs.reshape(TOKENS, D), grad_rows.reshape(TOKENS, D), grads[0], grads[1], grads[2], grads[3], grads[4], grads[5], grads[6], grads[7], grads[8], grads[9], grads[10], grads[11], grads[12], grads[13], grads[14], grads[15], grads[16], grads[17])
```

```python
from functools import partial

import jax
import jax.numpy as jnp
from jax import lax
from jax.sharding import Mesh, PartitionSpec as P

H = 8
DK = 128
DV = 256
CONV = 4
SPAN = 64


EPSILON = 1e-06
MIXER_FLOOR = 0.001
HIGHEST = lax.Precision.HIGHEST


def causal_conv(values, kernel_taps, seg_ids):
    taps_count = kernel_taps.shape[0]
    columns = values.shape[1]
    summed = values * kernel_taps[taps_count - 1][None, :]
    for offset in range(1, taps_count):
        moved = jnp.concatenate(
            [jnp.zeros((offset, columns), values.dtype), values[:-offset]], axis=0
        )
        earlier = jnp.concatenate([jnp.full((offset,), -1, jnp.int32), seg_ids[:-offset]], axis=0)
        matches = (earlier == seg_ids).astype(values.dtype)
        summed = summed + kernel_taps[taps_count - 1 - offset][None, :] * moved * matches[:, None]
    return jax.nn.silu(summed)


def unit_rows(values):
    return values * lax.rsqrt(jnp.sum(values * values, axis=-1, keepdims=True) + EPSILON)


def gated_norm(mixed_rows, gain, gate_rows):
    scaled = mixed_rows * lax.rsqrt(
        jnp.mean(mixed_rows * mixed_rows, axis=-1, keepdims=True) + MIXER_FLOOR
    )
    return scaled * gain * jax.nn.silu(gate_rows)


def block_step(state_now, inputs):
    query_block, key_block, value_block, beta_block, decay_block, seg_block, seg_prior = inputs
    length = seg_block.shape[0]
    row_index = lax.broadcasted_iota(jnp.int32, (length, length), 0)
    col_index = lax.broadcasted_iota(jnp.int32, (length, length), 1)
    causal = (seg_block[:, None] == seg_block[None, :]) & (col_index <= row_index)
    strict = causal & (col_index < row_index)
    cumulative = jnp.cumsum(decay_block, axis=-1)
    spread = jnp.where(causal[None], cumulative[:, :, None] - cumulative[:, None, :], 0.0)
    ratio = jnp.exp(spread) * causal[None].astype(jnp.float32)
    carry_in = (seg_block == seg_prior).astype(jnp.float32)
    growth = jnp.exp(cumulative) * carry_in[None, :]
    key_inner = jnp.einsum("hik,hjk->hij", key_block, key_block, precision=HIGHEST)
    lower_part = jnp.where(strict[None], beta_block[:, :, None] * ratio * key_inner, 0.0)
    recalled = jnp.einsum("hik,hvk->hiv", key_block, state_now, precision=HIGHEST)
    target_rows = beta_block[:, :, None] * (value_block - growth[:, :, None] * recalled)
    system = lower_part + jnp.eye(length, dtype=jnp.float32)[None]
    written = jax.scipy.linalg.solve_triangular(system, target_rows, lower=True, unit_diagonal=True)
    scores = jnp.einsum("hik,hjk->hij", query_block, key_block, precision=HIGHEST) * ratio
    outputs = growth[:, :, None] * jnp.einsum(
        "hik,hvk->hiv", query_block, state_now, precision=HIGHEST
    )
    outputs = outputs + jnp.einsum("hij,hjv->hiv", scores, written, precision=HIGHEST)
    fading = ratio[:, length - 1, :]
    new_state = growth[:, length - 1][:, None, None] * state_now
    new_state = new_state + jnp.einsum(
        "hjv,hjk->hvk", fading[:, :, None] * written, key_block, precision=HIGHEST
    )
    return (new_state, outputs)


def mixer_core(
    seg_ids,
    seg_before,
    query_raw,
    key_raw,
    value_raw,
    gate_raw,
    beta_raw,
    decay_raw,
    conv_query,
    conv_key,
    conv_value,
    decay_log,
    step_bias,
    mixer_gain,
):
    row_count = query_raw.shape[0]
    heads_here = decay_log.shape[0]
    blocks = row_count // SPAN
    queries = unit_rows(
        causal_conv(query_raw, conv_query, seg_ids).reshape(row_count, heads_here, DK)
    ) * DK ** (-0.5)
    keys_unit = unit_rows(
        causal_conv(key_raw, conv_key, seg_ids).reshape(row_count, heads_here, DK)
    )
    values = causal_conv(value_raw, conv_value, seg_ids).reshape(row_count, heads_here, DV)
    beta_rates = jax.nn.sigmoid(beta_raw)
    decays = -jnp.exp(decay_log)[None, :] * jax.nn.softplus(decay_raw + step_bias[None, :])

    def heads_first(member_array):
        return jnp.swapaxes(member_array.reshape((blocks, SPAN) + member_array.shape[1:]), 1, 2)

    seg_blocks = seg_ids.reshape(blocks, SPAN)
    initial = jnp.zeros((heads_here, DV, DK), jnp.float32)
    ignored, outputs = lax.scan(
        jax.checkpoint(block_step),
        initial,
        (
            heads_first(queries),
            heads_first(keys_unit),
            heads_first(values),
            heads_first(beta_rates),
            heads_first(decays),
            seg_blocks,
            seg_before,
        ),
    )
    mixed_rows = jnp.swapaxes(outputs, 1, 2).reshape(row_count, heads_here, DV)
    gated_rows = gated_norm(mixed_rows, mixer_gain, gate_raw.reshape(row_count, heads_here, DV))
    return gated_rows.reshape(row_count, heads_here * DV)


SWAP = [(0, 1), (1, 0)]
PLANE = ("z", "y")
SMALL = 128


def trade(values, axis):
    return lax.ppermute(values, axis, SWAP)


def paired(own, other, index, axis):
    first = jnp.where(index == 0, own, other)
    second = jnp.where(index == 0, other, own)
    return jnp.stack([first, second], axis=axis)


def gather_tokens(own):
    rows, columns = own.shape
    pair = paired(own, trade(own, "xh"), lax.axis_index("xh"), 0)
    full = paired(pair, trade(pair, "c"), lax.axis_index("c"), 1)
    return full.reshape(4 * rows, columns)


def scatter_tokens(terms):
    rows = terms.shape[0] // 4
    columns = terms.shape[1]
    core = lax.axis_index("c")
    half = lax.axis_index("xh")
    parts = terms.reshape(2, 2, rows, columns)
    kept = lax.dynamic_index_in_dim(parts, core, 1, keepdims=False)
    sent = lax.dynamic_index_in_dim(parts, 1 - core, 1, keepdims=False).astype(jnp.bfloat16)
    summed = kept + trade(sent, "c").astype(jnp.float32)
    kept = lax.dynamic_index_in_dim(summed, half, 0, keepdims=False)
    sent = lax.dynamic_index_in_dim(summed, 1 - half, 0, keepdims=False).astype(jnp.bfloat16)
    return kept + trade(sent, "xh").astype(jnp.float32)


def gather_weights(block):
    both = jnp.stack([block, trade(block, "xl")], axis=0)
    full = lax.all_gather(both, PLANE, axis=0, tiled=False)
    return full.reshape(-1, block.shape[1])


def scatter_grads(grads):
    columns = grads.shape[1]
    both = lax.psum_scatter(grads, PLANE, scatter_dimension=0, tiled=True)
    both = both.reshape(2, -1, columns)
    return both[0].astype(jnp.float32) + trade(both[1], "xl").astype(jnp.float32)


def features_in(rows):
    count = rows.shape[0]
    halves = rows.reshape(count, 2, -1)
    flip = lax.axis_index("xl") == 1
    first = jnp.where(flip, halves[:, 1], halves[:, 0]).reshape(count, 16, 64)
    second = jnp.where(flip, halves[:, 0], halves[:, 1]).reshape(count, 16, 64)
    return jnp.concatenate([first, second], axis=2).reshape(count, -1)


def features_out(rows):
    count = rows.shape[0]
    blocks = rows.reshape(count, 16, 2, 64)
    flip = lax.axis_index("xl") == 1
    first = blocks[:, :, 0].reshape(count, -1)
    second = blocks[:, :, 1].reshape(count, -1)
    low = jnp.where(flip, second, first)
    high = jnp.where(flip, first, second)
    return jnp.concatenate([low, high], axis=1)


def sum_over(values, axes):
    for axis in axes:
        size = lax.axis_size(axis)
        step = 1
        while step < size:
            values = values + lax.ppermute(values, axis, [(i, i ^ step) for i in range(size)])
            step *= 2
    return values


def product(left, right):
    return jnp.dot(left, right, preferred_element_type=jnp.float32)


def product_t(left, right):
    return jnp.einsum("gf,df->gd", left, right, preferred_element_type=jnp.float32)


def t_product(left, right):
    return jnp.einsum(
        "gd,gf->df", left, right, preferred_element_type=jnp.float32
    ).astype(jnp.bfloat16)


def shards(
    layer_input,
    teacher_out,
    lengths,
    norm1_gain,
    query_weight,
    key_weight,
    value_weight,
    output_gate,
    beta_weight,
    decay_weight,
    decay_log,
    step_bias,
    query_taps,
    key_taps,
    value_taps,
    mixer_gain,
    out_weight,
    norm2_gain,
    gate_weight,
    up_weight,
    down_weight,
):
    tok_rows = layer_input.shape[0]
    group_rows = 4 * tok_rows
    all_rows = 32 * group_rows
    rows_dp = norm1_gain.shape[0]
    group_index = lax.axis_index("xl") * 16 + lax.axis_index("z") * 4 + lax.axis_index("y")
    tensor_index = lax.axis_index("xh") * 2 + lax.axis_index("c")
    heads_here = decay_log.shape[0]
    own_lengths = lax.dynamic_index_in_dim(lengths, group_index, 0, keepdims=False)
    boundary = jnp.cumsum(own_lengths)
    positions = jnp.arange(group_rows, dtype=jnp.int32)
    seg_ids = jnp.sum((positions[:, None] >= boundary[None, :]).astype(jnp.int32), axis=1)
    seg_before = jnp.concatenate([jnp.full((1,), -1, jnp.int32), seg_ids[SPAN - 1 : -1 : SPAN]])
    own_rows = tensor_index * tok_rows + jnp.arange(tok_rows, dtype=jnp.int32)
    validity = (own_rows < boundary[-1]).astype(jnp.float32)[:, None]
    loss_scale = jnp.float32(all_rows) / jnp.sum(lengths).astype(jnp.float32)

    filler = jnp.zeros((rows_dp, SMALL - 2 * heads_here - 2), jnp.bfloat16)
    mixer_block = jnp.concatenate(
        [
            query_weight,
            key_weight,
            value_weight,
            output_gate,
            beta_weight,
            decay_weight,
            norm1_gain[:, None],
            norm2_gain[:, None],
            filler,
            out_weight,
        ],
        axis=1,
    )
    ffn_block = jnp.concatenate([gate_weight, up_weight, down_weight], axis=1)
    mixer_full = gather_weights(mixer_block)
    ffn_full = gather_weights(ffn_block)
    input_own = features_in(layer_input)
    teacher_own = features_in(teacher_out).astype(jnp.float32)
    input_all = gather_tokens(input_own)

    qk_width = query_taps.shape[1]
    v_width = value_taps.shape[1]
    f_width = gate_weight.shape[1]
    proj_width = 2 * qk_width + 2 * v_width
    proj_full = mixer_full[:, : proj_width + SMALL]
    outw_full = mixer_full[:, proj_width + SMALL :]
    gains = mixer_full[:, proj_width : proj_width + SMALL].T.astype(jnp.float32)
    gain_first = gains[2 * heads_here][None, :]
    gain_second = gains[2 * heads_here + 1][None, :]
    gate_up_full = ffn_full[:, : 2 * f_width]
    down_full = ffn_full[:, 2 * f_width :]

    input_float = input_own.astype(jnp.float32)
    scale_one = lax.rsqrt(jnp.mean(input_float * input_float, axis=-1, keepdims=True) + EPSILON)
    every = input_all.astype(jnp.float32)
    scale_all = lax.rsqrt(jnp.mean(every * every, axis=-1, keepdims=True) + EPSILON)
    normed_one = (every * scale_all * gain_first).astype(jnp.bfloat16)

    raw = product(normed_one, proj_full)
    query_raw = raw[:, :qk_width]
    key_raw = raw[:, qk_width : 2 * qk_width]
    value_raw = raw[:, 2 * qk_width : 2 * qk_width + v_width]
    gate_raw = raw[:, 2 * qk_width + v_width : proj_width]
    beta_raw = raw[:, proj_width : proj_width + heads_here]
    decay_raw = raw[:, proj_width + heads_here : proj_width + 2 * heads_here]
    core = partial(mixer_core, seg_ids, seg_before)
    gated_rows, pullback = jax.vjp(
        core,
        query_raw,
        key_raw,
        value_raw,
        gate_raw,
        beta_raw,
        decay_raw,
        query_taps.astype(jnp.float32),
        key_taps.astype(jnp.float32),
        value_taps.astype(jnp.float32),
        decay_log,
        step_bias,
        mixer_gain.astype(jnp.float32),
    )
    gated_low = gated_rows.astype(jnp.bfloat16)
    hidden = input_float + scatter_tokens(product_t(gated_low, outw_full))
    scale_two = lax.rsqrt(jnp.mean(hidden * hidden, axis=-1, keepdims=True) + EPSILON)
    normed_two = gather_tokens((hidden * scale_two * gain_second).astype(jnp.bfloat16))
    gate_up = product(normed_two, gate_up_full)
    gate_in = gate_up[:, :f_width]
    up_in = gate_up[:, f_width:]
    sigma = jax.nn.sigmoid(gate_in)
    act_low = (gate_in * sigma * up_in).astype(jnp.bfloat16)
    layer_out = hidden + scatter_tokens(product_t(act_low, down_full))
    grad_layer = loss_scale * validity * (layer_out - teacher_own)
    grad_branch_two = gather_tokens(grad_layer.astype(jnp.bfloat16))
    grad_act = product(grad_branch_two, down_full)
    grad_gate_in = (grad_act * up_in * sigma * (1.0 + gate_in * (1.0 - sigma))).astype(jnp.bfloat16)
    grad_up_in = (grad_act * gate_in * sigma).astype(jnp.bfloat16)
    grad_gate_up = jnp.concatenate([grad_gate_in, grad_up_in], axis=1)
    grad_normed_two = scatter_tokens(product_t(grad_gate_up, gate_up_full))
    down_sum = scatter_grads(t_product(grad_branch_two, act_low))
    gate_up_sum = scatter_grads(t_product(normed_two, grad_gate_up))

    weighted_two = gain_second * grad_normed_two
    grad_gain_two = jnp.sum(grad_normed_two * hidden * scale_two, axis=0)
    grad_hidden = (
        grad_layer
        + scale_two * weighted_two
        - hidden
        * (scale_two * scale_two * scale_two)
        * jnp.mean(weighted_two * hidden, axis=-1, keepdims=True)
    )
    grad_branch_one = gather_tokens(grad_hidden.astype(jnp.bfloat16))
    outw_grad = t_product(grad_branch_one, gated_low)
    grad_gated = product(grad_branch_one, outw_full)
    (
        grad_query_raw,
        grad_key_raw,
        grad_value_raw,
        grad_gate_raw,
        grad_beta_raw,
        grad_decay_raw,
        grad_qtaps,
        grad_ktaps,
        grad_vtaps,
        grad_dlog,
        grad_bias,
        grad_mgain,
    ) = pullback(grad_gated)
    raw_low = jnp.concatenate(
        [
            grad_query_raw,
            grad_key_raw,
            grad_value_raw,
            grad_gate_raw,
            grad_beta_raw,
            grad_decay_raw,
            jnp.zeros((group_rows, SMALL - 2 * heads_here), jnp.float32),
        ],
        axis=1,
    ).astype(jnp.bfloat16)
    proj_grad = t_product(normed_one, raw_low)
    grad_normed_one = scatter_tokens(product_t(raw_low, proj_full))
    weighted_one = gain_first * grad_normed_one
    grad_gain_one = jnp.sum(grad_normed_one * input_float * scale_one, axis=0)
    grad_input = (
        grad_hidden
        + scale_one * weighted_one
        - input_float
        * (scale_one * scale_one * scale_one)
        * jnp.mean(weighted_one * input_float, axis=-1, keepdims=True)
    )
    mixer_sum = scatter_grads(jnp.concatenate([proj_grad, outw_grad], axis=1))

    taps = jnp.concatenate([grad_qtaps, grad_ktaps, grad_vtaps], axis=1)
    gain_pair = features_out(jnp.stack([grad_gain_one, grad_gain_two]))
    n_taps = taps.size
    n_all = 2 * gain_pair.shape[1] + grad_mgain.shape[0]
    flat = jnp.concatenate(
        [gain_pair.reshape(-1), grad_mgain, taps.reshape(-1), grad_dlog, grad_bias]
    )
    flat = jnp.pad(flat, (0, -flat.shape[0] % 1024)).reshape(-1, 128)
    flat = sum_over(flat, ("xl", "z", "y"))
    shared_rows = n_all // 128
    shared = sum_over(flat[:shared_rows], ("xh", "c")).reshape(-1)
    flat = flat.reshape(-1)
    taps_sum = flat[n_all : n_all + n_taps].reshape(CONV, -1)
    heads_at = n_all + n_taps
    features = gain_pair.shape[1]
    norm1_grad = lax.dynamic_slice_in_dim(shared, group_index * rows_dp, rows_dp)
    norm2_grad = lax.dynamic_slice_in_dim(shared, features + group_index * rows_dp, rows_dp)
    small_at = proj_width
    out_at = proj_width + SMALL
    return (
        features_out(layer_out),
        features_out(grad_input),
        norm1_grad,
        mixer_sum[:, :qk_width],
        mixer_sum[:, qk_width : 2 * qk_width],
        mixer_sum[:, 2 * qk_width : 2 * qk_width + v_width],
        mixer_sum[:, 2 * qk_width + v_width : proj_width],
        mixer_sum[:, small_at : small_at + heads_here],
        mixer_sum[:, small_at + heads_here : small_at + 2 * heads_here],
        flat[heads_at : heads_at + heads_here],
        flat[heads_at + heads_here : heads_at + 2 * heads_here],
        taps_sum[:, :qk_width],
        taps_sum[:, qk_width : 2 * qk_width],
        taps_sum[:, 2 * qk_width :],
        shared[2 * features :],
        mixer_sum[:, out_at:],
        norm2_grad,
        gate_up_sum[:, :f_width],
        gate_up_sum[:, f_width:],
        down_sum,
    )


def solution(mesh):
    fine = Mesh(mesh.devices.reshape(2, 4, 4, 2, 2), ("xl", "z", "y", "xh", "c"))
    dp = ("xl", "z", "y")
    tensor = ("xh", "c")
    tokens = P(dp + tensor, None)
    weight = P(dp, tensor)
    gain = P(dp)
    heads = P(tensor)
    taps = P(None, tensor)
    in_specs = (
        (tokens, tokens, P(), gain)
        + (weight,) * 6
        + (heads, heads, taps, taps, taps, P(), weight, gain)
        + (weight,) * 3
    )
    out_specs = (
        (tokens, tokens, gain)
        + (weight,) * 6
        + (heads, heads, taps, taps, taps, P(), weight, gain)
        + (weight,) * 3
    )
    return jax.shard_map(shards, mesh=fine, in_specs=in_specs, out_specs=out_specs, check_vma=False)
```

```python
from functools import partial

import jax
import jax.numpy as jnp
from jax import lax
from jax.experimental import pallas as pl
from jax.experimental.pallas import tpu as pltpu
from jax.sharding import Mesh, PartitionSpec as P

DK = 128
DV = 256
CONV = 4
EPSILON = 1e-06
MIXER_FLOOR = 0.001
SPAN = 128
HEADS = 2
CHUNKS = 4
ROWS = SPAN * CHUNKS
QK = HEADS * DK
VW = HEADS * DV
CONVW = 2 * QK + VW
SMALL = 128
SMALL_AT = VW + CONVW
PROJ = SMALL_AT + SMALL
GATE_BLOCKS = VW // 128
Q_BLOCK = VW // 128
K_BLOCK = Q_BLOCK + HEADS
PAIRS = [(n, h) for n in range(CHUNKS) for h in range(HEADS)]
F32 = jnp.float32
BF16 = jnp.bfloat16


def contract(left, right, dims):
    return lax.dot_general(left, right, (dims, ((), ())), preferred_element_type=F32)


def halves(values):
    high = values.astype(BF16)
    return high, (values - high.astype(F32)).astype(BF16)


def dot_parts(left, right, dims):
    (lh, ll), (rh, rl) = left, right
    return contract(lh, rh, dims) + (contract(lh, rl, dims) + contract(ll, rh, dims))


NN = ((1,), (0,))
NT = ((1,), (1,))


def mm(left, right):
    return dot_parts(halves(left), halves(right), NN)


def mm_t(left, right):
    return dot_parts(halves(left), halves(right), NT)


def mm_exact(left, right):
    return lax.dot_general(
        left, right, (NN, ((), ())), precision=lax.Precision.HIGHEST, preferred_element_type=F32
    )


def iota(shape, axis):
    return lax.broadcasted_iota(jnp.int32, shape, axis)


def segment(position, first, second):
    return jnp.where(position >= first, 1, 0) + jnp.where(position >= second, 1, 0)


def silu(values):
    return values * jax.nn.sigmoid(values)


def silu_slope(values):
    s = jax.nn.sigmoid(values)
    return s * (1.0 + values * (1.0 - s))


def softplus(values):
    return jnp.maximum(values, 0.0) + jnp.log1p(jnp.exp(-jnp.abs(values)))


def invert_all(lowers):
    r, c = iota((SPAN, SPAN), 0), iota((SPAN, SPAN), 1)
    eye = jnp.where(r == c, 1.0, 0.0)
    near = (r >> 3) == (c >> 3)
    diag = [jnp.where(near, a, 0.0) for a in lowers]
    diag_parts = [halves(d) for d in diag]
    square = [dot_parts(d, d, NN) for d in diag_parts]
    square_parts = [halves(s) for s in square]
    fourth = [dot_parts(s, s, NN) for s in square_parts]
    inverse = [eye - d for d in diag]
    inverse = [x + dot_parts(halves(x), s, NN) for x, s in zip(inverse, square_parts)]
    inverse = [x + mm(x, s) for x, s in zip(inverse, fourth)]
    shift = 3
    while (1 << shift) < SPAN:
        corner = ((r >> (shift + 1)) == (c >> (shift + 1))) & ((r >> shift) != (c >> shift))
        parts = [halves(x) for x in inverse]
        moved = [
            dot_parts(halves(jnp.where(corner, a, 0.0)), x, NN) for a, x in zip(lowers, parts)
        ]
        inverse = [
            x - dot_parts(p, halves(m), NN) for x, p, m in zip(inverse, parts, moved)
        ]
        shift += 1
    return inverse


def chunk(n):
    return slice(n * SPAN, (n + 1) * SPAN)


def lanes(index, width=128):
    return slice(index * width, (index + 1) * width)


def row_scale(values):
    return lax.rsqrt(jnp.sum(values * values, axis=1, keepdims=True) + EPSILON)


def decay_terms(n, small, bias, rate, first, second):
    betas = jax.nn.sigmoid(small)
    decays = -rate * softplus(small + bias)
    r, c = iota((SPAN, SPAN), 0), iota((SPAN, SPAN), 1)
    total = mm_exact(jnp.where(c <= r, 1.0, 0.0), decays)
    turned = total.T
    position = iota((SPAN, 1), 0) + n * SPAN
    own = segment(position, first, second)
    ends = jnp.int32(n * SPAN + SPAN - 1)
    last = own == segment(ends, first, second)
    terms = []
    for h in range(HEADS):
        column = total[:, HEADS + h : HEADS + h + 1]
        if n:
            carried = own == segment(jnp.int32(n * SPAN - 1), first, second)
            growth = jnp.where(carried, jnp.exp(column), 0.0)
        else:
            growth = jnp.zeros((SPAN, 1), F32)
        final = column[SPAN - 1 : SPAN]
        fade = jnp.where(last, jnp.exp(jnp.where(last, final - column, 0.0)), 0.0)
        terms.append((betas[:, h : h + 1], column, turned[HEADS + h : HEADS + h + 1], growth, fade))
    return terms


def same_segment(n, first, second):
    r, c = iota((SPAN, SPAN), 0), iota((SPAN, SPAN), 1)
    base = n * SPAN
    return (segment(r + base, first, second) == segment(c + base, first, second)) & (c <= r)


def mixer_forward_kernel(
    bounds, raw, taps, vectors, gain, gated, conv, ratios, inner, scores, solved, written, states, mixed
):
    first, second = bounds[0], bounds[1]
    bias, rate = vectors[0:1], vectors[1:2]
    queries, keys, values, terms = {}, {}, {}, {}
    for n in range(CHUNKS):
        rows = chunk(n)
        position = iota((SPAN, 1), 0) + n * SPAN
        own = segment(position, first, second)
        joins = [
            jnp.where((position >= o) & (segment(position - o, first, second) == own), 1.0, 0.0)
            for o in range(1, CONV)
        ]

        def convolved(block):
            here = raw[rows, lanes(GATE_BLOCKS + block)]
            summed = here * taps[CONV - 1 : CONV, lanes(block)]
            for o in range(1, CONV):
                if n:
                    moved = raw[n * SPAN - o : (n + 1) * SPAN - o, lanes(GATE_BLOCKS + block)]
                else:
                    moved = pltpu.roll(here, o, 0)
                tap = taps[CONV - 1 - o : CONV - o, lanes(block)]
                summed = summed + tap * (moved * joins[o - 1])
            conv[rows, lanes(block)] = summed
            return silu(summed)

        for h in range(HEADS):
            q = convolved(Q_BLOCK + h)
            queries[n, h] = q * (row_scale(q) * DK ** (-0.5))
            k = convolved(K_BLOCK + h)
            keys[n, h] = k * row_scale(k)
            values[n, h] = jnp.concatenate(
                [convolved(2 * h), convolved(2 * h + 1)], axis=1
            )
        small = raw[rows, SMALL_AT:PROJ]
        for h, term in enumerate(decay_terms(n, small, bias, rate, first, second)):
            terms[n, h] = term

    r, c = iota((SPAN, SPAN), 0), iota((SPAN, SPAN), 1)
    key_parts = {p: halves(keys[p]) for p in PAIRS}
    query_parts = {p: halves(queries[p]) for p in PAIRS}
    lowers, score = [], {}
    for n in range(CHUNKS):
        causal = same_segment(n, first, second)
        for h in range(HEADS):
            p = (n, h)
            beta, column, row, growth, fade = terms[p]
            ratio = jnp.where(causal, jnp.exp(jnp.where(causal, column - row, 0.0)), 0.0)
            met = dot_parts(key_parts[p], key_parts[p], NT)
            lower = jnp.where(c < r, ratio * met, 0.0)
            score[p] = ratio * dot_parts(query_parts[p], key_parts[p], NT)
            at = n * HEADS + h
            ratios[at] = ratio
            inner[at] = lower
            scores[at] = score[p]
            lowers.append(beta * lower)
    inverses = invert_all(lowers)
    own_part, state_part, key_fade = {}, {}, {}
    for p, x in zip(PAIRS, inverses):
        n, h = p
        beta, column, row, growth, fade = terms[p]
        solved[n * HEADS + h] = x
        parts = halves(x)
        own_part[p] = dot_parts(parts, halves(beta * values[p]), NN)
        state_part[p] = halves(dot_parts(parts, halves((beta * growth) * keys[p]), NN))
        key_fade[p] = halves((fade * keys[p]).T)
    held = [jnp.zeros((DK, DV), F32) for h in range(HEADS)]
    for n in range(CHUNKS):
        for h in range(HEADS):
            p = (n, h)
            growth = terms[p][3]
            states[n * HEADS + h] = held[h]
            state = halves(held[h])
            wrote = own_part[p] - dot_parts(state_part[p], state, NN)
            wrote_parts = halves(wrote)
            written[chunk(n), lanes(h, DV)] = wrote
            out = growth * dot_parts(query_parts[p], state, NN)
            out = out + dot_parts(halves(score[p]), wrote_parts, NN)
            held[h] = growth[SPAN - 1 : SPAN] * held[h] + dot_parts(key_fade[p], wrote_parts, NN)
            mixed[chunk(n), lanes(h, DV)] = out
            scale = lax.rsqrt(jnp.mean(out * out, axis=1, keepdims=True) + MIXER_FLOOR)
            gate = raw[chunk(n), lanes(h, DV)]
            gated[chunk(n), lanes(h, DV)] = (out * scale * gain[...] * silu(gate)).astype(BF16)


def mixer_backward_kernel(
    bounds, grad_mixed, raw, taps, vectors, conv, ratios, inner, scores, solved, written, states,
    grad_raw, grad_taps, grad_vectors, slopes,
):
    first, second = bounds[0], bounds[1]
    bias, rate = vectors[0:1], vectors[1:2]
    r, c = iota((SPAN, SPAN), 0), iota((SPAN, SPAN), 1)
    lane = iota((SPAN, SMALL), 1)
    terms, queries, keys, values, grad_out = {}, {}, {}, {}, {}
    for n in range(CHUNKS):
        rows = chunk(n)
        small = raw[rows, SMALL_AT:PROJ]
        for h, term in enumerate(decay_terms(n, small, bias, rate, first, second)):
            p = (n, h)
            terms[p] = term
            q = silu(conv[rows, lanes(Q_BLOCK + h)])
            queries[p] = q * (row_scale(q) * DK ** (-0.5))
            k = silu(conv[rows, lanes(K_BLOCK + h)])
            keys[p] = k * row_scale(k)
            values[p] = silu(conv[rows, lanes(h, DV)])
            grad_out[p] = grad_mixed[rows, lanes(h, DV)]

    from_out, from_state, into_state, key_turned, out_parts = {}, {}, {}, {}, {}
    for p in PAIRS:
        n, h = p
        at = n * HEADS + h
        beta, column, row, growth, fade = terms[p]
        turned = halves(solved[at].T)
        out_parts[p] = halves(grad_out[p])
        pulled = dot_parts(halves(scores[at].T), out_parts[p], NN)
        from_out[p] = dot_parts(turned, halves(pulled), NN)
        from_state[p] = halves(dot_parts(turned, halves(fade * keys[p]), NN))
        into_state[p] = mm(queries[p].T, growth * grad_out[p])
        key_turned[p] = halves(((beta * growth) * keys[p]).T)
    held = [jnp.zeros((DK, DV), F32) for h in range(HEADS)]
    grad_target, grad_held, grad_held_parts = {}, {}, {}
    for n in reversed(range(CHUNKS)):
        for h in range(HEADS):
            p = (n, h)
            growth = terms[p][3]
            grad_held[p] = held[h]
            grad_held_parts[p] = halves(held[h])
            target = from_out[p] + dot_parts(from_state[p], grad_held_parts[p], NN)
            grad_target[p] = halves(target), target
            kept = growth[SPAN - 1 : SPAN] * held[h] + into_state[p]
            held[h] = kept - dot_parts(key_turned[p], grad_target[p][0], NN)

    log_sum = jnp.zeros((1, SMALL), F32)
    bias_sum = jnp.zeros((1, SMALL), F32)
    for n in range(CHUNKS):
        rows = chunk(n)
        grad_total = jnp.zeros((SPAN, SMALL), F32)
        grad_beta = jnp.zeros((SPAN, SMALL), F32)
        for h in range(HEADS):
            p = (n, h)
            at = n * HEADS + h
            beta, column, row, growth, fade = terms[p]
            target_parts, target = grad_target[p]
            state = states[at]
            state_parts = halves(state)
            wrote_parts = halves(written[rows, lanes(h, DV)])
            q, k, v = queries[p], keys[p], values[p]
            q_parts, k_parts = halves(q), halves(k)
            score, lower, ratio = scores[at], inner[at], ratios[at]
            out_state = dot_parts(out_parts[p], state_parts, NT)
            target_state = dot_parts(target_parts, state_parts, NT)
            wrote_state = dot_parts(wrote_parts, grad_held_parts[p], NT)
            grad_score = dot_parts(out_parts[p], wrote_parts, NT)
            grad_lower = -dot_parts(target_parts, wrote_parts, NT)
            grad_met = beta * grad_lower * jnp.where(c < r, ratio, 0.0)
            grad_pair = grad_score * ratio
            recall = jnp.sum(target_state * k, axis=1, keepdims=True)
            grad_growth = jnp.sum(out_state * q, axis=1, keepdims=True) - beta * recall
            beta_col = jnp.sum(target * v, axis=1, keepdims=True) - growth * recall
            beta_col = beta_col + jnp.sum(grad_lower * lower, axis=1, keepdims=True)
            faded = jnp.sum(wrote_state * k, axis=1, keepdims=True) * fade
            grad_q = growth * out_state + dot_parts(halves(grad_pair), k_parts, NN)
            grad_k = fade * wrote_state - (beta * growth) * target_state
            grad_k = grad_k + dot_parts(halves(grad_pair.T), q_parts, NN)
            grad_k = grad_k + dot_parts(halves(grad_met + grad_met.T), k_parts, NN)
            grad_v = beta * target
            held_grad = jnp.sum(state * grad_held[p], axis=1, keepdims=True)
            at_end = jnp.sum(held_grad, axis=0, keepdims=True) * growth[SPAN - 1 : SPAN]
            at_end = at_end + jnp.sum(faded, axis=0, keepdims=True)
            moved = grad_score * score + beta * (grad_lower * lower)
            col = jnp.sum(moved, axis=1, keepdims=True) - jnp.sum(moved.T, axis=1, keepdims=True)
            col = col + grad_growth * growth - faded
            col = col + jnp.where(iota((SPAN, 1), 0) == SPAN - 1, at_end, 0.0)
            grad_total = jnp.where(lane == HEADS + h, col, grad_total)
            grad_beta = jnp.where(lane == h, beta_col, grad_beta)
            pre = conv[rows, lanes(Q_BLOCK + h)]
            raw_q = silu(pre)
            scale = row_scale(raw_q)
            along = jnp.sum(grad_q * raw_q, axis=1, keepdims=True)
            back = (grad_q - raw_q * ((scale * scale) * along)) * (scale * DK ** (-0.5))
            slopes[rows, lanes(Q_BLOCK + h)] = back * silu_slope(pre)
            pre = conv[rows, lanes(K_BLOCK + h)]
            raw_k = silu(pre)
            scale = row_scale(raw_k)
            along = jnp.sum(grad_k * raw_k, axis=1, keepdims=True)
            back = (grad_k - raw_k * ((scale * scale) * along)) * scale
            slopes[rows, lanes(K_BLOCK + h)] = back * silu_slope(pre)
            wide = lanes(h, DV)
            slopes[rows, wide] = grad_v * silu_slope(conv[rows, wide])
        grad_decays = mm_exact(jnp.where(c >= r, 1.0, 0.0), grad_total)
        small = raw[rows, SMALL_AT:PROJ]
        shifted = small + bias
        grad_step = -grad_decays * rate * jax.nn.sigmoid(shifted)
        betas = jax.nn.sigmoid(small)
        grad_raw[rows, CONVW : CONVW + SMALL] = (
            grad_beta * betas * (1.0 - betas) + grad_step
        ).astype(BF16)
        bias_sum = bias_sum + jnp.sum(grad_step, axis=0, keepdims=True)
        log_sum = log_sum - jnp.sum(
            grad_decays * rate * softplus(shifted), axis=0, keepdims=True
        )
    grad_vectors[0:1] = log_sum
    grad_vectors[1:2] = bias_sum

    slopes[ROWS : ROWS + 8] = jnp.zeros((8, CONVW), F32)
    for block in range(CONVW // 128):
        sums = [jnp.zeros((1, 128), F32) for o in range(CONV)]
        for n in range(CHUNKS):
            rows = chunk(n)
            position = iota((SPAN, 1), 0) + n * SPAN
            own = segment(position, first, second)
            here = raw[rows, lanes(GATE_BLOCKS + block)]
            total = jnp.zeros((SPAN, 128), F32)
            for o in range(CONV):
                moved = slopes[n * SPAN + o : (n + 1) * SPAN + o, lanes(block)]
                if o:
                    moved = jnp.where(segment(position + o, first, second) == own, moved, 0.0)
                total = total + taps[CONV - 1 - o : CONV - o, lanes(block)] * moved
                sums[o] = sums[o] + jnp.sum(moved * here, axis=0, keepdims=True)
            grad_raw[rows, lanes(block)] = total.astype(BF16)
        for o in range(CONV):
            grad_taps[CONV - 1 - o : CONV - o, lanes(block)] = sums[o]


def vmem(count):
    return [pl.BlockSpec(memory_space=pltpu.VMEM)] * count


LIMIT = pltpu.CompilerParams(vmem_limit_bytes=56 * 1024 * 1024)
SMEM = pl.BlockSpec(memory_space=pltpu.SMEM)
SAVED = [
    jax.ShapeDtypeStruct((ROWS, CONVW), F32),
    jax.ShapeDtypeStruct((len(PAIRS), SPAN, SPAN), F32),
    jax.ShapeDtypeStruct((len(PAIRS), SPAN, SPAN), F32),
    jax.ShapeDtypeStruct((len(PAIRS), SPAN, SPAN), F32),
    jax.ShapeDtypeStruct((len(PAIRS), SPAN, SPAN), F32),
    jax.ShapeDtypeStruct((ROWS, VW), F32),
    jax.ShapeDtypeStruct((len(PAIRS), DK, DV), F32),
    jax.ShapeDtypeStruct((ROWS, VW), F32),
]


def mixer_forward(bounds, raw, taps, vectors, gain):
    outs = [jax.ShapeDtypeStruct((ROWS, VW), BF16)] + SAVED
    return pl.pallas_call(
        mixer_forward_kernel,
        out_shape=outs,
        in_specs=[SMEM] + vmem(4),
        out_specs=vmem(len(outs)),
        compiler_params=LIMIT,
        name="mixer_forward",
    )(bounds, raw, taps, vectors, gain)


def mixer_backward(bounds, grad_mixed, raw, taps, vectors, saved):
    outs = [
        jax.ShapeDtypeStruct((ROWS, CONVW + SMALL), BF16),
        jax.ShapeDtypeStruct((8, CONVW), F32),
        jax.ShapeDtypeStruct((8, SMALL), F32),
    ]
    return pl.pallas_call(
        mixer_backward_kernel,
        out_shape=outs,
        in_specs=[SMEM] + vmem(4 + len(saved)),
        out_specs=vmem(len(outs)),
        scratch_shapes=[pltpu.VMEM((ROWS + 8, CONVW), F32)],
        compiler_params=LIMIT,
        name="mixer_backward",
    )(bounds, grad_mixed, raw, taps, vectors, *saved)


TN = ((0,), (0,))
OWN = ROWS // 4
TILE = 512
STEP = 512
WIDE = 384


def whole(*shape):
    return pl.BlockSpec(shape, lambda i: (0,) * len(shape))


def place_rows(places, j):
    return pl.ds(pl.multiple_of(places[j] * OWN, OWN), OWN)


def project_kernel(places, x0, x1, x2, x3, small, weights, raw, normed, gains, steps):
    step = pl.program_id(0)

    @pl.when(step == 0)
    def prepare():
        r, c = iota((8, SMALL), 0), iota((8, SMALL), 1)
        pick = jnp.where((r < 2) & (c == r + 2 * HEADS), 1.0, 0.0).astype(BF16)
        gains[...] = contract(pick, small[...], NT)
        for j, x in enumerate((x0, x1, x2, x3)):
            values = x[...].astype(F32)
            scale = lax.rsqrt(jnp.mean(values * values, axis=1, keepdims=True) + EPSILON)
            low = (values * scale * gains[0:1]).astype(BF16)
            rows = place_rows(places, j)
            normed[rows, :] = low
            for s in range(steps.shape[0]):
                steps[s, rows, :] = low[:, s * STEP : (s + 1) * STEP]

    product = contract(steps[step], weights[:, VW:], NN)

    @pl.when(step == 0)
    def start():
        raw[...] = product

    @pl.when(step > 0)
    def add():
        raw[...] += product


def project(places, blocks, weights):
    features = weights.shape[0]
    count = features // STEP
    return pl.pallas_call(
        project_kernel,
        grid=(count,),
        out_shape=[
            jax.ShapeDtypeStruct((ROWS, PROJ), F32),
            jax.ShapeDtypeStruct((ROWS, features), BF16),
            jax.ShapeDtypeStruct((8, features), F32),
        ],
        in_specs=[SMEM]
        + [whole(OWN, features)] * 4
        + [
            pl.BlockSpec((features, SMALL), lambda i: (0, (VW + SMALL_AT) // SMALL)),
            pl.BlockSpec((STEP, weights.shape[1]), lambda i: (i, 0)),
        ],
        out_specs=[whole(ROWS, PROJ), whole(ROWS, features), whole(8, features)],
        scratch_shapes=[pltpu.VMEM((count, ROWS, STEP), BF16)],
        compiler_params=LIMIT,
        name="project",
    )(places, *blocks, weights, weights)


def split_rows(product, kept_own, kept_other, sent_own, sent_other):
    kept_own[...] = product[:OWN]
    kept_other[...] = product[OWN : 2 * OWN]
    sent_own[...] = product[2 * OWN : 3 * OWN].astype(BF16)
    sent_other[...] = product[3 * OWN :].astype(BF16)


def split_outs(features):
    shape = (OWN, features)
    outs = [jax.ShapeDtypeStruct(shape, F32)] * 2 + [jax.ShapeDtypeStruct(shape, BF16)] * 2
    return outs, [pl.BlockSpec((OWN, TILE), lambda i: (0, i))] * 4


def mix_out_kernel(places, gated, weights, kept_own, kept_other, sent_own, sent_other, turned):
    @pl.when(pl.program_id(0) == 0)
    def prepare():
        for j in range(4):
            turned[j * OWN : (j + 1) * OWN] = gated[place_rows(places, j), :]

    split_rows(
        contract(turned[...], weights[...], NT), kept_own, kept_other, sent_own, sent_other
    )


def mix_out(places, gated, weights):
    features = weights.shape[0]
    outs, specs = split_outs(features)
    return pl.pallas_call(
        mix_out_kernel,
        grid=(features // TILE,),
        out_shape=outs + [jax.ShapeDtypeStruct((ROWS, VW), BF16)],
        in_specs=[SMEM, whole(ROWS, VW), pl.BlockSpec((TILE, VW), lambda i: (i, 0))],
        out_specs=specs + [whole(ROWS, VW)],
        compiler_params=LIMIT,
        name="mix_out",
    )(places, gated, weights)


def gate_up_kernel(x0, x1, x2, x3, weights, act, gate, up, rows, held, *, units):
    step = pl.program_id(0)

    for j, x in enumerate((x0, x1, x2, x3)):

        @pl.when(step == 0)
        def prepare():
            held[j * OWN : (j + 1) * OWN] = x[...]

        @pl.when(step == j)
        def keep():
            rows[...] = x[...]

    for q in range(WIDE // 128):

        @pl.when(step * WIDE + q * 128 < units)
        def pair():
            product = contract(held[...], weights[:, lanes(q, 256)], NN)
            gate_in, up_in = product[:, :128], product[:, 128:]
            gate[:, lanes(q)] = gate_in
            up[:, lanes(q)] = up_in
            act[:, lanes(q)] = (silu(gate_in) * up_in).astype(BF16)


def gate_up(blocks, weights, units):
    features = weights.shape[0]
    tile = pl.BlockSpec((ROWS, WIDE), lambda i: (0, i))
    return pl.pallas_call(
        partial(gate_up_kernel, units=units),
        grid=(pl.cdiv(units, WIDE),),
        out_shape=[
            jax.ShapeDtypeStruct((ROWS, units), BF16),
            jax.ShapeDtypeStruct((ROWS, units), F32),
            jax.ShapeDtypeStruct((ROWS, units), F32),
            jax.ShapeDtypeStruct((ROWS, features), BF16),
        ],
        in_specs=[whole(OWN, features)] * 4
        + [pl.BlockSpec((features, 2 * WIDE), lambda i: (0, i))],
        out_specs=[
            tile,
            tile,
            tile,
            pl.BlockSpec((OWN, features), lambda i: (jnp.minimum(i, 3), 0)),
        ],
        scratch_shapes=[pltpu.VMEM((ROWS, features), BF16)],
        compiler_params=LIMIT,
        name="gate_up",
    )(*blocks, weights)


def rows_back_kernel(left, weights, kept_own, kept_other, sent_own, sent_other):
    split_rows(contract(left[...], weights[...], NT), kept_own, kept_other, sent_own, sent_other)


def rows_back(left, weights, block, name):
    features = weights.shape[0]
    width = left.shape[1]
    outs, specs = split_outs(features)
    return pl.pallas_call(
        rows_back_kernel,
        grid=(features // TILE,),
        out_shape=outs,
        in_specs=[whole(ROWS, width), pl.BlockSpec((TILE, width), lambda i: (i, block))],
        out_specs=specs,
        compiler_params=LIMIT,
        name=name,
    )(left, weights)


def act_back_kernel(x0, x1, x2, x3, weights, gate, up, grads, rows, steps, total, gates, ups):
    step = pl.program_id(0)

    for j, x in enumerate((x0, x1, x2, x3)):
        at = slice(j * OWN, (j + 1) * OWN)

        @pl.when(step == 0)
        def prepare():
            for s in range(steps.shape[0]):
                steps[s, at, :] = x[:, s * STEP : (s + 1) * STEP]

        @pl.when(step == j)
        def keep():
            rows[...] = x[...]
            gates[at] = gate[...]
            ups[at] = up[...]

    product = contract(steps[step], weights[...], NN)

    @pl.when(step == 0)
    def start():
        total[...] = product

    @pl.when(step > 0)
    def add():
        total[...] += product

    @pl.when(step == pl.num_programs(0) - 1)
    def finish():
        for b in range(total.shape[1] // 128):
            grad, gate_in, up_in = total[:, lanes(b)], gates[:, lanes(b)], ups[:, lanes(b)]
            s = jax.nn.sigmoid(gate_in)
            grads[:, lanes(2 * b)] = (grad * up_in * s * (1.0 + gate_in * (1.0 - s))).astype(BF16)
            grads[:, lanes(2 * b + 1)] = (grad * gate_in * s).astype(BF16)


def act_back(blocks, weights, gate, up):
    features = weights.shape[0]
    units = gate.shape[1]
    count = features // STEP
    part = pl.BlockSpec((OWN, units), lambda i: (i, 0))
    return pl.pallas_call(
        act_back_kernel,
        grid=(count,),
        out_shape=[
            jax.ShapeDtypeStruct((ROWS, 2 * units), BF16),
            jax.ShapeDtypeStruct((ROWS, features), BF16),
        ],
        in_specs=[whole(OWN, features)] * 4
        + [pl.BlockSpec((STEP, units), lambda i: (i, 2)), part, part],
        out_specs=[
            whole(ROWS, 2 * units),
            pl.BlockSpec((OWN, features), lambda i: (i, 0)),
        ],
        scratch_shapes=[
            pltpu.VMEM((count, ROWS, STEP), BF16),
            pltpu.VMEM((ROWS, units), F32),
            pltpu.VMEM((ROWS, units), F32),
            pltpu.VMEM((ROWS, units), F32),
        ],
        compiler_params=LIMIT,
        name="act_back",
    )(*blocks, weights, gate, up)


def gated_back_kernel(
    places, x0, x1, x2, x3, weights, raw_gate, mixed, gain, grad_mixed, grad_gate, grad_gain, turned
):
    gain_sum = jnp.zeros((1, DV), F32)
    for j, x in enumerate((x0, x1, x2, x3)):
        turned[j * OWN : (j + 1) * OWN] = x[...]
        grads = contract(x[...], weights[...], NN)
        rows = place_rows(places, j)
        for h in range(HEADS):
            out = mixed[rows, lanes(h, DV)]
            gate = raw_gate[rows, lanes(h, DV)]
            grad = grads[:, lanes(h, DV)]
            scale = lax.rsqrt(jnp.mean(out * out, axis=1, keepdims=True) + MIXER_FLOOR)
            opened = grad * silu(gate)
            scaled = out * scale
            gain_sum = gain_sum + jnp.sum(opened * scaled, axis=0, keepdims=True)
            grad_gate[rows, lanes(h, DV)] = (
                grad * scaled * gain[...] * silu_slope(gate)
            ).astype(BF16)
            inward = opened * gain[...]
            along = jnp.mean(inward * out, axis=1, keepdims=True)
            grad_mixed[rows, lanes(h, DV)] = scale * inward - out * (
                (scale * scale * scale) * along
            )
    grad_gain[0:1] = gain_sum


def gated_back(places, blocks, weights, raw, mixed, gain):
    features = weights.shape[0]
    return pl.pallas_call(
        gated_back_kernel,
        grid=(1,),
        out_shape=[
            jax.ShapeDtypeStruct((ROWS, VW), F32),
            jax.ShapeDtypeStruct((ROWS, VW), BF16),
            jax.ShapeDtypeStruct((8, DV), F32),
            jax.ShapeDtypeStruct((ROWS, features), BF16),
        ],
        in_specs=[SMEM]
        + [whole(OWN, features)] * 4
        + [whole(features, VW), whole(ROWS, VW), whole(ROWS, VW), whole(1, DV)],
        out_specs=[whole(ROWS, VW), whole(ROWS, VW), whole(8, DV), whole(ROWS, features)],
        compiler_params=LIMIT,
        name="gated_back",
    )(places, *blocks, weights, raw, mixed, gain)


def input_back_kernel(
    places, gate, conv, weights, kept_own, kept_other, sent_own, sent_other, turned
):
    @pl.when(pl.program_id(0) == 0)
    def prepare():
        for j in range(4):
            rows = place_rows(places, j)
            turned[j * OWN : (j + 1) * OWN, :VW] = gate[rows, :]
            turned[j * OWN : (j + 1) * OWN, VW:] = conv[rows, :]

    split_rows(
        contract(turned[...], weights[:, VW:], NT), kept_own, kept_other, sent_own, sent_other
    )


def input_back(places, gate, conv, weights):
    features = weights.shape[0]
    outs, specs = split_outs(features)
    return pl.pallas_call(
        input_back_kernel,
        grid=(features // TILE,),
        out_shape=outs,
        in_specs=[
            SMEM,
            whole(ROWS, VW),
            whole(ROWS, CONVW + SMALL),
            pl.BlockSpec((TILE, weights.shape[1]), lambda i: (i, 0)),
        ],
        out_specs=specs,
        scratch_shapes=[pltpu.VMEM((ROWS, PROJ), BF16)],
        compiler_params=LIMIT,
        name="input_back",
    )(places, gate, conv, weights)


def grads_kernel(count, *refs):
    out = refs[-1]
    at = 0
    for i in range(count):
        left, right = refs[2 * i], refs[2 * i + 1]
        width = right.shape[1]
        out[:, at : at + width] = contract(left[...], right[...], TN).astype(BF16)
        at += width


def weight_grads(pairs, name):
    features = pairs[0][0].shape[1]
    width = sum(right.shape[1] for left, right in pairs)
    specs = []
    for left, right in pairs:
        specs += [pl.BlockSpec((ROWS, STEP), lambda i: (0, i)), whole(ROWS, right.shape[1])]
    return pl.pallas_call(
        partial(grads_kernel, len(pairs)),
        grid=(features // STEP,),
        out_shape=jax.ShapeDtypeStruct((features, width), BF16),
        in_specs=specs,
        out_specs=pl.BlockSpec((STEP, width), lambda i: (i, 0)),
        compiler_params=LIMIT,
        name=name,
    )(*[operand for pair in pairs for operand in pair])


SWAP = [(0, 1), (1, 0)]
PLANE = ("z", "y")


def trade(values, axis):
    return lax.ppermute(values, axis, SWAP)


def gather_tokens(own):
    across = trade(own, "xh")
    return own, across, trade(own, "c"), trade(across, "c")


def scatter_tokens(kept_own, kept_other, sent_own, sent_other):
    other = kept_other + trade(sent_other, "c").astype(jnp.float32)
    own = kept_own + trade(sent_own, "c").astype(jnp.float32)
    return own + trade(other.astype(jnp.bfloat16), "xh").astype(jnp.float32)


def gather_weights(*blocks):
    other = jnp.concatenate([trade(block, "xl") for block in blocks], axis=1)
    both = jnp.stack([jnp.concatenate(blocks, axis=1), other], axis=0)
    full = lax.all_gather(both, PLANE, axis=0, tiled=False)
    return full.reshape(-1, other.shape[1])


def scatter_grads(grads):
    both = lax.psum_scatter(grads, PLANE, scatter_dimension=0, tiled=True)
    both = both.reshape(2, -1, grads.shape[1])
    return both[0].astype(jnp.float32) + trade(both[1], "xl").astype(jnp.float32)


def features_in(rows):
    count = rows.shape[0]
    halves = rows.reshape(count, 2, -1)
    flip = lax.axis_index("xl") == 1
    first = jnp.where(flip, halves[:, 1], halves[:, 0]).reshape(count, 16, 64)
    second = jnp.where(flip, halves[:, 0], halves[:, 1]).reshape(count, 16, 64)
    return jnp.concatenate([first, second], axis=2).reshape(count, -1)


def features_out(rows):
    count = rows.shape[0]
    blocks = rows.reshape(count, 16, 2, 64)
    flip = lax.axis_index("xl") == 1
    first = blocks[:, :, 0].reshape(count, -1)
    second = blocks[:, :, 1].reshape(count, -1)
    low = jnp.where(flip, second, first)
    high = jnp.where(flip, first, second)
    return jnp.concatenate([low, high], axis=1)


def sum_over(values, axes):
    for axis in axes:
        size = lax.axis_size(axis)
        step = 1
        while step < size:
            values = values + lax.ppermute(values, axis, [(i, i ^ step) for i in range(size)])
            step *= 2
    return values


def shards(
    layer_input,
    teacher_out,
    lengths,
    norm1_gain,
    query_weight,
    key_weight,
    value_weight,
    output_gate,
    beta_weight,
    decay_weight,
    decay_log,
    step_bias,
    query_taps,
    key_taps,
    value_taps,
    mixer_gain,
    out_weight,
    norm2_gain,
    gate_weight,
    up_weight,
    down_weight,
):
    tok_rows = layer_input.shape[0]
    rows_dp = norm1_gain.shape[0]
    group_index = lax.axis_index("xl") * 16 + lax.axis_index("z") * 4 + lax.axis_index("y")
    half, core = lax.axis_index("xh"), lax.axis_index("c")
    tensor_index = half * 2 + core
    places = jnp.stack(
        [tensor_index, 2 - 2 * half + core, 2 * half + 1 - core, 3 - tensor_index]
    ).astype(jnp.int32)
    heads_here = decay_log.shape[0]
    own_lengths = lax.dynamic_index_in_dim(lengths, group_index, 0, keepdims=False)
    boundary = jnp.cumsum(own_lengths)
    own_rows = tensor_index * tok_rows + jnp.arange(tok_rows, dtype=jnp.int32)
    validity = (own_rows < boundary[-1]).astype(jnp.float32)[:, None]
    loss_scale = jnp.float32(128 * tok_rows) / jnp.sum(lengths).astype(jnp.float32)

    qk_width = query_taps.shape[1]
    v_width = value_taps.shape[1]
    f_width = gate_weight.shape[1]
    filler = jnp.zeros((rows_dp, SMALL - 2 * heads_here - 2), jnp.bfloat16)
    mixer_block = jnp.concatenate(
        [out_weight, output_gate, value_weight, query_weight, key_weight], axis=1
    )
    small_block = jnp.concatenate(
        [beta_weight, decay_weight, norm1_gain[:, None], norm2_gain[:, None], filler], axis=1
    )
    paired_units = jnp.stack(
        [gate_weight.reshape(rows_dp, -1, 128), up_weight.reshape(rows_dp, -1, 128)], axis=2
    ).reshape(rows_dp, 2 * f_width)
    mixer_full = gather_weights(mixer_block, small_block)
    ffn_full = gather_weights(jnp.concatenate([paired_units, down_weight], axis=1))
    input_own = features_in(layer_input)
    teacher_own = features_in(teacher_out).astype(jnp.float32)
    conv_taps = jnp.concatenate([value_taps, query_taps, key_taps], axis=1).astype(jnp.float32)
    vectors = jnp.pad(
        jnp.stack([step_bias, jnp.exp(decay_log)]),
        ((0, 6), (heads_here, SMALL - 2 * heads_here)),
    )
    gain_mixer = mixer_gain.astype(jnp.float32)[None, :]

    input_blocks = gather_tokens(input_own)
    raw, normed_one, gains = project(places, input_blocks, mixer_full)
    gain_first, gain_second = gains[0:1], gains[1:2]
    input_float = input_own.astype(jnp.float32)
    scale_one = lax.rsqrt(jnp.mean(input_float * input_float, axis=-1, keepdims=True) + EPSILON)
    gated_low, *saved, mixed = mixer_forward(boundary, raw, conv_taps, vectors, gain_mixer)
    *terms, gated_turned = mix_out(places, gated_low, mixer_full)
    hidden = input_float + scatter_tokens(*terms)
    scale_two = lax.rsqrt(jnp.mean(hidden * hidden, axis=-1, keepdims=True) + EPSILON)
    normed_two = (hidden * scale_two * gain_second).astype(jnp.bfloat16)
    act_low, gate_in, up_in, normed_rows = gate_up(gather_tokens(normed_two), ffn_full, f_width)
    layer_out = hidden + scatter_tokens(*rows_back(act_low, ffn_full, 2, "down"))
    grad_layer = loss_scale * validity * (layer_out - teacher_own)
    grad_gate_up, grad_rows = act_back(
        gather_tokens(grad_layer.astype(jnp.bfloat16)), ffn_full, gate_in, up_in
    )
    units_grad = weight_grads([(normed_rows, grad_gate_up)], "units_grads")
    units_grad, grad_gate_up = lax.optimization_barrier((units_grad, grad_gate_up))
    units_sum = scatter_grads(units_grad)
    grad_normed_two = scatter_tokens(*rows_back(grad_gate_up, ffn_full, 0, "normed_back"))

    weighted_two = gain_second * grad_normed_two
    grad_gain_two = jnp.sum(grad_normed_two * hidden * scale_two, axis=0)
    grad_hidden = (
        grad_layer
        + scale_two * weighted_two
        - hidden
        * (scale_two * scale_two * scale_two)
        * jnp.mean(weighted_two * hidden, axis=-1, keepdims=True)
    )
    grad_mixed, gate_low, gain_grad, grad_turned = gated_back(
        places, gather_tokens(grad_hidden.astype(jnp.bfloat16)), mixer_full, raw, mixed, gain_mixer
    )
    raw_low, taps_grad, vectors_grad = mixer_backward(
        boundary, grad_mixed, raw, conv_taps, vectors, saved
    )
    last_grad = weight_grads(
        [
            (grad_turned, gated_turned),
            (normed_one, gate_low),
            (normed_one, raw_low),
            (grad_rows, act_low),
        ],
        "mixer_grads",
    )
    last_grad, raw_low = lax.optimization_barrier((last_grad, raw_low))
    last_sum = scatter_grads(last_grad)
    grad_normed_one = scatter_tokens(*input_back(places, gate_low, raw_low, mixer_full))
    weighted_one = gain_first * grad_normed_one
    grad_gain_one = jnp.sum(grad_normed_one * input_float * scale_one, axis=0)
    grad_input = (
        grad_hidden
        + scale_one * weighted_one
        - input_float
        * (scale_one * scale_one * scale_one)
        * jnp.mean(weighted_one * input_float, axis=-1, keepdims=True)
    )

    gain_pair = features_out(jnp.stack([grad_gain_one, grad_gain_two]))
    features = gain_pair.shape[1]
    taps = taps_grad[:CONV]
    n_all = 2 * features + DV
    flat = jnp.concatenate(
        [
            gain_pair.reshape(-1),
            gain_grad[0],
            taps.reshape(-1),
            vectors_grad[:2, heads_here : 2 * heads_here].reshape(-1),
        ]
    )
    flat = jnp.pad(flat, (0, -flat.shape[0] % 1024)).reshape(-1, 128)
    flat = sum_over(flat, ("xl", "z", "y"))
    shared = sum_over(flat[: n_all // 128], ("xh", "c")).reshape(-1)
    flat = flat.reshape(-1)
    taps_sum = flat[n_all : n_all + taps.size].reshape(CONV, -1)
    heads_at = n_all + taps.size
    norm1_grad = lax.dynamic_slice_in_dim(shared, group_index * rows_dp, rows_dp)
    norm2_grad = lax.dynamic_slice_in_dim(shared, features + group_index * rows_dp, rows_dp)
    q_at = 2 * VW + v_width
    k_at = q_at + qk_width
    small_at = k_at + qk_width
    units_sum = units_sum.reshape(rows_dp, -1, 2, 128)
    return (
        features_out(layer_out),
        features_out(grad_input),
        norm1_grad,
        last_sum[:, q_at:k_at],
        last_sum[:, k_at:small_at],
        last_sum[:, 2 * VW : q_at],
        last_sum[:, VW : 2 * VW],
        last_sum[:, small_at : small_at + heads_here],
        last_sum[:, small_at + heads_here : small_at + 2 * heads_here],
        flat[heads_at : heads_at + heads_here],
        flat[heads_at + heads_here : heads_at + 2 * heads_here],
        taps_sum[:, v_width : v_width + qk_width],
        taps_sum[:, v_width + qk_width :],
        taps_sum[:, :v_width],
        shared[2 * features :],
        last_sum[:, :VW],
        norm2_grad,
        units_sum[:, :, 0].reshape(rows_dp, f_width),
        units_sum[:, :, 1].reshape(rows_dp, f_width),
        last_sum[:, VW + PROJ :],
    )


def solution(mesh):
    fine = Mesh(mesh.devices.reshape(2, 4, 4, 2, 2), ("xl", "z", "y", "xh", "c"))
    dp = ("xl", "z", "y")
    tensor = ("xh", "c")
    tokens = P(dp + tensor, None)
    weight = P(dp, tensor)
    gain = P(dp)
    heads = P(tensor)
    taps = P(None, tensor)
    in_specs = (
        (tokens, tokens, P(), gain)
        + (weight,) * 6
        + (heads, heads, taps, taps, taps, P(), weight, gain)
        + (weight,) * 3
    )
    out_specs = (
        (tokens, tokens, gain)
        + (weight,) * 6
        + (heads, heads, taps, taps, taps, P(), weight, gain)
        + (weight,) * 3
    )
    return jax.shard_map(shards, mesh=fine, in_specs=in_specs, out_specs=out_specs, check_vma=False)
```

```python
from functools import partial

import jax
import jax.numpy as jnp
from jax import lax
from jax.experimental import pallas as pl
from jax.experimental.pallas import tpu as pltpu
from jax.sharding import Mesh, PartitionSpec as P

DK = 128
DV = 256
CONV = 4
EPSILON = 1e-06
MIXER_FLOOR = 0.001
SPAN = 128
HEADS = 2
CHUNKS = 4
ROWS = SPAN * CHUNKS
QK = HEADS * DK
VW = HEADS * DV
CONVW = 2 * QK + VW
SMALL = 128
SMALL_AT = VW + CONVW
PROJ = SMALL_AT + SMALL
GATE_BLOCKS = VW // 128
Q_BLOCK = VW // 128
K_BLOCK = Q_BLOCK + HEADS
PAIRS = [(n, h) for n in range(CHUNKS) for h in range(HEADS)]
F32 = jnp.float32
BF16 = jnp.bfloat16


def contract(left, right, dims):
    return lax.dot_general(left, right, (dims, ((), ())), preferred_element_type=F32)


def halves(values):
    high = values.astype(BF16)
    return high, (values - high.astype(F32)).astype(BF16)


def dot_parts(left, right, dims):
    (lh, ll), (rh, rl) = left, right
    return contract(lh, rh, dims) + (contract(lh, rl, dims) + contract(ll, rh, dims))


NN = ((1,), (0,))
NT = ((1,), (1,))


def mm(left, right):
    return dot_parts(halves(left), halves(right), NN)


def mm_t(left, right):
    return dot_parts(halves(left), halves(right), NT)


def mm_exact(left, right):
    return lax.dot_general(
        left, right, (NN, ((), ())), precision=lax.Precision.HIGHEST, preferred_element_type=F32
    )


def iota(shape, axis):
    return lax.broadcasted_iota(jnp.int32, shape, axis)


def segment(position, first, second):
    return jnp.where(position >= first, 1, 0) + jnp.where(position >= second, 1, 0)


def silu(values):
    return values * jax.nn.sigmoid(values)


def silu_slope(values):
    s = jax.nn.sigmoid(values)
    return s * (1.0 + values * (1.0 - s))


def softplus(values):
    return jnp.maximum(values, 0.0) + jnp.log1p(jnp.exp(-jnp.abs(values)))


def invert_all(lowers):
    r, c = iota((SPAN, SPAN), 0), iota((SPAN, SPAN), 1)
    eye = jnp.where(r == c, 1.0, 0.0)
    near = (r >> 3) == (c >> 3)
    diag = [jnp.where(near, a, 0.0) for a in lowers]
    diag_parts = [halves(d) for d in diag]
    square = [dot_parts(d, d, NN) for d in diag_parts]
    square_parts = [halves(s) for s in square]
    fourth = [dot_parts(s, s, NN) for s in square_parts]
    inverse = [eye - d for d in diag]
    inverse = [x + dot_parts(halves(x), s, NN) for x, s in zip(inverse, square_parts)]
    inverse = [x + mm(x, s) for x, s in zip(inverse, fourth)]
    shift = 3
    while (1 << shift) < SPAN:
        corner = ((r >> (shift + 1)) == (c >> (shift + 1))) & ((r >> shift) != (c >> shift))
        parts = [halves(x) for x in inverse]
        moved = [
            dot_parts(halves(jnp.where(corner, a, 0.0)), x, NN) for a, x in zip(lowers, parts)
        ]
        inverse = [
            x - dot_parts(p, halves(m), NN) for x, p, m in zip(inverse, parts, moved)
        ]
        shift += 1
    return inverse


def chunk(n):
    return slice(n * SPAN, (n + 1) * SPAN)


def lanes(index, width=128):
    return slice(index * width, (index + 1) * width)


def row_scale(values):
    return lax.rsqrt(jnp.sum(values * values, axis=1, keepdims=True) + EPSILON)


def decay_terms(n, small, bias, rate, first, second):
    betas = jax.nn.sigmoid(small)
    decays = -rate * softplus(small + bias)
    r, c = iota((SPAN, SPAN), 0), iota((SPAN, SPAN), 1)
    total = mm_exact(jnp.where(c <= r, 1.0, 0.0), decays)
    turned = total.T
    position = iota((SPAN, 1), 0) + n * SPAN
    own = segment(position, first, second)
    ends = jnp.int32(n * SPAN + SPAN - 1)
    last = own == segment(ends, first, second)
    terms = []
    for h in range(HEADS):
        column = total[:, HEADS + h : HEADS + h + 1]
        if n:
            carried = own == segment(jnp.int32(n * SPAN - 1), first, second)
            growth = jnp.where(carried, jnp.exp(column), 0.0)
        else:
            growth = jnp.zeros((SPAN, 1), F32)
        final = column[SPAN - 1 : SPAN]
        fade = jnp.where(last, jnp.exp(jnp.where(last, final - column, 0.0)), 0.0)
        terms.append((betas[:, h : h + 1], column, turned[HEADS + h : HEADS + h + 1], growth, fade))
    return terms


def same_segment(n, first, second):
    r, c = iota((SPAN, SPAN), 0), iota((SPAN, SPAN), 1)
    base = n * SPAN
    return (segment(r + base, first, second) == segment(c + base, first, second)) & (c <= r)


def mixer_forward_kernel(
    bounds, raw, taps, vectors, gain, gated, conv, ratios, inner, scores, solved, written, states, mixed
):
    first, second = bounds[0], bounds[1]
    bias, rate = vectors[0:1], vectors[1:2]
    queries, keys, values, terms = {}, {}, {}, {}
    for n in range(CHUNKS):
        rows = chunk(n)
        position = iota((SPAN, 1), 0) + n * SPAN
        own = segment(position, first, second)
        joins = [
            jnp.where((position >= o) & (segment(position - o, first, second) == own), 1.0, 0.0)
            for o in range(1, CONV)
        ]

        def convolved(block):
            here = raw[rows, lanes(GATE_BLOCKS + block)]
            summed = here * taps[CONV - 1 : CONV, lanes(block)]
            for o in range(1, CONV):
                if n:
                    moved = raw[n * SPAN - o : (n + 1) * SPAN - o, lanes(GATE_BLOCKS + block)]
                else:
                    moved = pltpu.roll(here, o, 0)
                tap = taps[CONV - 1 - o : CONV - o, lanes(block)]
                summed = summed + tap * (moved * joins[o - 1])
            conv[rows, lanes(block)] = summed
            return silu(summed)

        for h in range(HEADS):
            q = convolved(Q_BLOCK + h)
            queries[n, h] = q * (row_scale(q) * DK ** (-0.5))
            k = convolved(K_BLOCK + h)
            keys[n, h] = k * row_scale(k)
            values[n, h] = jnp.concatenate(
                [convolved(2 * h), convolved(2 * h + 1)], axis=1
            )
        small = raw[rows, SMALL_AT:PROJ]
        for h, term in enumerate(decay_terms(n, small, bias, rate, first, second)):
            terms[n, h] = term

    r, c = iota((SPAN, SPAN), 0), iota((SPAN, SPAN), 1)
    key_parts = {p: halves(keys[p]) for p in PAIRS}
    query_parts = {p: halves(queries[p]) for p in PAIRS}
    lowers, score = [], {}
    for n in range(CHUNKS):
        causal = same_segment(n, first, second)
        for h in range(HEADS):
            p = (n, h)
            beta, column, row, growth, fade = terms[p]
            ratio = jnp.where(causal, jnp.exp(jnp.where(causal, column - row, 0.0)), 0.0)
            met = dot_parts(key_parts[p], key_parts[p], NT)
            lower = jnp.where(c < r, ratio * met, 0.0)
            score[p] = ratio * dot_parts(query_parts[p], key_parts[p], NT)
            at = n * HEADS + h
            ratios[at] = ratio
            inner[at] = lower
            scores[at] = score[p]
            lowers.append(beta * lower)
    inverses = invert_all(lowers)
    own_part, state_part, key_fade = {}, {}, {}
    for p, x in zip(PAIRS, inverses):
        n, h = p
        beta, column, row, growth, fade = terms[p]
        solved[n * HEADS + h] = x
        parts = halves(x)
        own_part[p] = dot_parts(parts, halves(beta * values[p]), NN)
        state_part[p] = halves(dot_parts(parts, halves((beta * growth) * keys[p]), NN))
        key_fade[p] = halves((fade * keys[p]).T)
    held = [jnp.zeros((DK, DV), F32) for h in range(HEADS)]
    for n in range(CHUNKS):
        for h in range(HEADS):
            p = (n, h)
            growth = terms[p][3]
            states[n * HEADS + h] = held[h]
            state = halves(held[h])
            wrote = own_part[p] - dot_parts(state_part[p], state, NN)
            wrote_parts = halves(wrote)
            written[chunk(n), lanes(h, DV)] = wrote
            out = growth * dot_parts(query_parts[p], state, NN)
            out = out + dot_parts(halves(score[p]), wrote_parts, NN)
            held[h] = growth[SPAN - 1 : SPAN] * held[h] + dot_parts(key_fade[p], wrote_parts, NN)
            mixed[chunk(n), lanes(h, DV)] = out
            scale = lax.rsqrt(jnp.mean(out * out, axis=1, keepdims=True) + MIXER_FLOOR)
            gate = raw[chunk(n), lanes(h, DV)]
            gated[chunk(n), lanes(h, DV)] = (out * scale * gain[...] * silu(gate)).astype(BF16)


def mixer_backward_kernel(
    bounds, grad_mixed, raw, taps, vectors, conv, ratios, inner, scores, solved, written, states,
    grad_raw, grad_taps, grad_vectors, slopes,
):
    first, second = bounds[0], bounds[1]
    bias, rate = vectors[0:1], vectors[1:2]
    r, c = iota((SPAN, SPAN), 0), iota((SPAN, SPAN), 1)
    lane = iota((SPAN, SMALL), 1)
    terms, queries, keys, values, grad_out = {}, {}, {}, {}, {}
    for n in range(CHUNKS):
        rows = chunk(n)
        small = raw[rows, SMALL_AT:PROJ]
        for h, term in enumerate(decay_terms(n, small, bias, rate, first, second)):
            p = (n, h)
            terms[p] = term
            q = silu(conv[rows, lanes(Q_BLOCK + h)])
            queries[p] = q * (row_scale(q) * DK ** (-0.5))
            k = silu(conv[rows, lanes(K_BLOCK + h)])
            keys[p] = k * row_scale(k)
            values[p] = silu(conv[rows, lanes(h, DV)])
            grad_out[p] = grad_mixed[rows, lanes(h, DV)]

    from_out, from_state, into_state, key_turned, out_parts = {}, {}, {}, {}, {}
    for p in PAIRS:
        n, h = p
        at = n * HEADS + h
        beta, column, row, growth, fade = terms[p]
        turned = halves(solved[at].T)
        out_parts[p] = halves(grad_out[p])
        pulled = dot_parts(halves(scores[at].T), out_parts[p], NN)
        from_out[p] = dot_parts(turned, halves(pulled), NN)
        from_state[p] = halves(dot_parts(turned, halves(fade * keys[p]), NN))
        into_state[p] = mm(queries[p].T, growth * grad_out[p])
        key_turned[p] = halves(((beta * growth) * keys[p]).T)
    held = [jnp.zeros((DK, DV), F32) for h in range(HEADS)]
    grad_target, grad_held, grad_held_parts = {}, {}, {}
    for n in reversed(range(CHUNKS)):
        for h in range(HEADS):
            p = (n, h)
            growth = terms[p][3]
            grad_held[p] = held[h]
            grad_held_parts[p] = halves(held[h])
            target = from_out[p] + dot_parts(from_state[p], grad_held_parts[p], NN)
            grad_target[p] = halves(target), target
            kept = growth[SPAN - 1 : SPAN] * held[h] + into_state[p]
            held[h] = kept - dot_parts(key_turned[p], grad_target[p][0], NN)

    log_sum = jnp.zeros((1, SMALL), F32)
    bias_sum = jnp.zeros((1, SMALL), F32)
    for n in range(CHUNKS):
        rows = chunk(n)
        grad_total = jnp.zeros((SPAN, SMALL), F32)
        grad_beta = jnp.zeros((SPAN, SMALL), F32)
        for h in range(HEADS):
            p = (n, h)
            at = n * HEADS + h
            beta, column, row, growth, fade = terms[p]
            target_parts, target = grad_target[p]
            state = states[at]
            state_parts = halves(state)
            wrote_parts = halves(written[rows, lanes(h, DV)])
            q, k, v = queries[p], keys[p], values[p]
            q_parts, k_parts = halves(q), halves(k)
            score, lower, ratio = scores[at], inner[at], ratios[at]
            out_state = dot_parts(out_parts[p], state_parts, NT)
            target_state = dot_parts(target_parts, state_parts, NT)
            wrote_state = dot_parts(wrote_parts, grad_held_parts[p], NT)
            grad_score = dot_parts(out_parts[p], wrote_parts, NT)
            grad_lower = -dot_parts(target_parts, wrote_parts, NT)
            grad_met = beta * grad_lower * jnp.where(c < r, ratio, 0.0)
            grad_pair = grad_score * ratio
            recall = jnp.sum(target_state * k, axis=1, keepdims=True)
            grad_growth = jnp.sum(out_state * q, axis=1, keepdims=True) - beta * recall
            beta_col = jnp.sum(target * v, axis=1, keepdims=True) - growth * recall
            beta_col = beta_col + jnp.sum(grad_lower * lower, axis=1, keepdims=True)
            faded = jnp.sum(wrote_state * k, axis=1, keepdims=True) * fade
            grad_q = growth * out_state + dot_parts(halves(grad_pair), k_parts, NN)
            grad_k = fade * wrote_state - (beta * growth) * target_state
            grad_k = grad_k + dot_parts(halves(grad_pair.T), q_parts, NN)
            grad_k = grad_k + dot_parts(halves(grad_met + grad_met.T), k_parts, NN)
            grad_v = beta * target
            held_grad = jnp.sum(state * grad_held[p], axis=1, keepdims=True)
            at_end = jnp.sum(held_grad, axis=0, keepdims=True) * growth[SPAN - 1 : SPAN]
            at_end = at_end + jnp.sum(faded, axis=0, keepdims=True)
            moved = grad_score * score + beta * (grad_lower * lower)
            col = jnp.sum(moved, axis=1, keepdims=True) - jnp.sum(moved.T, axis=1, keepdims=True)
            col = col + grad_growth * growth - faded
            col = col + jnp.where(iota((SPAN, 1), 0) == SPAN - 1, at_end, 0.0)
            grad_total = jnp.where(lane == HEADS + h, col, grad_total)
            grad_beta = jnp.where(lane == h, beta_col, grad_beta)
            pre = conv[rows, lanes(Q_BLOCK + h)]
            raw_q = silu(pre)
            scale = row_scale(raw_q)
            along = jnp.sum(grad_q * raw_q, axis=1, keepdims=True)
            back = (grad_q - raw_q * ((scale * scale) * along)) * (scale * DK ** (-0.5))
            slopes[rows, lanes(Q_BLOCK + h)] = back * silu_slope(pre)
            pre = conv[rows, lanes(K_BLOCK + h)]
            raw_k = silu(pre)
            scale = row_scale(raw_k)
            along = jnp.sum(grad_k * raw_k, axis=1, keepdims=True)
            back = (grad_k - raw_k * ((scale * scale) * along)) * scale
            slopes[rows, lanes(K_BLOCK + h)] = back * silu_slope(pre)
            wide = lanes(h, DV)
            slopes[rows, wide] = grad_v * silu_slope(conv[rows, wide])
        grad_decays = mm_exact(jnp.where(c >= r, 1.0, 0.0), grad_total)
        small = raw[rows, SMALL_AT:PROJ]
        shifted = small + bias
        grad_step = -grad_decays * rate * jax.nn.sigmoid(shifted)
        betas = jax.nn.sigmoid(small)
        grad_raw[rows, CONVW : CONVW + SMALL] = (
            grad_beta * betas * (1.0 - betas) + grad_step
        ).astype(BF16)
        bias_sum = bias_sum + jnp.sum(grad_step, axis=0, keepdims=True)
        log_sum = log_sum - jnp.sum(
            grad_decays * rate * softplus(shifted), axis=0, keepdims=True
        )
    grad_vectors[0:1] = log_sum
    grad_vectors[1:2] = bias_sum

    slopes[ROWS : ROWS + 8] = jnp.zeros((8, CONVW), F32)
    for block in range(CONVW // 128):
        sums = [jnp.zeros((1, 128), F32) for o in range(CONV)]
        for n in range(CHUNKS):
            rows = chunk(n)
            position = iota((SPAN, 1), 0) + n * SPAN
            own = segment(position, first, second)
            here = raw[rows, lanes(GATE_BLOCKS + block)]
            total = jnp.zeros((SPAN, 128), F32)
            for o in range(CONV):
                moved = slopes[n * SPAN + o : (n + 1) * SPAN + o, lanes(block)]
                if o:
                    moved = jnp.where(segment(position + o, first, second) == own, moved, 0.0)
                total = total + taps[CONV - 1 - o : CONV - o, lanes(block)] * moved
                sums[o] = sums[o] + jnp.sum(moved * here, axis=0, keepdims=True)
            grad_raw[rows, lanes(block)] = total.astype(BF16)
        for o in range(CONV):
            grad_taps[CONV - 1 - o : CONV - o, lanes(block)] = sums[o]


def lasting(micros):
    return pl.CostEstimate(
        flops=int(micros * 1e9), transcendentals=0, bytes_accessed=int(micros * 3e6)
    )


def vmem(count):
    return [pl.BlockSpec(memory_space=pltpu.VMEM)] * count


LIMIT = pltpu.CompilerParams(vmem_limit_bytes=56 * 1024 * 1024)
SMEM = pl.BlockSpec(memory_space=pltpu.SMEM)
SAVED = [
    jax.ShapeDtypeStruct((ROWS, CONVW), F32),
    jax.ShapeDtypeStruct((len(PAIRS), SPAN, SPAN), F32),
    jax.ShapeDtypeStruct((len(PAIRS), SPAN, SPAN), F32),
    jax.ShapeDtypeStruct((len(PAIRS), SPAN, SPAN), F32),
    jax.ShapeDtypeStruct((len(PAIRS), SPAN, SPAN), F32),
    jax.ShapeDtypeStruct((ROWS, VW), F32),
    jax.ShapeDtypeStruct((len(PAIRS), DK, DV), F32),
    jax.ShapeDtypeStruct((ROWS, VW), F32),
]


def mixer_forward(bounds, raw, taps, vectors, gain):
    outs = [jax.ShapeDtypeStruct((ROWS, VW), BF16)] + SAVED
    return pl.pallas_call(
        mixer_forward_kernel,
        out_shape=outs,
        in_specs=[SMEM] + vmem(4),
        out_specs=vmem(len(outs)),
        compiler_params=LIMIT,
        cost_estimate=lasting(12.5),
        name="mixer_forward",
    )(bounds, raw, taps, vectors, gain)


def mixer_backward(bounds, grad_mixed, raw, taps, vectors, saved):
    outs = [
        jax.ShapeDtypeStruct((ROWS, CONVW + SMALL), BF16),
        jax.ShapeDtypeStruct((8, CONVW), F32),
        jax.ShapeDtypeStruct((8, SMALL), F32),
    ]
    return pl.pallas_call(
        mixer_backward_kernel,
        out_shape=outs,
        in_specs=[SMEM] + vmem(4 + len(saved)),
        out_specs=vmem(len(outs)),
        scratch_shapes=[pltpu.VMEM((ROWS + 8, CONVW), F32)],
        compiler_params=LIMIT,
        cost_estimate=lasting(18.5),
        name="mixer_backward",
    )(bounds, grad_mixed, raw, taps, vectors, *saved)


TN = ((0,), (0,))
OWN = ROWS // 4
TILE = 512
STEP = 512
WIDE = 384
HALF = 768


def whole(*shape):
    return pl.BlockSpec(shape, lambda i: (0,) * len(shape))


def place_rows(places, j):
    return pl.ds(pl.multiple_of(places[j] * OWN, OWN), OWN)


def project_kernel(places, x0, x1, x2, x3, small, weights, raw, normed, gains, steps):
    step = pl.program_id(0)

    @pl.when(step == 0)
    def prepare():
        r, c = iota((8, SMALL), 0), iota((8, SMALL), 1)
        pick = jnp.where((r < 2) & (c == r + 2 * HEADS), 1.0, 0.0).astype(BF16)
        gains[...] = contract(pick, small[...], NT)
        for j, x in enumerate((x0, x1, x2, x3)):
            values = x[...].astype(F32)
            scale = lax.rsqrt(jnp.mean(values * values, axis=1, keepdims=True) + EPSILON)
            low = (values * scale * gains[0:1]).astype(BF16)
            rows = place_rows(places, j)
            normed[rows, :] = low
            for s in range(steps.shape[0]):
                steps[s, rows, :] = low[:, s * STEP : (s + 1) * STEP]

    product = contract(steps[step], weights[:, VW:], NN)

    @pl.when(step == 0)
    def start():
        raw[...] = product

    @pl.when(step > 0)
    def add():
        raw[...] += product


def project(places, blocks, weights):
    features = weights.shape[0]
    count = features // STEP
    return pl.pallas_call(
        project_kernel,
        grid=(count,),
        out_shape=[
            jax.ShapeDtypeStruct((ROWS, PROJ), F32),
            jax.ShapeDtypeStruct((ROWS, features), BF16),
            jax.ShapeDtypeStruct((8, features), F32),
        ],
        in_specs=[SMEM]
        + [whole(OWN, features)] * 4
        + [
            pl.BlockSpec((features, SMALL), lambda i: (0, (VW + SMALL_AT) // SMALL)),
            pl.BlockSpec((STEP, VW + PROJ), lambda i: (i, 0)),
        ],
        out_specs=[whole(ROWS, PROJ), whole(ROWS, features), whole(8, features)],
        scratch_shapes=[pltpu.VMEM((count, ROWS, STEP), BF16)],
        compiler_params=LIMIT,
        cost_estimate=lasting(12),
        name="project",
    )(places, *blocks, weights, weights)


def split_rows(product, kept_other, sent_other, kept_own, sent_own):
    kept_own[...] = product[:OWN]
    sent_own[...] = product[OWN : 2 * OWN].astype(BF16)
    kept_other[...] = product[2 * OWN : 3 * OWN]
    sent_other[...] = product[3 * OWN :].astype(BF16)


def split_outs(features):
    shape = (OWN, features)
    pair = [jax.ShapeDtypeStruct(shape, F32), jax.ShapeDtypeStruct(shape, BF16)]
    return pair * 2, [pl.BlockSpec((OWN, TILE), lambda i: (0, i))] * 4


def mix_out_kernel(places, gated, weights, kept_other, sent_other, kept_own, sent_own, turned):
    @pl.when(pl.program_id(0) == 0)
    def prepare():
        for j in range(4):
            turned[j * OWN : (j + 1) * OWN] = gated[place_rows(places, j), :]

    split_rows(
        contract(turned[...], weights[...], NT), kept_other, sent_other, kept_own, sent_own
    )


def mix_out(places, gated, weights):
    features = weights.shape[0]
    outs, specs = split_outs(features)
    return pl.pallas_call(
        mix_out_kernel,
        grid=(features // TILE,),
        out_shape=outs + [jax.ShapeDtypeStruct((ROWS, VW), BF16)],
        in_specs=[SMEM, whole(ROWS, VW), pl.BlockSpec((TILE, VW), lambda i: (i, 0))],
        out_specs=specs + [whole(ROWS, VW)],
        compiler_params=LIMIT,
        cost_estimate=lasting(5),
        name="mix_out",
    )(places, gated, weights)


def gate_up_kernel(x0, x1, x2, x3, weights, act, gate, up, rows, held, *, units):
    step = pl.program_id(0)

    for j, x in enumerate((x0, x1, x2, x3)):

        @pl.when(step == 0)
        def prepare():
            held[j * OWN : (j + 1) * OWN] = x[...]

        @pl.when(step == j)
        def keep():
            rows[...] = x[...]

    for q in range(WIDE // 128):

        @pl.when(step * WIDE + q * 128 < units)
        def pair():
            product = contract(held[...], weights[:, lanes(q, 256)], NN)
            gate_in, up_in = product[:, :128], product[:, 128:]
            gate[:, lanes(q)] = gate_in
            up[:, lanes(q)] = up_in
            act[:, lanes(q)] = (silu(gate_in) * up_in).astype(BF16)


def gate_up(blocks, weights, units):
    features = weights.shape[0]
    tile = pl.BlockSpec((ROWS, WIDE), lambda i: (0, i))
    return pl.pallas_call(
        partial(gate_up_kernel, units=units),
        grid=(pl.cdiv(units, WIDE),),
        out_shape=[
            jax.ShapeDtypeStruct((ROWS, units), BF16),
            jax.ShapeDtypeStruct((ROWS, units), F32),
            jax.ShapeDtypeStruct((ROWS, units), F32),
            jax.ShapeDtypeStruct((ROWS, features), BF16),
        ],
        in_specs=[whole(OWN, features)] * 4
        + [pl.BlockSpec((features, 2 * WIDE), lambda i: (0, i))],
        out_specs=[
            tile,
            tile,
            tile,
            pl.BlockSpec((OWN, features), lambda i: (jnp.minimum(i, 3), 0)),
        ],
        scratch_shapes=[pltpu.VMEM((ROWS, features), BF16)],
        compiler_params=LIMIT,
        cost_estimate=lasting(12.5),
        name="gate_up",
    )(*blocks, weights)


def half_back_kernel(left, weights, kept, sent):
    product = contract(left[...], weights[...], NT)
    kept[...] = product[:OWN]
    sent[...] = product[OWN:].astype(BF16)


def half_back(left, part, weights, block, tile, micros, name):
    features = weights.shape[0]
    width = left.shape[1]
    shape = (OWN, features)
    return pl.pallas_call(
        half_back_kernel,
        grid=(features // tile,),
        out_shape=[jax.ShapeDtypeStruct(shape, F32), jax.ShapeDtypeStruct(shape, BF16)],
        in_specs=[
            pl.BlockSpec((2 * OWN, width), lambda i: (part, 0)),
            pl.BlockSpec((tile, width), lambda i: (i, block)),
        ],
        out_specs=[pl.BlockSpec((OWN, tile), lambda i: (0, i))] * 2,
        compiler_params=LIMIT,
        cost_estimate=lasting(micros),
        name=name,
    )(left, weights)


def down_first_kernel(left, low, low_across, *refs):
    *high, kept, sent, weights = refs
    for b in range(low.shape[0] // 64):
        for o, half in enumerate((low, low_across)):
            rows = slice(b * 128 + o * 64, b * 128 + o * 64 + 64)
            weights[rows, :HALF] = half[b * 64 : b * 64 + 64]
    for i, block in enumerate(high):
        weights[:, HALF + i * 128 : HALF + (i + 1) * 128] = block[...]
    product = contract(left[...], weights[...], NT)
    kept[...] = product[:OWN]
    sent[...] = product[OWN:].astype(BF16)


def down_first(left, part, low, low_across, full):
    features = full.shape[0]
    width = left.shape[1]
    tile = 2 * STEP
    shape = (OWN, features)
    half = pl.BlockSpec((tile // 2, HALF), lambda i: (i, 0))
    column = pl.BlockSpec((OWN, tile), lambda i: (0, i))
    blocks = range((full.shape[1] + HALF - width) // 128, full.shape[1] // 128)
    return pl.pallas_call(
        down_first_kernel,
        grid=(features // tile,),
        out_shape=[
            jax.ShapeDtypeStruct(shape, F32),
            jax.ShapeDtypeStruct(shape, BF16),
            jax.ShapeDtypeStruct((features, width), BF16),
        ],
        in_specs=[pl.BlockSpec((2 * OWN, width), lambda i: (part, 0)), half, half]
        + [pl.BlockSpec((tile, 128), partial(lambda b, i: (i, b), b)) for b in blocks],
        out_specs=[column, column, pl.BlockSpec((tile, width), lambda i: (i, 0))],
        compiler_params=LIMIT,
        cost_estimate=lasting(6),
        name="down_first",
    )(left, low, low_across, *[full] * len(blocks))


def act_back_kernel(x0, x1, weights, gate, up, grads, rows, steps, total, gates, ups):
    step = pl.program_id(0)

    for j, x in enumerate((x0, x1)):
        at = slice(j * OWN, (j + 1) * OWN)

        @pl.when(step == 0)
        def prepare():
            for s in range(steps.shape[0]):
                steps[s, at, :] = x[:, s * STEP : (s + 1) * STEP]

        @pl.when(step == j)
        def keep():
            rows[...] = x[...]
            gates[at] = gate[...]
            ups[at] = up[...]

    product = contract(steps[step], weights[...], NN)

    @pl.when(step == 0)
    def start():
        total[...] = product

    @pl.when(step > 0)
    def add():
        total[...] += product

    @pl.when(step == pl.num_programs(0) - 1)
    def finish():
        for b in range(total.shape[1] // 128):
            grad, gate_in, up_in = total[:, lanes(b)], gates[:, lanes(b)], ups[:, lanes(b)]
            s = jax.nn.sigmoid(gate_in)
            grads[:, lanes(2 * b)] = (grad * up_in * s * (1.0 + gate_in * (1.0 - s))).astype(BF16)
            grads[:, lanes(2 * b + 1)] = (grad * gate_in * s).astype(BF16)


def act_back(blocks, part, weights, block, gate, up):
    features = weights.shape[0]
    units = gate.shape[1]
    count = features // STEP
    rows = pl.BlockSpec((OWN, units), lambda i: (2 * part + jnp.minimum(i, 1), 0))
    return pl.pallas_call(
        act_back_kernel,
        grid=(count,),
        out_shape=[
            jax.ShapeDtypeStruct((2 * OWN, 2 * units), BF16),
            jax.ShapeDtypeStruct((2 * OWN, features), BF16),
        ],
        in_specs=[whole(OWN, features)] * 2
        + [pl.BlockSpec((STEP, units), lambda i: (i, block)), rows, rows],
        out_specs=[
            whole(2 * OWN, 2 * units),
            pl.BlockSpec((OWN, features), lambda i: (jnp.minimum(i, 1), 0)),
        ],
        scratch_shapes=[
            pltpu.VMEM((count, 2 * OWN, STEP), BF16),
            pltpu.VMEM((2 * OWN, units), F32),
            pltpu.VMEM((2 * OWN, units), F32),
            pltpu.VMEM((2 * OWN, units), F32),
        ],
        compiler_params=LIMIT,
        cost_estimate=lasting(8),
        name="act_back",
    )(*blocks, weights, gate, up)


def gated_back_kernel(
    places, x0, x1, x2, x3, weights, raw_gate, mixed, gain, grad_mixed, grad_gate, grad_gain, turned
):
    gain_sum = jnp.zeros((1, DV), F32)
    for j, x in enumerate((x0, x1, x2, x3)):
        turned[j * OWN : (j + 1) * OWN] = x[...]
        grads = contract(x[...], weights[...], NN)
        rows = place_rows(places, j)
        for h in range(HEADS):
            out = mixed[rows, lanes(h, DV)]
            gate = raw_gate[rows, lanes(h, DV)]
            grad = grads[:, lanes(h, DV)]
            scale = lax.rsqrt(jnp.mean(out * out, axis=1, keepdims=True) + MIXER_FLOOR)
            opened = grad * silu(gate)
            scaled = out * scale
            gain_sum = gain_sum + jnp.sum(opened * scaled, axis=0, keepdims=True)
            grad_gate[rows, lanes(h, DV)] = (
                grad * scaled * gain[...] * silu_slope(gate)
            ).astype(BF16)
            inward = opened * gain[...]
            along = jnp.mean(inward * out, axis=1, keepdims=True)
            grad_mixed[rows, lanes(h, DV)] = scale * inward - out * (
                (scale * scale * scale) * along
            )
    grad_gain[0:1] = gain_sum


def gated_back(places, blocks, weights, raw, mixed, gain):
    features = weights.shape[0]
    return pl.pallas_call(
        gated_back_kernel,
        grid=(1,),
        out_shape=[
            jax.ShapeDtypeStruct((ROWS, VW), F32),
            jax.ShapeDtypeStruct((ROWS, VW), BF16),
            jax.ShapeDtypeStruct((8, DV), F32),
            jax.ShapeDtypeStruct((ROWS, features), BF16),
        ],
        in_specs=[SMEM]
        + [whole(OWN, features)] * 4
        + [whole(features, VW), whole(ROWS, VW), whole(ROWS, VW), whole(1, DV)],
        out_specs=[whole(ROWS, VW), whole(ROWS, VW), whole(8, DV), whole(ROWS, features)],
        compiler_params=LIMIT,
        cost_estimate=lasting(6.5),
        name="gated_back",
    )(places, *blocks, weights, raw, mixed, gain)


def input_back_kernel(
    places, gate, conv, weights, kept_other, sent_other, kept_own, sent_own, turned
):
    @pl.when(pl.program_id(0) == 0)
    def prepare():
        for j in range(4):
            rows = place_rows(places, j)
            turned[j * OWN : (j + 1) * OWN, :VW] = gate[rows, :]
            turned[j * OWN : (j + 1) * OWN, VW:] = conv[rows, :]

    split_rows(
        contract(turned[...], weights[:, VW:], NT), kept_other, sent_other, kept_own, sent_own
    )


def input_back(places, gate, conv, weights):
    features = weights.shape[0]
    outs, specs = split_outs(features)
    return pl.pallas_call(
        input_back_kernel,
        grid=(features // TILE,),
        out_shape=outs,
        in_specs=[
            SMEM,
            whole(ROWS, VW),
            whole(ROWS, CONVW + SMALL),
            pl.BlockSpec((TILE, VW + PROJ), lambda i: (i, 0)),
        ],
        out_specs=specs,
        scratch_shapes=[pltpu.VMEM((ROWS, PROJ), BF16)],
        compiler_params=LIMIT,
        cost_estimate=lasting(8.5),
        name="input_back",
    )(places, gate, conv, weights)


def grads_kernel(counts, *refs):
    out = refs[-1]
    at, used = 0, 0
    for count in counts:
        total = contract(refs[used][...], refs[used + 1][...], TN)
        for i in range(1, count):
            total = total + contract(refs[used + 2 * i][...], refs[used + 2 * i + 1][...], TN)
        used += 2 * count
        width = total.shape[1]
        out[:, at : at + width] = total.astype(BF16)
        at += width


def weight_grads(groups, micros, name):
    operands, specs, counts, width = [], [], [], 0
    for group in groups:
        counts.append(len(group))
        for left, right in group:
            (left, part), (right, other) = left, right
            rows = min(left.shape[0], right.shape[0])
            operands += [left, right]
            specs += [
                pl.BlockSpec((rows, STEP), partial(lambda p, i: (p, i), part)),
                pl.BlockSpec((rows, right.shape[1]), partial(lambda p, i: (p, 0), other)),
            ]
        width += right.shape[1]
    features = groups[0][0][0][0].shape[1]
    return pl.pallas_call(
        partial(grads_kernel, counts),
        grid=(features // STEP,),
        out_shape=jax.ShapeDtypeStruct((features, width), BF16),
        in_specs=specs,
        out_specs=pl.BlockSpec((STEP, width), lambda i: (i, 0)),
        compiler_params=LIMIT,
        cost_estimate=lasting(micros),
        name=name,
    )(*operands)


def pack_kernel(*refs):
    out = refs[-1]
    at = 0
    for ref in refs[:-1]:
        out[:, at : at + ref.shape[1]] = ref[...]
        at += ref.shape[1]


def pack(*blocks):
    shape = (blocks[0].shape[0], sum(block.shape[1] for block in blocks))
    return pl.pallas_call(
        pack_kernel,
        out_shape=jax.ShapeDtypeStruct(shape, BF16),
        in_specs=vmem(len(blocks)),
        out_specs=pl.BlockSpec(memory_space=pltpu.VMEM),
        compiler_params=LIMIT,
        cost_estimate=lasting(1.7),
        name="pack",
    )(*blocks)


def pack_both_kernel(count, *refs):
    rows = refs[0].shape[0]
    out = refs[-1]
    at = 0
    for i in range(count):
        width = refs[2 * i].shape[1]
        out[:rows, at : at + width] = refs[2 * i][...]
        out[rows:, at : at + width] = refs[2 * i + 1][...]
        at += width
    for ref in refs[2 * count : -1]:
        half = ref.shape[1] // 2
        out[:rows, at : at + half] = ref[:, :half]
        out[rows:, at : at + half] = ref[:, half:]
        at += half


def pack_both(pairs, *halved):
    rows = pairs[0][0].shape[0]
    width = sum(own.shape[1] for own, other in pairs) + sum(b.shape[1] for b in halved) // 2
    operands = [block for pair in pairs for block in pair] + list(halved)
    return pl.pallas_call(
        partial(pack_both_kernel, len(pairs)),
        out_shape=jax.ShapeDtypeStruct((2 * rows, width), BF16),
        in_specs=vmem(len(operands)),
        out_specs=pl.BlockSpec(memory_space=pltpu.VMEM),
        compiler_params=LIMIT,
        cost_estimate=lasting(2),
        name="pack_both",
    )(*operands)


SWAP = [(0, 1), (1, 0)]
PLANE = ("z", "y")


def trade(values, axis):
    return lax.ppermute(values, axis, SWAP)


def gather_tokens(own):
    across = trade(own, "xh")
    return own, trade(own, "c"), across, trade(across, "c")


def scatter_tokens(kept_other, sent_other, kept_own, sent_own):
    other = kept_other + trade(sent_other, "c").astype(jnp.float32)
    own = kept_own + trade(sent_own, "c").astype(jnp.float32)
    return own + trade(other.astype(jnp.bfloat16), "xh").astype(jnp.float32)


def scatter_halves(far, near, operand):
    kept, sent = far
    low = (kept + trade(sent, "c").astype(jnp.float32)).astype(jnp.bfloat16)
    low, operand = lax.optimization_barrier((low, operand))
    kept, sent = near(operand)
    own = kept + trade(sent, "c").astype(jnp.float32)
    return own + trade(low, "xh").astype(jnp.float32)


def gather_plane(block):
    return lax.all_gather(block, PLANE, axis=0, tiled=False).reshape(-1, block.shape[1])


def scatter_grads(grads):
    both = lax.psum_scatter(grads, PLANE, scatter_dimension=0, tiled=True)
    both = both.reshape(2, -1, grads.shape[1])
    return both[0].astype(jnp.float32) + trade(both[1], "xl").astype(jnp.float32)


def features_in(rows):
    count = rows.shape[0]
    halves = rows.reshape(count, 2, -1)
    flip = lax.axis_index("xl") == 1
    first = jnp.where(flip, halves[:, 1], halves[:, 0]).reshape(count, 16, 64)
    second = jnp.where(flip, halves[:, 0], halves[:, 1]).reshape(count, 16, 64)
    return jnp.concatenate([first, second], axis=2).reshape(count, -1)


def features_out(rows):
    count = rows.shape[0]
    blocks = rows.reshape(count, 16, 2, 64)
    flip = lax.axis_index("xl") == 1
    first = blocks[:, :, 0].reshape(count, -1)
    second = blocks[:, :, 1].reshape(count, -1)
    low = jnp.where(flip, second, first)
    high = jnp.where(flip, first, second)
    return jnp.concatenate([low, high], axis=1)


def sum_over(values, axes):
    for axis in axes:
        size = lax.axis_size(axis)
        step = 1
        while step < size:
            values = values + lax.ppermute(values, axis, [(i, i ^ step) for i in range(size)])
            step *= 2
    return values


def shards(
    layer_input,
    teacher_out,
    lengths,
    norm1_gain,
    query_weight,
    key_weight,
    value_weight,
    output_gate,
    beta_weight,
    decay_weight,
    decay_log,
    step_bias,
    query_taps,
    key_taps,
    value_taps,
    mixer_gain,
    out_weight,
    norm2_gain,
    gate_weight,
    up_weight,
    down_weight,
):
    tok_rows = layer_input.shape[0]
    rows_dp = norm1_gain.shape[0]
    group_index = lax.axis_index("xl") * 16 + lax.axis_index("z") * 4 + lax.axis_index("y")
    half, core = lax.axis_index("xh"), lax.axis_index("c")
    tensor_index = half * 2 + core
    places = jnp.stack(
        [tensor_index, 2 * half + 1 - core, 2 - 2 * half + core, 3 - tensor_index]
    ).astype(jnp.int32)
    heads_here = decay_log.shape[0]
    own_lengths = lax.dynamic_index_in_dim(lengths, group_index, 0, keepdims=False)
    boundary = jnp.cumsum(own_lengths)
    own_rows = tensor_index * tok_rows + jnp.arange(tok_rows, dtype=jnp.int32)
    validity = (own_rows < boundary[-1]).astype(jnp.float32)[:, None]
    loss_scale = jnp.float32(128 * tok_rows) / jnp.sum(lengths).astype(jnp.float32)

    qk_width = query_taps.shape[1]
    v_width = value_taps.shape[1]
    f_width = gate_weight.shape[1]
    filler = jnp.zeros((rows_dp, SMALL - 2 * heads_here - 2), jnp.bfloat16)
    mixer_block = pack(out_weight, output_gate, value_weight, query_weight, key_weight)
    small_block = jnp.concatenate(
        [beta_weight, decay_weight, norm1_gain[:, None], norm2_gain[:, None], filler], axis=1
    )
    paired_units = jnp.stack(
        [gate_weight.reshape(rows_dp, -1, 128), up_weight.reshape(rows_dp, -1, 128)], axis=2
    ).reshape(rows_dp, 2 * f_width)
    mixer_full = gather_plane(
        pack_both(
            [(mixer_block, trade(mixer_block, "xl")), (small_block, trade(small_block, "xl"))],
            down_weight[:, :HALF],
        )
    )
    ffn_block = jnp.concatenate([paired_units, down_weight[:, HALF:]], axis=1)
    ffn_full = gather_plane(pack_both([(ffn_block, trade(ffn_block, "xl"))]))
    input_own = features_in(layer_input)
    teacher_own = features_in(teacher_out).astype(jnp.float32)
    conv_taps = jnp.concatenate([value_taps, query_taps, key_taps], axis=1).astype(jnp.float32)
    vectors = jnp.pad(
        jnp.stack([step_bias, jnp.exp(decay_log)]),
        ((0, 6), (heads_here, SMALL - 2 * heads_here)),
    )
    gain_mixer = mixer_gain.astype(jnp.float32)[None, :]

    mixer_full, *input_blocks = lax.optimization_barrier((mixer_full, *gather_tokens(input_own)))
    down_low = mixer_full[:, VW + PROJ :].reshape(16, 2, rows_dp, HALF // 2)
    down_low = down_low.swapaxes(1, 2).reshape(-1, HALF)
    down_low, mixer_full = lax.optimization_barrier((down_low, mixer_full))
    low_across = trade(down_low, "xl")
    raw, normed_one, gains = project(places, input_blocks, mixer_full)
    gain_first, gain_second = gains[0:1], gains[1:2]
    input_float = input_own.astype(jnp.float32)
    scale_one = lax.rsqrt(jnp.mean(input_float * input_float, axis=-1, keepdims=True) + EPSILON)
    gated_low, *saved, mixed = mixer_forward(boundary, raw, conv_taps, vectors, gain_mixer)
    gated_low, low_across = lax.optimization_barrier((gated_low, low_across))
    *terms, gated_turned = mix_out(places, gated_low, mixer_full)
    hidden = input_float + scatter_tokens(*terms)
    scale_two = lax.rsqrt(jnp.mean(hidden * hidden, axis=-1, keepdims=True) + EPSILON)
    normed_two = (hidden * scale_two * gain_second).astype(jnp.bfloat16)
    blocks = gather_tokens(normed_two)
    act_low, gate_in, up_in, normed_rows = gate_up(blocks, ffn_full, f_width)
    *far, down_full = down_first(act_low, 1, down_low, low_across, ffn_full)
    layer_out = hidden + scatter_halves(
        far, lambda act: half_back(act, 0, down_full, 0, 1024, 5, "down_near"), act_low
    )
    grad_layer = loss_scale * validity * (layer_out - teacher_own)
    grad_low = grad_layer.astype(jnp.bfloat16)
    across = trade(grad_low, "xh")
    grads_near, rows_near = act_back(
        (grad_low, trade(grad_low, "c")), 0, down_full, 0, gate_in, up_in
    )
    across, grads_near = lax.optimization_barrier((across, grads_near))
    grads_far, rows_far = act_back(
        (across, trade(across, "c")), 1, down_full, 0, gate_in, up_in
    )
    units_grad = weight_grads(
        [[((normed_rows, 0), (grads_near, 0)), ((normed_rows, 1), (grads_far, 0))]], 10.5, "units_grads"
    )
    units_grad, grads_far, grads_near = lax.optimization_barrier((units_grad, grads_far, grads_near))
    units_sum = scatter_grads(units_grad)
    far = half_back(grads_far, 0, ffn_full, 0, 512, 8, "normed_far")
    grad_normed_two = scatter_halves(
        far, lambda grads: half_back(grads, 0, ffn_full, 0, 512, 8, "normed_near"), grads_near
    )

    weighted_two = gain_second * grad_normed_two
    grad_gain_two = jnp.sum(grad_normed_two * hidden * scale_two, axis=0)
    grad_hidden = (
        grad_layer
        + scale_two * weighted_two
        - hidden
        * (scale_two * scale_two * scale_two)
        * jnp.mean(weighted_two * hidden, axis=-1, keepdims=True)
    )
    grad_mixed, gate_low, gain_grad, grad_turned = gated_back(
        places, gather_tokens(grad_hidden.astype(jnp.bfloat16)), mixer_full, raw, mixed, gain_mixer
    )
    raw_low, taps_grad, vectors_grad = mixer_backward(
        boundary, grad_mixed, raw, conv_taps, vectors, saved
    )
    last_grad = weight_grads(
        [
            [((grad_turned, 0), (gated_turned, 0))],
            [((normed_one, 0), (gate_low, 0))],
            [((normed_one, 0), (raw_low, 0))],
            [((rows_near, 0), (act_low, 0)), ((rows_far, 0), (act_low, 1))],
        ],
        14.5,
        "mixer_grads",
    )
    last_grad, raw_low = lax.optimization_barrier((last_grad, raw_low))
    last_sum = scatter_grads(last_grad)
    grad_normed_one = scatter_tokens(*input_back(places, gate_low, raw_low, mixer_full))
    weighted_one = gain_first * grad_normed_one
    grad_gain_one = jnp.sum(grad_normed_one * input_float * scale_one, axis=0)
    grad_input = (
        grad_hidden
        + scale_one * weighted_one
        - input_float
        * (scale_one * scale_one * scale_one)
        * jnp.mean(weighted_one * input_float, axis=-1, keepdims=True)
    )

    gain_pair = features_out(jnp.stack([grad_gain_one, grad_gain_two]))
    features = gain_pair.shape[1]
    taps = taps_grad[:CONV]
    n_all = 2 * features + DV
    flat = jnp.concatenate(
        [
            gain_pair.reshape(-1),
            gain_grad[0],
            taps.reshape(-1),
            vectors_grad[:2, heads_here : 2 * heads_here].reshape(-1),
        ]
    )
    flat = jnp.pad(flat, (0, -flat.shape[0] % 1024)).reshape(-1, 128)
    flat = sum_over(flat, ("xl", "z", "y"))
    shared = sum_over(flat[: n_all // 128], ("xh", "c")).reshape(-1)
    flat = flat.reshape(-1)
    taps_sum = flat[n_all : n_all + taps.size].reshape(CONV, -1)
    heads_at = n_all + taps.size
    norm1_grad = lax.dynamic_slice_in_dim(shared, group_index * rows_dp, rows_dp)
    norm2_grad = lax.dynamic_slice_in_dim(shared, features + group_index * rows_dp, rows_dp)
    q_at = 2 * VW + v_width
    k_at = q_at + qk_width
    small_at = k_at + qk_width
    units_sum = units_sum.reshape(rows_dp, -1, 2, 128)
    return (
        features_out(layer_out),
        features_out(grad_input),
        norm1_grad,
        last_sum[:, q_at:k_at],
        last_sum[:, k_at:small_at],
        last_sum[:, 2 * VW : q_at],
        last_sum[:, VW : 2 * VW],
        last_sum[:, small_at : small_at + heads_here],
        last_sum[:, small_at + heads_here : small_at + 2 * heads_here],
        flat[heads_at : heads_at + heads_here],
        flat[heads_at + heads_here : heads_at + 2 * heads_here],
        taps_sum[:, v_width : v_width + qk_width],
        taps_sum[:, v_width + qk_width :],
        taps_sum[:, :v_width],
        shared[2 * features :],
        last_sum[:, :VW],
        norm2_grad,
        units_sum[:, :, 0].reshape(rows_dp, f_width),
        units_sum[:, :, 1].reshape(rows_dp, f_width),
        last_sum[:, VW + PROJ :],
    )


def solution(mesh):
    fine = Mesh(mesh.devices.reshape(2, 4, 4, 2, 2), ("xl", "z", "y", "xh", "c"))
    dp = ("xl", "z", "y")
    tensor = ("xh", "c")
    tokens = P(dp + tensor, None)
    weight = P(dp, tensor)
    gain = P(dp)
    heads = P(tensor)
    taps = P(None, tensor)
    in_specs = (
        (tokens, tokens, P(), gain)
        + (weight,) * 6
        + (heads, heads, taps, taps, taps, P(), weight, gain)
        + (weight,) * 3
    )
    out_specs = (
        (tokens, tokens, gain)
        + (weight,) * 6
        + (heads, heads, taps, taps, taps, P(), weight, gain)
        + (weight,) * 3
    )
    return jax.shard_map(shards, mesh=fine, in_specs=in_specs, out_specs=out_specs, check_vma=False)
```

```python
from functools import partial

import jax
import jax.numpy as jnp
from jax import lax
from jax.experimental import pallas as pl
from jax.experimental.pallas import tpu as pltpu
from jax.sharding import Mesh, PartitionSpec as P

DK = 128
DV = 256
CONV = 4
EPSILON = 1e-06
MIXER_FLOOR = 0.001
SPAN = 128
HEADS = 2
CHUNKS = 4
ROWS = SPAN * CHUNKS
QK = HEADS * DK
VW = HEADS * DV
CONVW = 2 * QK + VW
SMALL = 128
SMALL_AT = VW + CONVW
PROJ = SMALL_AT + SMALL
GATE_BLOCKS = VW // 128
Q_BLOCK = VW // 128
K_BLOCK = Q_BLOCK + HEADS
PAIRS = [(n, h) for n in range(CHUNKS) for h in range(HEADS)]
F32 = jnp.float32
BF16 = jnp.bfloat16


def contract(left, right, dims):
    return lax.dot_general(left, right, (dims, ((), ())), preferred_element_type=F32)


def halves(values):
    high = values.astype(BF16)
    return high, (values - high.astype(F32)).astype(BF16)


def dot_parts(left, right, dims):
    (lh, ll), (rh, rl) = left, right
    return contract(lh, rh, dims) + (contract(lh, rl, dims) + contract(ll, rh, dims))


NN = ((1,), (0,))
NT = ((1,), (1,))


def mm(left, right):
    return dot_parts(halves(left), halves(right), NN)


def mm_t(left, right):
    return dot_parts(halves(left), halves(right), NT)


def mm_exact(left, right):
    return lax.dot_general(
        left, right, (NN, ((), ())), precision=lax.Precision.HIGHEST, preferred_element_type=F32
    )


def iota(shape, axis):
    return lax.broadcasted_iota(jnp.int32, shape, axis)


def segment(position, first, second):
    return jnp.where(position >= first, 1, 0) + jnp.where(position >= second, 1, 0)


def silu(values):
    return values * jax.nn.sigmoid(values)


def silu_slope(values):
    s = jax.nn.sigmoid(values)
    return s * (1.0 + values * (1.0 - s))


def softplus(values):
    return jnp.maximum(values, 0.0) + jnp.log1p(jnp.exp(-jnp.abs(values)))


def invert_all(lowers):
    r, c = iota((SPAN, SPAN), 0), iota((SPAN, SPAN), 1)
    eye = jnp.where(r == c, 1.0, 0.0)
    near = (r >> 3) == (c >> 3)
    diag = [jnp.where(near, a, 0.0) for a in lowers]
    diag_parts = [halves(d) for d in diag]
    square = [dot_parts(d, d, NN) for d in diag_parts]
    square_parts = [halves(s) for s in square]
    fourth = [dot_parts(s, s, NN) for s in square_parts]
    inverse = [eye - d for d in diag]
    inverse = [x + dot_parts(halves(x), s, NN) for x, s in zip(inverse, square_parts)]
    inverse = [x + mm(x, s) for x, s in zip(inverse, fourth)]
    shift = 3
    while (1 << shift) < SPAN:
        corner = ((r >> (shift + 1)) == (c >> (shift + 1))) & ((r >> shift) != (c >> shift))
        parts = [halves(x) for x in inverse]
        moved = [
            dot_parts(halves(jnp.where(corner, a, 0.0)), x, NN) for a, x in zip(lowers, parts)
        ]
        inverse = [
            x - dot_parts(p, halves(m), NN) for x, p, m in zip(inverse, parts, moved)
        ]
        shift += 1
    return inverse


def chunk(n):
    return slice(n * SPAN, (n + 1) * SPAN)


def lanes(index, width=128):
    return slice(index * width, (index + 1) * width)


def row_scale(values):
    return lax.rsqrt(jnp.sum(values * values, axis=1, keepdims=True) + EPSILON)


def decay_terms(n, small, bias, rate, first, second):
    betas = jax.nn.sigmoid(small)
    decays = -rate * softplus(small + bias)
    r, c = iota((SPAN, SPAN), 0), iota((SPAN, SPAN), 1)
    total = mm_exact(jnp.where(c <= r, 1.0, 0.0), decays)
    turned = total.T
    position = iota((SPAN, 1), 0) + n * SPAN
    own = segment(position, first, second)
    ends = jnp.int32(n * SPAN + SPAN - 1)
    last = own == segment(ends, first, second)
    terms = []
    for h in range(HEADS):
        column = total[:, HEADS + h : HEADS + h + 1]
        if n:
            carried = own == segment(jnp.int32(n * SPAN - 1), first, second)
            growth = jnp.where(carried, jnp.exp(column), 0.0)
        else:
            growth = jnp.zeros((SPAN, 1), F32)
        final = column[SPAN - 1 : SPAN]
        fade = jnp.where(last, jnp.exp(jnp.where(last, final - column, 0.0)), 0.0)
        terms.append((betas[:, h : h + 1], column, turned[HEADS + h : HEADS + h + 1], growth, fade))
    return terms


def same_segment(n, first, second):
    r, c = iota((SPAN, SPAN), 0), iota((SPAN, SPAN), 1)
    base = n * SPAN
    return (segment(r + base, first, second) == segment(c + base, first, second)) & (c <= r)


def mixer_forward_kernel(
    bounds, raw, taps, vectors, gain, gated, conv, ratios, inner, scores, solved, written, states, mixed
):
    first, second = bounds[0], bounds[1]
    bias, rate = vectors[0:1], vectors[1:2]
    queries, keys, values, terms = {}, {}, {}, {}
    for n in range(CHUNKS):
        rows = chunk(n)
        position = iota((SPAN, 1), 0) + n * SPAN
        own = segment(position, first, second)
        joins = [
            jnp.where((position >= o) & (segment(position - o, first, second) == own), 1.0, 0.0)
            for o in range(1, CONV)
        ]

        def convolved(block):
            here = raw[rows, lanes(GATE_BLOCKS + block)]
            summed = here * taps[CONV - 1 : CONV, lanes(block)]
            for o in range(1, CONV):
                if n:
                    moved = raw[n * SPAN - o : (n + 1) * SPAN - o, lanes(GATE_BLOCKS + block)]
                else:
                    moved = pltpu.roll(here, o, 0)
                tap = taps[CONV - 1 - o : CONV - o, lanes(block)]
                summed = summed + tap * (moved * joins[o - 1])
            conv[rows, lanes(block)] = summed
            return silu(summed)

        for h in range(HEADS):
            q = convolved(Q_BLOCK + h)
            queries[n, h] = q * (row_scale(q) * DK ** (-0.5))
            k = convolved(K_BLOCK + h)
            keys[n, h] = k * row_scale(k)
            values[n, h] = jnp.concatenate(
                [convolved(2 * h), convolved(2 * h + 1)], axis=1
            )
        small = raw[rows, SMALL_AT:PROJ]
        for h, term in enumerate(decay_terms(n, small, bias, rate, first, second)):
            terms[n, h] = term

    r, c = iota((SPAN, SPAN), 0), iota((SPAN, SPAN), 1)
    key_parts = {p: halves(keys[p]) for p in PAIRS}
    query_parts = {p: halves(queries[p]) for p in PAIRS}
    lowers, score = [], {}
    for n in range(CHUNKS):
        causal = same_segment(n, first, second)
        for h in range(HEADS):
            p = (n, h)
            beta, column, row, growth, fade = terms[p]
            ratio = jnp.where(causal, jnp.exp(jnp.where(causal, column - row, 0.0)), 0.0)
            met = dot_parts(key_parts[p], key_parts[p], NT)
            lower = jnp.where(c < r, ratio * met, 0.0)
            score[p] = ratio * dot_parts(query_parts[p], key_parts[p], NT)
            at = n * HEADS + h
            ratios[at] = ratio
            inner[at] = lower
            scores[at] = score[p]
            lowers.append(beta * lower)
    inverses = invert_all(lowers)
    own_part, state_part, key_fade = {}, {}, {}
    for p, x in zip(PAIRS, inverses):
        n, h = p
        beta, column, row, growth, fade = terms[p]
        solved[n * HEADS + h] = x
        parts = halves(x)
        own_part[p] = dot_parts(parts, halves(beta * values[p]), NN)
        state_part[p] = halves(dot_parts(parts, halves((beta * growth) * keys[p]), NN))
        key_fade[p] = halves((fade * keys[p]).T)
    held = [jnp.zeros((DK, DV), F32) for h in range(HEADS)]
    for n in range(CHUNKS):
        for h in range(HEADS):
            p = (n, h)
            growth = terms[p][3]
            states[n * HEADS + h] = held[h]
            state = halves(held[h])
            wrote = own_part[p] - dot_parts(state_part[p], state, NN)
            wrote_parts = halves(wrote)
            written[chunk(n), lanes(h, DV)] = wrote
            out = growth * dot_parts(query_parts[p], state, NN)
            out = out + dot_parts(halves(score[p]), wrote_parts, NN)
            held[h] = growth[SPAN - 1 : SPAN] * held[h] + dot_parts(key_fade[p], wrote_parts, NN)
            mixed[chunk(n), lanes(h, DV)] = out
            scale = lax.rsqrt(jnp.mean(out * out, axis=1, keepdims=True) + MIXER_FLOOR)
            gate = raw[chunk(n), lanes(h, DV)]
            gated[chunk(n), lanes(h, DV)] = (out * scale * gain[...] * silu(gate)).astype(BF16)


def mixer_backward_kernel(
    bounds, grad_mixed, raw, taps, vectors, conv, ratios, inner, scores, solved, written, states,
    grad_raw, grad_taps, grad_vectors, slopes,
):
    first, second = bounds[0], bounds[1]
    bias, rate = vectors[0:1], vectors[1:2]
    r, c = iota((SPAN, SPAN), 0), iota((SPAN, SPAN), 1)
    lane = iota((SPAN, SMALL), 1)
    terms, queries, keys, values, grad_out = {}, {}, {}, {}, {}
    for n in range(CHUNKS):
        rows = chunk(n)
        small = raw[rows, SMALL_AT:PROJ]
        for h, term in enumerate(decay_terms(n, small, bias, rate, first, second)):
            p = (n, h)
            terms[p] = term
            q = silu(conv[rows, lanes(Q_BLOCK + h)])
            queries[p] = q * (row_scale(q) * DK ** (-0.5))
            k = silu(conv[rows, lanes(K_BLOCK + h)])
            keys[p] = k * row_scale(k)
            values[p] = silu(conv[rows, lanes(h, DV)])
            grad_out[p] = grad_mixed[rows, lanes(h, DV)]

    from_out, from_state, into_state, key_turned, out_parts = {}, {}, {}, {}, {}
    for p in PAIRS:
        n, h = p
        at = n * HEADS + h
        beta, column, row, growth, fade = terms[p]
        turned = halves(solved[at].T)
        out_parts[p] = halves(grad_out[p])
        pulled = dot_parts(halves(scores[at].T), out_parts[p], NN)
        from_out[p] = dot_parts(turned, halves(pulled), NN)
        from_state[p] = halves(dot_parts(turned, halves(fade * keys[p]), NN))
        into_state[p] = mm(queries[p].T, growth * grad_out[p])
        key_turned[p] = halves(((beta * growth) * keys[p]).T)
    held = [jnp.zeros((DK, DV), F32) for h in range(HEADS)]
    grad_target, grad_held, grad_held_parts = {}, {}, {}
    for n in reversed(range(CHUNKS)):
        for h in range(HEADS):
            p = (n, h)
            growth = terms[p][3]
            grad_held[p] = held[h]
            grad_held_parts[p] = halves(held[h])
            target = from_out[p] + dot_parts(from_state[p], grad_held_parts[p], NN)
            grad_target[p] = halves(target), target
            kept = growth[SPAN - 1 : SPAN] * held[h] + into_state[p]
            held[h] = kept - dot_parts(key_turned[p], grad_target[p][0], NN)

    log_sum = jnp.zeros((1, SMALL), F32)
    bias_sum = jnp.zeros((1, SMALL), F32)
    for n in range(CHUNKS):
        rows = chunk(n)
        grad_total = jnp.zeros((SPAN, SMALL), F32)
        grad_beta = jnp.zeros((SPAN, SMALL), F32)
        for h in range(HEADS):
            p = (n, h)
            at = n * HEADS + h
            beta, column, row, growth, fade = terms[p]
            target_parts, target = grad_target[p]
            state = states[at]
            state_parts = halves(state)
            wrote_parts = halves(written[rows, lanes(h, DV)])
            q, k, v = queries[p], keys[p], values[p]
            q_parts, k_parts = halves(q), halves(k)
            score, lower, ratio = scores[at], inner[at], ratios[at]
            out_state = dot_parts(out_parts[p], state_parts, NT)
            target_state = dot_parts(target_parts, state_parts, NT)
            wrote_state = dot_parts(wrote_parts, grad_held_parts[p], NT)
            grad_score = dot_parts(out_parts[p], wrote_parts, NT)
            grad_lower = -dot_parts(target_parts, wrote_parts, NT)
            grad_met = beta * grad_lower * jnp.where(c < r, ratio, 0.0)
            grad_pair = grad_score * ratio
            recall = jnp.sum(target_state * k, axis=1, keepdims=True)
            grad_growth = jnp.sum(out_state * q, axis=1, keepdims=True) - beta * recall
            beta_col = jnp.sum(target * v, axis=1, keepdims=True) - growth * recall
            beta_col = beta_col + jnp.sum(grad_lower * lower, axis=1, keepdims=True)
            faded = jnp.sum(wrote_state * k, axis=1, keepdims=True) * fade
            grad_q = growth * out_state + dot_parts(halves(grad_pair), k_parts, NN)
            grad_k = fade * wrote_state - (beta * growth) * target_state
            grad_k = grad_k + dot_parts(halves(grad_pair.T), q_parts, NN)
            grad_k = grad_k + dot_parts(halves(grad_met + grad_met.T), k_parts, NN)
            grad_v = beta * target
            held_grad = jnp.sum(state * grad_held[p], axis=1, keepdims=True)
            at_end = jnp.sum(held_grad, axis=0, keepdims=True) * growth[SPAN - 1 : SPAN]
            at_end = at_end + jnp.sum(faded, axis=0, keepdims=True)
            moved = grad_score * score + beta * (grad_lower * lower)
            col = jnp.sum(moved, axis=1, keepdims=True) - jnp.sum(moved.T, axis=1, keepdims=True)
            col = col + grad_growth * growth - faded
            col = col + jnp.where(iota((SPAN, 1), 0) == SPAN - 1, at_end, 0.0)
            grad_total = jnp.where(lane == HEADS + h, col, grad_total)
            grad_beta = jnp.where(lane == h, beta_col, grad_beta)
            pre = conv[rows, lanes(Q_BLOCK + h)]
            raw_q = silu(pre)
            scale = row_scale(raw_q)
            along = jnp.sum(grad_q * raw_q, axis=1, keepdims=True)
            back = (grad_q - raw_q * ((scale * scale) * along)) * (scale * DK ** (-0.5))
            slopes[rows, lanes(Q_BLOCK + h)] = back * silu_slope(pre)
            pre = conv[rows, lanes(K_BLOCK + h)]
            raw_k = silu(pre)
            scale = row_scale(raw_k)
            along = jnp.sum(grad_k * raw_k, axis=1, keepdims=True)
            back = (grad_k - raw_k * ((scale * scale) * along)) * scale
            slopes[rows, lanes(K_BLOCK + h)] = back * silu_slope(pre)
            wide = lanes(h, DV)
            slopes[rows, wide] = grad_v * silu_slope(conv[rows, wide])
        grad_decays = mm_exact(jnp.where(c >= r, 1.0, 0.0), grad_total)
        small = raw[rows, SMALL_AT:PROJ]
        shifted = small + bias
        grad_step = -grad_decays * rate * jax.nn.sigmoid(shifted)
        betas = jax.nn.sigmoid(small)
        grad_raw[rows, CONVW : CONVW + SMALL] = (
            grad_beta * betas * (1.0 - betas) + grad_step
        ).astype(BF16)
        bias_sum = bias_sum + jnp.sum(grad_step, axis=0, keepdims=True)
        log_sum = log_sum - jnp.sum(
            grad_decays * rate * softplus(shifted), axis=0, keepdims=True
        )
    grad_vectors[0:1] = log_sum
    grad_vectors[1:2] = bias_sum

    slopes[ROWS : ROWS + 8] = jnp.zeros((8, CONVW), F32)
    for block in range(CONVW // 128):
        sums = [jnp.zeros((1, 128), F32) for o in range(CONV)]
        for n in range(CHUNKS):
            rows = chunk(n)
            position = iota((SPAN, 1), 0) + n * SPAN
            own = segment(position, first, second)
            here = raw[rows, lanes(GATE_BLOCKS + block)]
            total = jnp.zeros((SPAN, 128), F32)
            for o in range(CONV):
                moved = slopes[n * SPAN + o : (n + 1) * SPAN + o, lanes(block)]
                if o:
                    moved = jnp.where(segment(position + o, first, second) == own, moved, 0.0)
                total = total + taps[CONV - 1 - o : CONV - o, lanes(block)] * moved
                sums[o] = sums[o] + jnp.sum(moved * here, axis=0, keepdims=True)
            grad_raw[rows, lanes(block)] = total.astype(BF16)
        for o in range(CONV):
            grad_taps[CONV - 1 - o : CONV - o, lanes(block)] = sums[o]


def lasting(micros):
    return pl.CostEstimate(
        flops=int(micros * 1e9), transcendentals=0, bytes_accessed=int(micros * 3e6)
    )


def vmem(count):
    return [pl.BlockSpec(memory_space=pltpu.VMEM)] * count


LIMIT = pltpu.CompilerParams(vmem_limit_bytes=56 * 1024 * 1024)
SMEM = pl.BlockSpec(memory_space=pltpu.SMEM)
SAVED = [
    jax.ShapeDtypeStruct((ROWS, CONVW), F32),
    jax.ShapeDtypeStruct((len(PAIRS), SPAN, SPAN), F32),
    jax.ShapeDtypeStruct((len(PAIRS), SPAN, SPAN), F32),
    jax.ShapeDtypeStruct((len(PAIRS), SPAN, SPAN), F32),
    jax.ShapeDtypeStruct((len(PAIRS), SPAN, SPAN), F32),
    jax.ShapeDtypeStruct((ROWS, VW), F32),
    jax.ShapeDtypeStruct((len(PAIRS), DK, DV), F32),
    jax.ShapeDtypeStruct((ROWS, VW), F32),
]


def mixer_forward(bounds, raw, taps, vectors, gain):
    outs = [jax.ShapeDtypeStruct((ROWS, VW), BF16)] + SAVED
    return pl.pallas_call(
        mixer_forward_kernel,
        out_shape=outs,
        in_specs=[SMEM] + vmem(4),
        out_specs=vmem(len(outs)),
        compiler_params=LIMIT,
        cost_estimate=lasting(12.5),
        name="mixer_forward",
    )(bounds, raw, taps, vectors, gain)


def mixer_backward(bounds, grad_mixed, raw, taps, vectors, saved):
    outs = [
        jax.ShapeDtypeStruct((ROWS, CONVW + SMALL), BF16),
        jax.ShapeDtypeStruct((8, CONVW), F32),
        jax.ShapeDtypeStruct((8, SMALL), F32),
    ]
    return pl.pallas_call(
        mixer_backward_kernel,
        out_shape=outs,
        in_specs=[SMEM] + vmem(4 + len(saved)),
        out_specs=vmem(len(outs)),
        scratch_shapes=[pltpu.VMEM((ROWS + 8, CONVW), F32)],
        compiler_params=LIMIT,
        cost_estimate=lasting(18.5),
        name="mixer_backward",
    )(bounds, grad_mixed, raw, taps, vectors, *saved)


TN = ((0,), (0,))
OWN = ROWS // 4
TILE = 512
STEP = 512
WIDE = 384
HALF = 1024
FIRST = 768
EARLY = 512


def whole(*shape):
    return pl.BlockSpec(shape, lambda i: (0,) * len(shape))


def place_rows(places, j):
    return pl.ds(pl.multiple_of(places[j] * OWN, OWN), OWN)


def project_kernel(places, x0, x1, x2, x3, small, weights, raw, normed, gains, steps):
    step = pl.program_id(0)

    @pl.when(step == 0)
    def prepare():
        r, c = iota((8, SMALL), 0), iota((8, SMALL), 1)
        pick = jnp.where((r < 2) & (c == r + 2 * HEADS), 1.0, 0.0).astype(BF16)
        gains[...] = contract(pick, small[...], NT)
        for j, x in enumerate((x0, x1, x2, x3)):
            values = x[...].astype(F32)
            scale = lax.rsqrt(jnp.mean(values * values, axis=1, keepdims=True) + EPSILON)
            low = (values * scale * gains[0:1]).astype(BF16)
            rows = place_rows(places, j)
            normed[rows, :] = low
            for s in range(steps.shape[0]):
                steps[s, rows, :] = low[:, s * STEP : (s + 1) * STEP]

    product = contract(steps[step], weights[:, VW:], NN)

    @pl.when(step == 0)
    def start():
        raw[...] = product

    @pl.when(step > 0)
    def add():
        raw[...] += product


def project(places, blocks, weights):
    features = weights.shape[0]
    count = features // STEP
    return pl.pallas_call(
        project_kernel,
        grid=(count,),
        out_shape=[
            jax.ShapeDtypeStruct((ROWS, PROJ), F32),
            jax.ShapeDtypeStruct((ROWS, features), BF16),
            jax.ShapeDtypeStruct((8, features), F32),
        ],
        in_specs=[SMEM]
        + [whole(OWN, features)] * 4
        + [
            pl.BlockSpec((features, SMALL), lambda i: (0, (VW + SMALL_AT) // SMALL)),
            pl.BlockSpec((STEP, VW + PROJ), lambda i: (i, 0)),
        ],
        out_specs=[whole(ROWS, PROJ), whole(ROWS, features), whole(8, features)],
        scratch_shapes=[pltpu.VMEM((count, ROWS, STEP), BF16)],
        compiler_params=LIMIT,
        cost_estimate=lasting(12),
        name="project",
    )(places, *blocks, weights, weights)


def split_rows(product, kept_other, sent_other, kept_own, sent_own):
    kept_own[...] = product[:OWN]
    sent_own[...] = product[OWN : 2 * OWN].astype(BF16)
    kept_other[...] = product[2 * OWN : 3 * OWN]
    sent_other[...] = product[3 * OWN :].astype(BF16)


def split_outs(features):
    shape = (OWN, features)
    pair = [jax.ShapeDtypeStruct(shape, F32), jax.ShapeDtypeStruct(shape, BF16)]
    return pair * 2, [pl.BlockSpec((OWN, TILE), lambda i: (0, i))] * 4


def mix_out_kernel(places, gated, weights, kept_other, sent_other, kept_own, sent_own, turned):
    @pl.when(pl.program_id(0) == 0)
    def prepare():
        for j in range(4):
            turned[j * OWN : (j + 1) * OWN] = gated[place_rows(places, j), :]

    split_rows(
        contract(turned[...], weights[...], NT), kept_other, sent_other, kept_own, sent_own
    )


def mix_out(places, gated, weights):
    features = weights.shape[0]
    outs, specs = split_outs(features)
    return pl.pallas_call(
        mix_out_kernel,
        grid=(features // TILE,),
        out_shape=outs + [jax.ShapeDtypeStruct((ROWS, VW), BF16)],
        in_specs=[SMEM, whole(ROWS, VW), pl.BlockSpec((TILE, VW), lambda i: (i, 0))],
        out_specs=specs + [whole(ROWS, VW)],
        compiler_params=LIMIT,
        cost_estimate=lasting(5),
        name="mix_out",
    )(places, gated, weights)


def gate_up_kernel(x0, x1, x2, x3, weights, act, gate, up, rows, held, *, units):
    step = pl.program_id(0)

    for j, x in enumerate((x0, x1, x2, x3)):

        @pl.when(step == 0)
        def prepare():
            held[j * OWN : (j + 1) * OWN] = x[...]

        @pl.when(step == j)
        def keep():
            rows[...] = x[...]

    for q in range(WIDE // 128):

        @pl.when(step * WIDE + q * 128 < units)
        def pair():
            product = contract(held[...], weights[:, lanes(q, 256)], NN)
            gate_in, up_in = product[:, :128], product[:, 128:]
            gate[:, lanes(q)] = gate_in
            up[:, lanes(q)] = up_in
            act[:, lanes(q)] = (silu(gate_in) * up_in).astype(BF16)


def gate_up(blocks, weights, units):
    features = weights.shape[0]
    tile = pl.BlockSpec((ROWS, WIDE), lambda i: (0, i))
    return pl.pallas_call(
        partial(gate_up_kernel, units=units),
        grid=(pl.cdiv(units, WIDE),),
        out_shape=[
            jax.ShapeDtypeStruct((ROWS, units), BF16),
            jax.ShapeDtypeStruct((ROWS, units), F32),
            jax.ShapeDtypeStruct((ROWS, units), F32),
            jax.ShapeDtypeStruct((ROWS, features), BF16),
        ],
        in_specs=[whole(OWN, features)] * 4
        + [pl.BlockSpec((features, 2 * WIDE), lambda i: (0, i))],
        out_specs=[
            tile,
            tile,
            tile,
            pl.BlockSpec((OWN, features), lambda i: (jnp.minimum(i, 3), 0)),
        ],
        scratch_shapes=[pltpu.VMEM((ROWS, features), BF16)],
        compiler_params=LIMIT,
        cost_estimate=lasting(12.5),
        name="gate_up",
    )(*blocks, weights)


def half_back_kernel(left, weights, kept, sent):
    product = contract(left[...], weights[...], NT)
    kept[...] = product[:OWN]
    sent[...] = product[OWN:].astype(BF16)


def half_back(left, part, weights, block, tile, micros, name):
    features = weights.shape[0]
    width = left.shape[1]
    shape = (OWN, features)
    return pl.pallas_call(
        half_back_kernel,
        grid=(features // tile,),
        out_shape=[jax.ShapeDtypeStruct(shape, F32), jax.ShapeDtypeStruct(shape, BF16)],
        in_specs=[
            pl.BlockSpec((2 * OWN, width), lambda i: (part, 0)),
            pl.BlockSpec((tile, width), lambda i: (i, block)),
        ],
        out_specs=[pl.BlockSpec((OWN, tile), lambda i: (0, i))] * 2,
        compiler_params=LIMIT,
        cost_estimate=lasting(micros),
        name=name,
    )(left, weights)


def down_first_kernel(left, low, early, late, *refs):
    *high, kept, sent, weights = refs
    for b in range(low.shape[0] // 64):
        own = slice(b * 128, b * 128 + 64)
        other = slice(b * 128 + 64, b * 128 + 128)
        part = slice(b * 64, b * 64 + 64)
        weights[own, :HALF] = low[part]
        weights[other, :FIRST] = early[part]
        weights[other, FIRST:HALF] = late[part]
    for i, block in enumerate(high):
        weights[:, HALF + i * 128 : HALF + (i + 1) * 128] = block[...]
    product = contract(left[...], weights[...], NT)
    kept[...] = product[:OWN]
    sent[...] = product[OWN:].astype(BF16)


def down_first(left, part, low, early, late, full):
    features = full.shape[0]
    width = left.shape[1]
    tile = 2 * STEP
    shape = (OWN, features)
    parts = [
        pl.BlockSpec((tile // 2, half.shape[1]), lambda i: (i, 0)) for half in (low, early, late)
    ]
    column = pl.BlockSpec((OWN, tile), lambda i: (0, i))
    blocks = range((full.shape[1] + HALF - width) // 128, full.shape[1] // 128)
    return pl.pallas_call(
        down_first_kernel,
        grid=(features // tile,),
        out_shape=[
            jax.ShapeDtypeStruct(shape, F32),
            jax.ShapeDtypeStruct(shape, BF16),
            jax.ShapeDtypeStruct((features, width), BF16),
        ],
        in_specs=[pl.BlockSpec((2 * OWN, width), lambda i: (part, 0))]
        + parts
        + [pl.BlockSpec((tile, 128), partial(lambda b, i: (i, b), b)) for b in blocks],
        out_specs=[column, column, pl.BlockSpec((tile, width), lambda i: (i, 0))],
        compiler_params=LIMIT,
        cost_estimate=lasting(6),
        name="down_first",
    )(left, low, early, late, *[full] * len(blocks))


def act_back_kernel(x0, x1, weights, gate, up, grads, rows, steps, total, gates, ups):
    step = pl.program_id(0)

    for j, x in enumerate((x0, x1)):
        at = slice(j * OWN, (j + 1) * OWN)

        @pl.when(step == 0)
        def prepare():
            for s in range(steps.shape[0]):
                steps[s, at, :] = x[:, s * STEP : (s + 1) * STEP]

        @pl.when(step == j)
        def keep():
            rows[...] = x[...]
            gates[at] = gate[...]
            ups[at] = up[...]

    product = contract(steps[step], weights[...], NN)

    @pl.when(step == 0)
    def start():
        total[...] = product

    @pl.when(step > 0)
    def add():
        total[...] += product

    @pl.when(step == pl.num_programs(0) - 1)
    def finish():
        for b in range(total.shape[1] // 128):
            grad, gate_in, up_in = total[:, lanes(b)], gates[:, lanes(b)], ups[:, lanes(b)]
            s = jax.nn.sigmoid(gate_in)
            grads[:, lanes(2 * b)] = (grad * up_in * s * (1.0 + gate_in * (1.0 - s))).astype(BF16)
            grads[:, lanes(2 * b + 1)] = (grad * gate_in * s).astype(BF16)


def act_back(blocks, part, weights, block, gate, up):
    features = weights.shape[0]
    units = gate.shape[1]
    count = features // STEP
    rows = pl.BlockSpec((OWN, units), lambda i: (2 * part + jnp.minimum(i, 1), 0))
    return pl.pallas_call(
        act_back_kernel,
        grid=(count,),
        out_shape=[
            jax.ShapeDtypeStruct((2 * OWN, 2 * units), BF16),
            jax.ShapeDtypeStruct((2 * OWN, features), BF16),
        ],
        in_specs=[whole(OWN, features)] * 2
        + [pl.BlockSpec((STEP, units), lambda i: (i, block)), rows, rows],
        out_specs=[
            whole(2 * OWN, 2 * units),
            pl.BlockSpec((OWN, features), lambda i: (jnp.minimum(i, 1), 0)),
        ],
        scratch_shapes=[
            pltpu.VMEM((count, 2 * OWN, STEP), BF16),
            pltpu.VMEM((2 * OWN, units), F32),
            pltpu.VMEM((2 * OWN, units), F32),
            pltpu.VMEM((2 * OWN, units), F32),
        ],
        compiler_params=LIMIT,
        cost_estimate=lasting(8),
        name="act_back",
    )(*blocks, weights, gate, up)


def gated_back_kernel(
    places, x0, x1, x2, x3, weights, raw_gate, mixed, gain, grad_mixed, grad_gate, grad_gain, turned
):
    gain_sum = jnp.zeros((1, DV), F32)
    for j, x in enumerate((x0, x1, x2, x3)):
        turned[j * OWN : (j + 1) * OWN] = x[...]
        grads = contract(x[...], weights[...], NN)
        rows = place_rows(places, j)
        for h in range(HEADS):
            out = mixed[rows, lanes(h, DV)]
            gate = raw_gate[rows, lanes(h, DV)]
            grad = grads[:, lanes(h, DV)]
            scale = lax.rsqrt(jnp.mean(out * out, axis=1, keepdims=True) + MIXER_FLOOR)
            opened = grad * silu(gate)
            scaled = out * scale
            gain_sum = gain_sum + jnp.sum(opened * scaled, axis=0, keepdims=True)
            grad_gate[rows, lanes(h, DV)] = (
                grad * scaled * gain[...] * silu_slope(gate)
            ).astype(BF16)
            inward = opened * gain[...]
            along = jnp.mean(inward * out, axis=1, keepdims=True)
            grad_mixed[rows, lanes(h, DV)] = scale * inward - out * (
                (scale * scale * scale) * along
            )
    grad_gain[0:1] = gain_sum


def gated_back(places, blocks, weights, raw, mixed, gain):
    features = weights.shape[0]
    return pl.pallas_call(
        gated_back_kernel,
        grid=(1,),
        out_shape=[
            jax.ShapeDtypeStruct((ROWS, VW), F32),
            jax.ShapeDtypeStruct((ROWS, VW), BF16),
            jax.ShapeDtypeStruct((8, DV), F32),
            jax.ShapeDtypeStruct((ROWS, features), BF16),
        ],
        in_specs=[SMEM]
        + [whole(OWN, features)] * 4
        + [whole(features, VW), whole(ROWS, VW), whole(ROWS, VW), whole(1, DV)],
        out_specs=[whole(ROWS, VW), whole(ROWS, VW), whole(8, DV), whole(ROWS, features)],
        compiler_params=LIMIT,
        cost_estimate=lasting(6.5),
        name="gated_back",
    )(places, *blocks, weights, raw, mixed, gain)


def input_back_kernel(
    places, gate, conv, weights, kept_other, sent_other, kept_own, sent_own, turned
):
    @pl.when(pl.program_id(0) == 0)
    def prepare():
        for j in range(4):
            rows = place_rows(places, j)
            turned[j * OWN : (j + 1) * OWN, :VW] = gate[rows, :]
            turned[j * OWN : (j + 1) * OWN, VW:] = conv[rows, :]

    split_rows(
        contract(turned[...], weights[:, VW:], NT), kept_other, sent_other, kept_own, sent_own
    )


def input_back(places, gate, conv, weights):
    features = weights.shape[0]
    outs, specs = split_outs(features)
    return pl.pallas_call(
        input_back_kernel,
        grid=(features // TILE,),
        out_shape=outs,
        in_specs=[
            SMEM,
            whole(ROWS, VW),
            whole(ROWS, CONVW + SMALL),
            pl.BlockSpec((TILE, VW + PROJ), lambda i: (i, 0)),
        ],
        out_specs=specs,
        scratch_shapes=[pltpu.VMEM((ROWS, PROJ), BF16)],
        compiler_params=LIMIT,
        cost_estimate=lasting(8.5),
        name="input_back",
    )(places, gate, conv, weights)


def grads_kernel(counts, *refs):
    out = refs[-1]
    at, used = 0, 0
    for count in counts:
        total = contract(refs[used][...], refs[used + 1][...], TN)
        for i in range(1, count):
            total = total + contract(refs[used + 2 * i][...], refs[used + 2 * i + 1][...], TN)
        used += 2 * count
        width = total.shape[1]
        out[:, at : at + width] = total.astype(BF16)
        at += width


def weight_grads(groups, micros, name):
    operands, specs, counts, width = [], [], [], 0
    for group in groups:
        counts.append(len(group))
        for left, right in group:
            (left, part), (right, other) = left, right
            rows = min(left.shape[0], right.shape[0])
            operands += [left, right]
            specs += [
                pl.BlockSpec((rows, STEP), partial(lambda p, i: (p, i), part)),
                pl.BlockSpec((rows, right.shape[1]), partial(lambda p, i: (p, 0), other)),
            ]
        width += right.shape[1]
    features = groups[0][0][0][0].shape[1]
    return pl.pallas_call(
        partial(grads_kernel, counts),
        grid=(features // STEP,),
        out_shape=jax.ShapeDtypeStruct((features, width), BF16),
        in_specs=specs,
        out_specs=pl.BlockSpec((STEP, width), lambda i: (i, 0)),
        compiler_params=LIMIT,
        cost_estimate=lasting(micros),
        name=name,
    )(*operands)


def pack_kernel(*refs):
    out = refs[-1]
    at = 0
    for ref in refs[:-1]:
        out[:, at : at + ref.shape[1]] = ref[...]
        at += ref.shape[1]


def pack(*blocks):
    shape = (blocks[0].shape[0], sum(block.shape[1] for block in blocks))
    return pl.pallas_call(
        pack_kernel,
        out_shape=jax.ShapeDtypeStruct(shape, BF16),
        in_specs=vmem(len(blocks)),
        out_specs=pl.BlockSpec(memory_space=pltpu.VMEM),
        compiler_params=LIMIT,
        cost_estimate=lasting(1.7),
        name="pack",
    )(*blocks)


def pack_both_kernel(count, *refs):
    rows = refs[0].shape[0]
    out = refs[-1]
    at = 0
    for i in range(count):
        width = refs[2 * i].shape[1]
        out[:rows, at : at + width] = refs[2 * i][...]
        out[rows:, at : at + width] = refs[2 * i + 1][...]
        at += width
    for ref in refs[2 * count : -1]:
        half = ref.shape[1] // 2
        out[:rows, at : at + half] = ref[:, :half]
        out[rows:, at : at + half] = ref[:, half:]
        at += half


def pack_both(pairs, *halved):
    rows = pairs[0][0].shape[0]
    width = sum(own.shape[1] for own, other in pairs) + sum(b.shape[1] for b in halved) // 2
    operands = [block for pair in pairs for block in pair] + list(halved)
    return pl.pallas_call(
        partial(pack_both_kernel, len(pairs)),
        out_shape=jax.ShapeDtypeStruct((2 * rows, width), BF16),
        in_specs=vmem(len(operands)),
        out_specs=pl.BlockSpec(memory_space=pltpu.VMEM),
        compiler_params=LIMIT,
        cost_estimate=lasting(2),
        name="pack_both",
    )(*operands)


def down_part_kernel(left_a, right_a, left_b, right_b, own, other):
    product = contract(left_a[...], right_a[...], TN) + contract(left_b[...], right_b[...], TN)
    product = product.astype(BF16)
    for b in range(STEP // 128):
        own[b * 64 : b * 64 + 64] = product[b * 128 : b * 128 + 64]
        other[b * 64 : b * 64 + 64] = product[b * 128 + 64 : b * 128 + 128]


def down_part(near, far, act):
    features = near.shape[1]
    left = pl.BlockSpec((2 * OWN, STEP), lambda i: (0, i))
    return pl.pallas_call(
        down_part_kernel,
        grid=(features // STEP,),
        out_shape=[jax.ShapeDtypeStruct((features // 2, EARLY), BF16)] * 2,
        in_specs=[
            left,
            pl.BlockSpec((2 * OWN, EARLY), lambda i: (0, 0)),
            left,
            pl.BlockSpec((2 * OWN, EARLY), lambda i: (1, 0)),
        ],
        out_specs=[pl.BlockSpec((STEP // 2, EARLY), lambda i: (i, 0))] * 2,
        compiler_params=LIMIT,
        cost_estimate=lasting(3),
        name="down_part",
    )(near, act, far, act)


def last_grads_kernel(turned, gated, normed, gate, conv, near, far, act, own, other, out):
    here = normed[...]
    at = 0
    for left, right in ((turned[...], gated), (here, gate), (here, conv)):
        width = right.shape[1]
        out[:, at : at + width] = contract(left, right[...], TN).astype(BF16)
        at += width
    down = contract(near[...], act[: 2 * OWN, EARLY:], TN)
    down = down + contract(far[...], act[2 * OWN :, EARLY:], TN)
    out[:, at : at + down.shape[1]] = down.astype(BF16)
    at += down.shape[1]
    total = (own[...].astype(F32) + other[...].astype(F32)).astype(BF16)
    for b in range(STEP // 128):
        rows = slice(b * 64, b * 64 + 64)
        out[b * 128 : b * 128 + 64, at:] = total[rows, : EARLY // 2]
        out[b * 128 + 64 : b * 128 + 128, at:] = total[rows, EARLY // 2 :]


def last_grads(turned, gated, normed, gate, conv, near, far, act, own, other):
    features = normed.shape[1]
    width = VW + PROJ + act.shape[1] - EARLY // 2
    left = pl.BlockSpec((ROWS, STEP), lambda i: (0, i))
    half = pl.BlockSpec((2 * OWN, STEP), lambda i: (0, i))
    early = pl.BlockSpec((STEP // 2, EARLY), lambda i: (i, 0))
    return pl.pallas_call(
        last_grads_kernel,
        grid=(features // STEP,),
        out_shape=jax.ShapeDtypeStruct((features, width), BF16),
        in_specs=[
            left,
            whole(ROWS, VW),
            left,
            whole(ROWS, VW),
            whole(ROWS, CONVW + SMALL),
            half,
            half,
            whole(ROWS, act.shape[1]),
            early,
            early,
        ],
        out_specs=pl.BlockSpec((STEP, width), lambda i: (i, 0)),
        compiler_params=LIMIT,
        cost_estimate=lasting(13),
        name="last_grads",
    )(turned, gated, normed, gate, conv, near, far, act, own, other)


def finish_kernel(both, arrived, out, gate, value, query, key, beta, decay, down):
    rows = arrived.shape[0]

    def total(left, right):
        return both[:rows, left:right].astype(F32) + arrived[:, left:right].astype(F32)

    at = 0
    for ref in (out, gate, value, query, key):
        ref[...] = total(at, at + ref.shape[1])
        at += ref.shape[1]
    small = total(at, at + SMALL).T
    beta[...] = small[:HEADS]
    decay[...] = small[HEADS : 2 * HEADS]
    at += SMALL
    end = arrived.shape[1]
    down[:, : EARLY // 2] = both[:rows, end:].astype(F32)
    down[:, EARLY // 2 : EARLY] = both[rows:, end:].astype(F32)
    down[:, EARLY:] = total(at, end)


def finish(both, arrived, units):
    rows = arrived.shape[0]
    widths = (VW, VW, VW, QK, QK)
    return pl.pallas_call(
        finish_kernel,
        out_shape=[jax.ShapeDtypeStruct((rows, width), F32) for width in widths]
        + [jax.ShapeDtypeStruct((HEADS, rows), F32)] * 2
        + [jax.ShapeDtypeStruct((rows, units), F32)],
        in_specs=vmem(2),
        out_specs=vmem(8),
        compiler_params=LIMIT,
        cost_estimate=lasting(2),
        name="finish",
    )(both, arrived)


SWAP = [(0, 1), (1, 0)]
PLANE = ("z", "y")


def trade(values, axis):
    return lax.ppermute(values, axis, SWAP)


def gather_tokens(own):
    across = trade(own, "xh")
    return own, trade(own, "c"), across, trade(across, "c")


def scatter_tokens(kept_other, sent_other, kept_own, sent_own):
    other = kept_other + trade(sent_other, "c").astype(jnp.float32)
    own = kept_own + trade(sent_own, "c").astype(jnp.float32)
    return own + trade(other.astype(jnp.bfloat16), "xh").astype(jnp.float32)


def scatter_halves(far, near, operand):
    kept, sent = far
    low = (kept + trade(sent, "c").astype(jnp.float32)).astype(jnp.bfloat16)
    low, operand = lax.optimization_barrier((low, operand))
    kept, sent = near(operand)
    own = kept + trade(sent, "c").astype(jnp.float32)
    return own + trade(low, "xh").astype(jnp.float32)


def gather_plane(block):
    return lax.all_gather(block, PLANE, axis=0, tiled=False).reshape(-1, block.shape[1])


def scatter_grads(grads):
    both = lax.psum_scatter(grads, PLANE, scatter_dimension=0, tiled=True)
    both = both.reshape(2, -1, grads.shape[1])
    return both[0].astype(jnp.float32) + trade(both[1], "xl").astype(jnp.float32)


def features_in(rows):
    count = rows.shape[0]
    halves = rows.reshape(count, 2, -1)
    flip = lax.axis_index("xl") == 1
    first = jnp.where(flip, halves[:, 1], halves[:, 0]).reshape(count, 16, 64)
    second = jnp.where(flip, halves[:, 0], halves[:, 1]).reshape(count, 16, 64)
    return jnp.concatenate([first, second], axis=2).reshape(count, -1)


def features_out(rows):
    count = rows.shape[0]
    blocks = rows.reshape(count, 16, 2, 64)
    flip = lax.axis_index("xl") == 1
    first = blocks[:, :, 0].reshape(count, -1)
    second = blocks[:, :, 1].reshape(count, -1)
    low = jnp.where(flip, second, first)
    high = jnp.where(flip, first, second)
    return jnp.concatenate([low, high], axis=1)


def sum_over(values, axes):
    for axis in axes:
        size = lax.axis_size(axis)
        step = 1
        while step < size:
            values = values + lax.ppermute(values, axis, [(i, i ^ step) for i in range(size)])
            step *= 2
    return values


def shards(
    layer_input,
    teacher_out,
    lengths,
    norm1_gain,
    query_weight,
    key_weight,
    value_weight,
    output_gate,
    beta_weight,
    decay_weight,
    decay_log,
    step_bias,
    query_taps,
    key_taps,
    value_taps,
    mixer_gain,
    out_weight,
    norm2_gain,
    gate_weight,
    up_weight,
    down_weight,
):
    tok_rows = layer_input.shape[0]
    rows_dp = norm1_gain.shape[0]
    group_index = lax.axis_index("xl") * 16 + lax.axis_index("z") * 4 + lax.axis_index("y")
    half, core = lax.axis_index("xh"), lax.axis_index("c")
    tensor_index = half * 2 + core
    places = jnp.stack(
        [tensor_index, 2 * half + 1 - core, 2 - 2 * half + core, 3 - tensor_index]
    ).astype(jnp.int32)
    heads_here = decay_log.shape[0]
    own_lengths = lax.dynamic_index_in_dim(lengths, group_index, 0, keepdims=False)
    boundary = jnp.cumsum(own_lengths)
    own_rows = tensor_index * tok_rows + jnp.arange(tok_rows, dtype=jnp.int32)
    validity = (own_rows < boundary[-1]).astype(jnp.float32)[:, None]
    loss_scale = jnp.float32(128 * tok_rows) / jnp.sum(lengths).astype(jnp.float32)

    qk_width = query_taps.shape[1]
    v_width = value_taps.shape[1]
    f_width = gate_weight.shape[1]
    filler = jnp.zeros((rows_dp, SMALL - 2 * heads_here - 2), jnp.bfloat16)
    mixer_block = pack(out_weight, output_gate, value_weight, query_weight, key_weight)
    small_block = jnp.concatenate(
        [beta_weight, decay_weight, norm1_gain[:, None], norm2_gain[:, None], filler], axis=1
    )
    paired_units = jnp.stack(
        [gate_weight.reshape(rows_dp, -1, 128), up_weight.reshape(rows_dp, -1, 128)], axis=2
    ).reshape(rows_dp, 2 * f_width)
    mixer_full = gather_plane(
        pack_both(
            [(mixer_block, trade(mixer_block, "xl")), (small_block, trade(small_block, "xl"))],
            down_weight[:, :HALF],
        )
    )
    ffn_block = jnp.concatenate([paired_units, down_weight[:, HALF:]], axis=1)
    ffn_full = gather_plane(pack_both([(ffn_block, trade(ffn_block, "xl"))]))
    input_own = features_in(layer_input)
    teacher_own = features_in(teacher_out).astype(jnp.float32)
    conv_taps = jnp.concatenate([value_taps, query_taps, key_taps], axis=1).astype(jnp.float32)
    vectors = jnp.pad(
        jnp.stack([step_bias, jnp.exp(decay_log)]),
        ((0, 6), (heads_here, SMALL - 2 * heads_here)),
    )
    gain_mixer = mixer_gain.astype(jnp.float32)[None, :]

    mixer_full, *input_blocks = lax.optimization_barrier((mixer_full, *gather_tokens(input_own)))
    down_low = mixer_full[:, VW + PROJ :].reshape(16, 2, rows_dp, HALF // 2)
    down_low = down_low.swapaxes(1, 2).reshape(-1, HALF)
    low_first, low_last = down_low[:, :FIRST], down_low[:, FIRST:]
    low_first, mixer_full = lax.optimization_barrier((low_first, mixer_full))
    early = trade(low_first, "xl")
    raw, normed_one, gains = project(places, input_blocks, mixer_full)
    gain_first, gain_second = gains[0:1], gains[1:2]
    input_float = input_own.astype(jnp.float32)
    scale_one = lax.rsqrt(jnp.mean(input_float * input_float, axis=-1, keepdims=True) + EPSILON)
    gated_low, *saved, mixed = mixer_forward(boundary, raw, conv_taps, vectors, gain_mixer)
    gated_low, early = lax.optimization_barrier((gated_low, early))
    *terms, gated_turned = mix_out(places, gated_low, mixer_full)
    hidden = input_float + scatter_tokens(*terms)
    scale_two = lax.rsqrt(jnp.mean(hidden * hidden, axis=-1, keepdims=True) + EPSILON)
    normed_two = (hidden * scale_two * gain_second).astype(jnp.bfloat16)
    blocks = gather_tokens(normed_two)
    low_last, *blocks = lax.optimization_barrier((low_last, *blocks))
    late = trade(low_last, "xl")
    act_low, gate_in, up_in, normed_rows = gate_up(blocks, ffn_full, f_width)
    *far, down_full = down_first(act_low, 1, down_low, early, late, ffn_full)
    layer_out = hidden + scatter_halves(
        far, lambda act: half_back(act, 0, down_full, 0, 1024, 5, "down_near"), act_low
    )
    grad_layer = loss_scale * validity * (layer_out - teacher_own)
    grad_low = grad_layer.astype(jnp.bfloat16)
    across = trade(grad_low, "xh")
    grads_near, rows_near = act_back(
        (grad_low, trade(grad_low, "c")), 0, down_full, 0, gate_in, up_in
    )
    across, grads_near = lax.optimization_barrier((across, grads_near))
    grads_far, rows_far = act_back(
        (across, trade(across, "c")), 1, down_full, 0, gate_in, up_in
    )
    units_grad = weight_grads(
        [[((normed_rows, 0), (grads_near, 0)), ((normed_rows, 1), (grads_far, 0))]], 10.5, "units_grads"
    )
    units_grad, grads_far, grads_near = lax.optimization_barrier((units_grad, grads_far, grads_near))
    units_sum = scatter_grads(units_grad)
    far = half_back(grads_far, 0, ffn_full, 0, 512, 8, "normed_far")
    grad_normed_two = scatter_halves(
        far, lambda grads: half_back(grads, 0, ffn_full, 0, 512, 8, "normed_near"), grads_near
    )

    weighted_two = gain_second * grad_normed_two
    grad_gain_two = jnp.sum(grad_normed_two * hidden * scale_two, axis=0)
    grad_hidden = (
        grad_layer
        + scale_two * weighted_two
        - hidden
        * (scale_two * scale_two * scale_two)
        * jnp.mean(weighted_two * hidden, axis=-1, keepdims=True)
    )
    down_own, down_other = down_part(rows_near, rows_far, act_low)
    blocks = gather_tokens(grad_hidden.astype(jnp.bfloat16))
    down_other, *blocks = lax.optimization_barrier((down_other, *blocks))
    down_across = trade(down_other, "xl")
    grad_mixed, gate_low, gain_grad, grad_turned = gated_back(
        places, blocks, mixer_full, raw, mixed, gain_mixer
    )
    raw_low, taps_grad, vectors_grad = mixer_backward(
        boundary, grad_mixed, raw, conv_taps, vectors, saved
    )
    last_grad = last_grads(
        grad_turned,
        gated_turned,
        normed_one,
        gate_low,
        raw_low,
        rows_near,
        rows_far,
        act_low,
        down_own,
        down_across,
    )
    last_grad, raw_low = lax.optimization_barrier((last_grad, raw_low))
    last_both = lax.psum_scatter(last_grad, PLANE, scatter_dimension=0, tiled=True)
    last_arrived = trade(last_both[rows_dp:, : last_grad.shape[1] - EARLY // 2], "xl")
    out_grad, gate_grad, value_grad, query_grad, key_grad, beta_grad, decay_grad, down_grad = finish(
        last_both, last_arrived, f_width
    )
    grad_normed_one = scatter_tokens(*input_back(places, gate_low, raw_low, mixer_full))
    weighted_one = gain_first * grad_normed_one
    grad_gain_one = jnp.sum(grad_normed_one * input_float * scale_one, axis=0)
    grad_input = (
        grad_hidden
        + scale_one * weighted_one
        - input_float
        * (scale_one * scale_one * scale_one)
        * jnp.mean(weighted_one * input_float, axis=-1, keepdims=True)
    )

    gain_pair = features_out(jnp.stack([grad_gain_one, grad_gain_two]))
    features = gain_pair.shape[1]
    taps = taps_grad[:CONV]
    n_all = 2 * features + DV
    flat = jnp.concatenate(
        [
            gain_pair.reshape(-1),
            gain_grad[0],
            taps.reshape(-1),
            vectors_grad[:2, heads_here : 2 * heads_here].reshape(-1),
        ]
    )
    flat = jnp.pad(flat, (0, -flat.shape[0] % 1024)).reshape(-1, 128)
    flat = sum_over(flat, ("xl", "z", "y"))
    shared = sum_over(flat[: n_all // 128], ("xh", "c")).reshape(-1)
    flat = flat.reshape(-1)
    taps_sum = flat[n_all : n_all + taps.size].reshape(CONV, -1)
    heads_at = n_all + taps.size
    norm1_grad = lax.dynamic_slice_in_dim(shared, group_index * rows_dp, rows_dp)
    norm2_grad = lax.dynamic_slice_in_dim(shared, features + group_index * rows_dp, rows_dp)
    units_sum = units_sum.reshape(rows_dp, -1, 2, 128)
    return (
        features_out(layer_out),
        features_out(grad_input),
        norm1_grad,
        query_grad,
        key_grad,
        value_grad,
        gate_grad,
        beta_grad.T,
        decay_grad.T,
        flat[heads_at : heads_at + heads_here],
        flat[heads_at + heads_here : heads_at + 2 * heads_here],
        taps_sum[:, v_width : v_width + qk_width],
        taps_sum[:, v_width + qk_width :],
        taps_sum[:, :v_width],
        shared[2 * features :],
        out_grad,
        norm2_grad,
        units_sum[:, :, 0].reshape(rows_dp, f_width),
        units_sum[:, :, 1].reshape(rows_dp, f_width),
        down_grad,
    )


def solution(mesh):
    fine = Mesh(mesh.devices.reshape(2, 4, 4, 2, 2), ("xl", "z", "y", "xh", "c"))
    dp = ("xl", "z", "y")
    tensor = ("xh", "c")
    tokens = P(dp + tensor, None)
    weight = P(dp, tensor)
    gain = P(dp)
    heads = P(tensor)
    taps = P(None, tensor)
    in_specs = (
        (tokens, tokens, P(), gain)
        + (weight,) * 6
        + (heads, heads, taps, taps, taps, P(), weight, gain)
        + (weight,) * 3
    )
    out_specs = (
        (tokens, tokens, gain)
        + (weight,) * 6
        + (heads, heads, taps, taps, taps, P(), weight, gain)
        + (weight,) * 3
    )
    return jax.shard_map(shards, mesh=fine, in_specs=in_specs, out_specs=out_specs, check_vma=False)
```

```python
from functools import partial

import jax
import jax.numpy as jnp
from jax import lax
from jax.experimental import pallas as pl
from jax.experimental.pallas import tpu as pltpu
from jax.sharding import Mesh, PartitionSpec as P

DK = 128
DV = 256
CONV = 4
EPSILON = 1e-06
MIXER_FLOOR = 0.001
SPAN = 128
HEADS = 2
CHUNKS = 4
ROWS = SPAN * CHUNKS
QK = HEADS * DK
VW = HEADS * DV
CONVW = 2 * QK + VW
SMALL = 128
SMALL_AT = VW + CONVW
PROJ = SMALL_AT + SMALL
GATE_BLOCKS = VW // 128
Q_BLOCK = VW // 128
K_BLOCK = Q_BLOCK + HEADS
PAIRS = [(n, h) for n in range(CHUNKS) for h in range(HEADS)]
F32 = jnp.float32
BF16 = jnp.bfloat16


def contract(left, right, dims):
    return lax.dot_general(left, right, (dims, ((), ())), preferred_element_type=F32)


def halves(values):
    high = values.astype(BF16)
    return high, (values - high.astype(F32)).astype(BF16)


def dot_parts(left, right, dims):
    (lh, ll), (rh, rl) = left, right
    return contract(lh, rh, dims) + (contract(lh, rl, dims) + contract(ll, rh, dims))


NN = ((1,), (0,))
NT = ((1,), (1,))


def mm(left, right):
    return dot_parts(halves(left), halves(right), NN)


def mm_t(left, right):
    return dot_parts(halves(left), halves(right), NT)


def mm_exact(left, right):
    return lax.dot_general(
        left, right, (NN, ((), ())), precision=lax.Precision.HIGHEST, preferred_element_type=F32
    )


def iota(shape, axis):
    return lax.broadcasted_iota(jnp.int32, shape, axis)


def segment(position, first, second):
    return jnp.where(position >= first, 1, 0) + jnp.where(position >= second, 1, 0)


def silu(values):
    return values * jax.nn.sigmoid(values)


def silu_slope(values):
    s = jax.nn.sigmoid(values)
    return s * (1.0 + values * (1.0 - s))


def softplus(values):
    return jnp.maximum(values, 0.0) + jnp.log1p(jnp.exp(-jnp.abs(values)))


def invert_all(lowers):
    r, c = iota((SPAN, SPAN), 0), iota((SPAN, SPAN), 1)
    eye = jnp.where(r == c, 1.0, 0.0)
    near = (r >> 3) == (c >> 3)
    diag = [jnp.where(near, a, 0.0) for a in lowers]
    diag_parts = [halves(d) for d in diag]
    square = [dot_parts(d, d, NN) for d in diag_parts]
    square_parts = [halves(s) for s in square]
    fourth = [dot_parts(s, s, NN) for s in square_parts]
    inverse = [eye - d for d in diag]
    inverse = [x + dot_parts(halves(x), s, NN) for x, s in zip(inverse, square_parts)]
    inverse = [x + mm(x, s) for x, s in zip(inverse, fourth)]
    shift = 3
    while (1 << shift) < SPAN:
        corner = ((r >> (shift + 1)) == (c >> (shift + 1))) & ((r >> shift) != (c >> shift))
        parts = [halves(x) for x in inverse]
        moved = [
            dot_parts(halves(jnp.where(corner, a, 0.0)), x, NN) for a, x in zip(lowers, parts)
        ]
        inverse = [
            x - dot_parts(p, halves(m), NN) for x, p, m in zip(inverse, parts, moved)
        ]
        shift += 1
    return inverse


def chunk(n):
    return slice(n * SPAN, (n + 1) * SPAN)


def lanes(index, width=128):
    return slice(index * width, (index + 1) * width)


def row_scale(values):
    return lax.rsqrt(jnp.sum(values * values, axis=1, keepdims=True) + EPSILON)


def decay_terms(n, small, bias, rate, first, second):
    betas = jax.nn.sigmoid(small)
    decays = -rate * softplus(small + bias)
    r, c = iota((SPAN, SPAN), 0), iota((SPAN, SPAN), 1)
    total = mm_exact(jnp.where(c <= r, 1.0, 0.0), decays)
    turned = total.T
    position = iota((SPAN, 1), 0) + n * SPAN
    own = segment(position, first, second)
    ends = jnp.int32(n * SPAN + SPAN - 1)
    last = own == segment(ends, first, second)
    terms = []
    for h in range(HEADS):
        column = total[:, HEADS + h : HEADS + h + 1]
        if n:
            carried = own == segment(jnp.int32(n * SPAN - 1), first, second)
            growth = jnp.where(carried, jnp.exp(column), 0.0)
        else:
            growth = jnp.zeros((SPAN, 1), F32)
        final = column[SPAN - 1 : SPAN]
        fade = jnp.where(last, jnp.exp(jnp.where(last, final - column, 0.0)), 0.0)
        terms.append((betas[:, h : h + 1], column, turned[HEADS + h : HEADS + h + 1], growth, fade))
    return terms


def same_segment(n, first, second):
    r, c = iota((SPAN, SPAN), 0), iota((SPAN, SPAN), 1)
    base = n * SPAN
    return (segment(r + base, first, second) == segment(c + base, first, second)) & (c <= r)


def mixer_forward_kernel(
    bounds, raw, taps, vectors, gain, gated, conv, ratios, inner, scores, solved, written, states, mixed
):
    first, second = bounds[0], bounds[1]
    bias, rate = vectors[0:1], vectors[1:2]
    queries, keys, values, terms = {}, {}, {}, {}
    for n in range(CHUNKS):
        rows = chunk(n)
        position = iota((SPAN, 1), 0) + n * SPAN
        own = segment(position, first, second)
        joins = [
            jnp.where((position >= o) & (segment(position - o, first, second) == own), 1.0, 0.0)
            for o in range(1, CONV)
        ]

        def convolved(block):
            here = raw[rows, lanes(GATE_BLOCKS + block)]
            summed = here * taps[CONV - 1 : CONV, lanes(block)]
            for o in range(1, CONV):
                if n:
                    moved = raw[n * SPAN - o : (n + 1) * SPAN - o, lanes(GATE_BLOCKS + block)]
                else:
                    moved = pltpu.roll(here, o, 0)
                tap = taps[CONV - 1 - o : CONV - o, lanes(block)]
                summed = summed + tap * (moved * joins[o - 1])
            conv[rows, lanes(block)] = summed
            return silu(summed)

        for h in range(HEADS):
            q = convolved(Q_BLOCK + h)
            queries[n, h] = q * (row_scale(q) * DK ** (-0.5))
            k = convolved(K_BLOCK + h)
            keys[n, h] = k * row_scale(k)
            values[n, h] = jnp.concatenate(
                [convolved(2 * h), convolved(2 * h + 1)], axis=1
            )
        small = raw[rows, SMALL_AT:PROJ]
        for h, term in enumerate(decay_terms(n, small, bias, rate, first, second)):
            terms[n, h] = term

    r, c = iota((SPAN, SPAN), 0), iota((SPAN, SPAN), 1)
    key_parts = {p: halves(keys[p]) for p in PAIRS}
    query_parts = {p: halves(queries[p]) for p in PAIRS}
    lowers, score = [], {}
    for n in range(CHUNKS):
        causal = same_segment(n, first, second)
        for h in range(HEADS):
            p = (n, h)
            beta, column, row, growth, fade = terms[p]
            ratio = jnp.where(causal, jnp.exp(jnp.where(causal, column - row, 0.0)), 0.0)
            met = dot_parts(key_parts[p], key_parts[p], NT)
            lower = jnp.where(c < r, ratio * met, 0.0)
            score[p] = ratio * dot_parts(query_parts[p], key_parts[p], NT)
            at = n * HEADS + h
            ratios[at] = ratio
            inner[at] = lower
            scores[at] = score[p]
            lowers.append(beta * lower)
    inverses = invert_all(lowers)
    own_part, state_part, key_fade = {}, {}, {}
    for p, x in zip(PAIRS, inverses):
        n, h = p
        beta, column, row, growth, fade = terms[p]
        solved[n * HEADS + h] = x
        parts = halves(x)
        own_part[p] = dot_parts(parts, halves(beta * values[p]), NN)
        state_part[p] = halves(dot_parts(parts, halves((beta * growth) * keys[p]), NN))
        key_fade[p] = halves((fade * keys[p]).T)
    held = [jnp.zeros((DK, DV), F32) for h in range(HEADS)]
    for n in range(CHUNKS):
        for h in range(HEADS):
            p = (n, h)
            growth = terms[p][3]
            states[n * HEADS + h] = held[h]
            state = halves(held[h])
            wrote = own_part[p] - dot_parts(state_part[p], state, NN)
            wrote_parts = halves(wrote)
            written[chunk(n), lanes(h, DV)] = wrote
            out = growth * dot_parts(query_parts[p], state, NN)
            out = out + dot_parts(halves(score[p]), wrote_parts, NN)
            held[h] = growth[SPAN - 1 : SPAN] * held[h] + dot_parts(key_fade[p], wrote_parts, NN)
            mixed[chunk(n), lanes(h, DV)] = out
            scale = lax.rsqrt(jnp.mean(out * out, axis=1, keepdims=True) + MIXER_FLOOR)
            gate = raw[chunk(n), lanes(h, DV)]
            gated[chunk(n), lanes(h, DV)] = (out * scale * gain[...] * silu(gate)).astype(BF16)


def mixer_backward_kernel(
    bounds, grad_mixed, raw, taps, vectors, conv, ratios, inner, scores, solved, written, states,
    grad_raw, grad_taps, grad_vectors, slopes,
):
    first, second = bounds[0], bounds[1]
    bias, rate = vectors[0:1], vectors[1:2]
    r, c = iota((SPAN, SPAN), 0), iota((SPAN, SPAN), 1)
    lane = iota((SPAN, SMALL), 1)
    terms, queries, keys, values, grad_out = {}, {}, {}, {}, {}
    for n in range(CHUNKS):
        rows = chunk(n)
        small = raw[rows, SMALL_AT:PROJ]
        for h, term in enumerate(decay_terms(n, small, bias, rate, first, second)):
            p = (n, h)
            terms[p] = term
            q = silu(conv[rows, lanes(Q_BLOCK + h)])
            queries[p] = q * (row_scale(q) * DK ** (-0.5))
            k = silu(conv[rows, lanes(K_BLOCK + h)])
            keys[p] = k * row_scale(k)
            values[p] = silu(conv[rows, lanes(h, DV)])
            grad_out[p] = grad_mixed[rows, lanes(h, DV)]

    from_out, from_state, into_state, key_turned, out_parts = {}, {}, {}, {}, {}
    for p in PAIRS:
        n, h = p
        at = n * HEADS + h
        beta, column, row, growth, fade = terms[p]
        turned = halves(solved[at].T)
        out_parts[p] = halves(grad_out[p])
        pulled = dot_parts(halves(scores[at].T), out_parts[p], NN)
        from_out[p] = dot_parts(turned, halves(pulled), NN)
        from_state[p] = halves(dot_parts(turned, halves(fade * keys[p]), NN))
        into_state[p] = mm(queries[p].T, growth * grad_out[p])
        key_turned[p] = halves(((beta * growth) * keys[p]).T)
    held = [jnp.zeros((DK, DV), F32) for h in range(HEADS)]
    grad_target, grad_held, grad_held_parts = {}, {}, {}
    for n in reversed(range(CHUNKS)):
        for h in range(HEADS):
            p = (n, h)
            growth = terms[p][3]
            grad_held[p] = held[h]
            grad_held_parts[p] = halves(held[h])
            target = from_out[p] + dot_parts(from_state[p], grad_held_parts[p], NN)
            grad_target[p] = halves(target), target
            kept = growth[SPAN - 1 : SPAN] * held[h] + into_state[p]
            held[h] = kept - dot_parts(key_turned[p], grad_target[p][0], NN)

    log_sum = jnp.zeros((1, SMALL), F32)
    bias_sum = jnp.zeros((1, SMALL), F32)
    for n in range(CHUNKS):
        rows = chunk(n)
        grad_total = jnp.zeros((SPAN, SMALL), F32)
        grad_beta = jnp.zeros((SPAN, SMALL), F32)
        for h in range(HEADS):
            p = (n, h)
            at = n * HEADS + h
            beta, column, row, growth, fade = terms[p]
            target_parts, target = grad_target[p]
            state = states[at]
            state_parts = halves(state)
            wrote_parts = halves(written[rows, lanes(h, DV)])
            q, k, v = queries[p], keys[p], values[p]
            q_parts, k_parts = halves(q), halves(k)
            score, lower, ratio = scores[at], inner[at], ratios[at]
            out_state = dot_parts(out_parts[p], state_parts, NT)
            target_state = dot_parts(target_parts, state_parts, NT)
            wrote_state = dot_parts(wrote_parts, grad_held_parts[p], NT)
            grad_score = dot_parts(out_parts[p], wrote_parts, NT)
            grad_lower = -dot_parts(target_parts, wrote_parts, NT)
            grad_met = beta * grad_lower * jnp.where(c < r, ratio, 0.0)
            grad_pair = grad_score * ratio
            recall = jnp.sum(target_state * k, axis=1, keepdims=True)
            grad_growth = jnp.sum(out_state * q, axis=1, keepdims=True) - beta * recall
            beta_col = jnp.sum(target * v, axis=1, keepdims=True) - growth * recall
            beta_col = beta_col + jnp.sum(grad_lower * lower, axis=1, keepdims=True)
            faded = jnp.sum(wrote_state * k, axis=1, keepdims=True) * fade
            grad_q = growth * out_state + dot_parts(halves(grad_pair), k_parts, NN)
            grad_k = fade * wrote_state - (beta * growth) * target_state
            grad_k = grad_k + dot_parts(halves(grad_pair.T), q_parts, NN)
            grad_k = grad_k + dot_parts(halves(grad_met + grad_met.T), k_parts, NN)
            grad_v = beta * target
            held_grad = jnp.sum(state * grad_held[p], axis=1, keepdims=True)
            at_end = jnp.sum(held_grad, axis=0, keepdims=True) * growth[SPAN - 1 : SPAN]
            at_end = at_end + jnp.sum(faded, axis=0, keepdims=True)
            moved = grad_score * score + beta * (grad_lower * lower)
            col = jnp.sum(moved, axis=1, keepdims=True) - jnp.sum(moved.T, axis=1, keepdims=True)
            col = col + grad_growth * growth - faded
            col = col + jnp.where(iota((SPAN, 1), 0) == SPAN - 1, at_end, 0.0)
            grad_total = jnp.where(lane == HEADS + h, col, grad_total)
            grad_beta = jnp.where(lane == h, beta_col, grad_beta)
            pre = conv[rows, lanes(Q_BLOCK + h)]
            raw_q = silu(pre)
            scale = row_scale(raw_q)
            along = jnp.sum(grad_q * raw_q, axis=1, keepdims=True)
            back = (grad_q - raw_q * ((scale * scale) * along)) * (scale * DK ** (-0.5))
            slopes[rows, lanes(Q_BLOCK + h)] = back * silu_slope(pre)
            pre = conv[rows, lanes(K_BLOCK + h)]
            raw_k = silu(pre)
            scale = row_scale(raw_k)
            along = jnp.sum(grad_k * raw_k, axis=1, keepdims=True)
            back = (grad_k - raw_k * ((scale * scale) * along)) * scale
            slopes[rows, lanes(K_BLOCK + h)] = back * silu_slope(pre)
            wide = lanes(h, DV)
            slopes[rows, wide] = grad_v * silu_slope(conv[rows, wide])
        grad_decays = mm_exact(jnp.where(c >= r, 1.0, 0.0), grad_total)
        small = raw[rows, SMALL_AT:PROJ]
        shifted = small + bias
        grad_step = -grad_decays * rate * jax.nn.sigmoid(shifted)
        betas = jax.nn.sigmoid(small)
        grad_raw[rows, CONVW : CONVW + SMALL] = (
            grad_beta * betas * (1.0 - betas) + grad_step
        ).astype(BF16)
        bias_sum = bias_sum + jnp.sum(grad_step, axis=0, keepdims=True)
        log_sum = log_sum - jnp.sum(
            grad_decays * rate * softplus(shifted), axis=0, keepdims=True
        )
    grad_vectors[0:1] = log_sum
    grad_vectors[1:2] = bias_sum

    slopes[ROWS : ROWS + 8] = jnp.zeros((8, CONVW), F32)
    for block in range(CONVW // 128):
        sums = [jnp.zeros((1, 128), F32) for o in range(CONV)]
        for n in range(CHUNKS):
            rows = chunk(n)
            position = iota((SPAN, 1), 0) + n * SPAN
            own = segment(position, first, second)
            here = raw[rows, lanes(GATE_BLOCKS + block)]
            total = jnp.zeros((SPAN, 128), F32)
            for o in range(CONV):
                moved = slopes[n * SPAN + o : (n + 1) * SPAN + o, lanes(block)]
                if o:
                    moved = jnp.where(segment(position + o, first, second) == own, moved, 0.0)
                total = total + taps[CONV - 1 - o : CONV - o, lanes(block)] * moved
                sums[o] = sums[o] + jnp.sum(moved * here, axis=0, keepdims=True)
            grad_raw[rows, lanes(block)] = total.astype(BF16)
        for o in range(CONV):
            grad_taps[CONV - 1 - o : CONV - o, lanes(block)] = sums[o]


def lasting(micros):
    return pl.CostEstimate(
        flops=int(micros * 1e9), transcendentals=0, bytes_accessed=int(micros * 3e6)
    )


def vmem(count):
    return [pl.BlockSpec(memory_space=pltpu.VMEM)] * count


LIMIT = pltpu.CompilerParams(vmem_limit_bytes=56 * 1024 * 1024)
SMEM = pl.BlockSpec(memory_space=pltpu.SMEM)
SAVED = [
    jax.ShapeDtypeStruct((ROWS, CONVW), F32),
    jax.ShapeDtypeStruct((len(PAIRS), SPAN, SPAN), F32),
    jax.ShapeDtypeStruct((len(PAIRS), SPAN, SPAN), F32),
    jax.ShapeDtypeStruct((len(PAIRS), SPAN, SPAN), F32),
    jax.ShapeDtypeStruct((len(PAIRS), SPAN, SPAN), F32),
    jax.ShapeDtypeStruct((ROWS, VW), F32),
    jax.ShapeDtypeStruct((len(PAIRS), DK, DV), F32),
    jax.ShapeDtypeStruct((ROWS, VW), F32),
]


def mixer_forward(bounds, raw, taps, vectors, gain):
    outs = [jax.ShapeDtypeStruct((ROWS, VW), BF16)] + SAVED
    return pl.pallas_call(
        mixer_forward_kernel,
        out_shape=outs,
        in_specs=[SMEM] + vmem(4),
        out_specs=vmem(len(outs)),
        compiler_params=LIMIT,
        cost_estimate=lasting(12.5),
        name="mixer_forward",
    )(bounds, raw, taps, vectors, gain)


def mixer_backward(bounds, grad_mixed, raw, taps, vectors, saved):
    outs = [
        jax.ShapeDtypeStruct((ROWS, CONVW + SMALL), BF16),
        jax.ShapeDtypeStruct((8, CONVW), F32),
        jax.ShapeDtypeStruct((8, SMALL), F32),
    ]
    return pl.pallas_call(
        mixer_backward_kernel,
        out_shape=outs,
        in_specs=[SMEM] + vmem(4 + len(saved)),
        out_specs=vmem(len(outs)),
        scratch_shapes=[pltpu.VMEM((ROWS + 8, CONVW), F32)],
        compiler_params=LIMIT,
        cost_estimate=lasting(18.5),
        name="mixer_backward",
    )(bounds, grad_mixed, raw, taps, vectors, *saved)


TN = ((0,), (0,))
OWN = ROWS // 4
TILE = 512
STEP = 512
WIDE = 384
HALF = 1024
FIRST = 768
EARLY = 512


def whole(*shape):
    return pl.BlockSpec(shape, lambda i: (0,) * len(shape))


def place_rows(places, j):
    return pl.ds(pl.multiple_of(places[j] * OWN, OWN), OWN)


def project_kernel(places, x0, x1, x2, x3, small, weights, raw, normed, gains, steps):
    step = pl.program_id(0)

    @pl.when(step == 0)
    def prepare():
        r, c = iota((8, SMALL), 0), iota((8, SMALL), 1)
        pick = jnp.where((r < 2) & (c == r + 2 * HEADS), 1.0, 0.0).astype(BF16)
        gains[...] = contract(pick, small[...], NT)
        for j, x in enumerate((x0, x1, x2, x3)):
            values = x[...].astype(F32)
            scale = lax.rsqrt(jnp.mean(values * values, axis=1, keepdims=True) + EPSILON)
            low = (values * scale * gains[0:1]).astype(BF16)
            rows = place_rows(places, j)
            normed[rows, :] = low
            for s in range(steps.shape[0]):
                steps[s, rows, :] = low[:, s * STEP : (s + 1) * STEP]

    product = contract(steps[step], weights[:, VW:], NN)

    @pl.when(step == 0)
    def start():
        raw[...] = product

    @pl.when(step > 0)
    def add():
        raw[...] += product


def project(places, blocks, weights):
    features = weights.shape[0]
    count = features // STEP
    return pl.pallas_call(
        project_kernel,
        grid=(count,),
        out_shape=[
            jax.ShapeDtypeStruct((ROWS, PROJ), F32),
            jax.ShapeDtypeStruct((ROWS, features), BF16),
            jax.ShapeDtypeStruct((8, features), F32),
        ],
        in_specs=[SMEM]
        + [whole(OWN, features)] * 4
        + [
            pl.BlockSpec((features, SMALL), lambda i: (0, (VW + SMALL_AT) // SMALL)),
            pl.BlockSpec((STEP, VW + PROJ), lambda i: (i, 0)),
        ],
        out_specs=[whole(ROWS, PROJ), whole(ROWS, features), whole(8, features)],
        scratch_shapes=[pltpu.VMEM((count, ROWS, STEP), BF16)],
        compiler_params=LIMIT,
        cost_estimate=lasting(12),
        name="project",
    )(places, *blocks, weights, weights)


def split_rows(product, kept_other, sent_other, kept_own, sent_own):
    kept_own[...] = product[:OWN]
    sent_own[...] = product[OWN : 2 * OWN].astype(BF16)
    kept_other[...] = product[2 * OWN : 3 * OWN]
    sent_other[...] = product[3 * OWN :].astype(BF16)


def split_outs(features):
    shape = (OWN, features)
    pair = [jax.ShapeDtypeStruct(shape, F32), jax.ShapeDtypeStruct(shape, BF16)]
    return pair * 2, [pl.BlockSpec((OWN, TILE), lambda i: (0, i))] * 4


def mix_out_kernel(places, gated, weights, kept_other, sent_other, kept_own, sent_own, turned):
    @pl.when(pl.program_id(0) == 0)
    def prepare():
        for j in range(4):
            turned[j * OWN : (j + 1) * OWN] = gated[place_rows(places, j), :]

    split_rows(
        contract(turned[...], weights[...], NT), kept_other, sent_other, kept_own, sent_own
    )


def mix_out(places, gated, weights):
    features = weights.shape[0]
    outs, specs = split_outs(features)
    return pl.pallas_call(
        mix_out_kernel,
        grid=(features // TILE,),
        out_shape=outs + [jax.ShapeDtypeStruct((ROWS, VW), BF16)],
        in_specs=[SMEM, whole(ROWS, VW), pl.BlockSpec((TILE, VW), lambda i: (i, 0))],
        out_specs=specs + [whole(ROWS, VW)],
        compiler_params=LIMIT,
        cost_estimate=lasting(5),
        name="mix_out",
    )(places, gated, weights)


def gate_up_kernel(x0, x1, x2, x3, weights, act, gate, up, rows, held, *, units):
    step = pl.program_id(0)

    for j, x in enumerate((x0, x1, x2, x3)):

        @pl.when(step == 0)
        def prepare():
            held[j * OWN : (j + 1) * OWN] = x[...]

        @pl.when(step == j)
        def keep():
            rows[...] = x[...]

    for q in range(WIDE // 128):

        @pl.when(step * WIDE + q * 128 < units)
        def pair():
            product = contract(held[...], weights[:, lanes(q, 256)], NN)
            gate_in, up_in = product[:, :128], product[:, 128:]
            gate[:, lanes(q)] = gate_in
            up[:, lanes(q)] = up_in
            act[:, lanes(q)] = (silu(gate_in) * up_in).astype(BF16)


def gate_up(blocks, weights, units):
    features = weights.shape[0]
    tile = pl.BlockSpec((ROWS, WIDE), lambda i: (0, i))
    return pl.pallas_call(
        partial(gate_up_kernel, units=units),
        grid=(pl.cdiv(units, WIDE),),
        out_shape=[
            jax.ShapeDtypeStruct((ROWS, units), BF16),
            jax.ShapeDtypeStruct((ROWS, units), F32),
            jax.ShapeDtypeStruct((ROWS, units), F32),
            jax.ShapeDtypeStruct((ROWS, features), BF16),
        ],
        in_specs=[whole(OWN, features)] * 4
        + [pl.BlockSpec((features, 2 * WIDE), lambda i: (0, i))],
        out_specs=[
            tile,
            tile,
            tile,
            pl.BlockSpec((OWN, features), lambda i: (jnp.minimum(i, 3), 0)),
        ],
        scratch_shapes=[pltpu.VMEM((ROWS, features), BF16)],
        compiler_params=LIMIT,
        cost_estimate=lasting(12.5),
        name="gate_up",
    )(*blocks, weights)


def half_back_kernel(left, weights, kept, sent):
    product = contract(left[...], weights[...], NT)
    kept[...] = product[:OWN]
    sent[...] = product[OWN:].astype(BF16)


def half_back(left, part, weights, block, tile, micros, name):
    features = weights.shape[0]
    width = left.shape[1]
    shape = (OWN, features)
    return pl.pallas_call(
        half_back_kernel,
        grid=(features // tile,),
        out_shape=[jax.ShapeDtypeStruct(shape, F32), jax.ShapeDtypeStruct(shape, BF16)],
        in_specs=[
            pl.BlockSpec((2 * OWN, width), lambda i: (part, 0)),
            pl.BlockSpec((tile, width), lambda i: (i, block)),
        ],
        out_specs=[pl.BlockSpec((OWN, tile), lambda i: (0, i))] * 2,
        compiler_params=LIMIT,
        cost_estimate=lasting(micros),
        name=name,
    )(left, weights)


def down_first_kernel(left, low, early, late, *refs):
    *high, kept, sent, weights = refs
    for b in range(low.shape[0] // 64):
        own = slice(b * 128, b * 128 + 64)
        other = slice(b * 128 + 64, b * 128 + 128)
        part = slice(b * 64, b * 64 + 64)
        weights[own, :HALF] = low[part]
        weights[other, :FIRST] = early[part]
        weights[other, FIRST:HALF] = late[part]
    for i, block in enumerate(high):
        weights[:, HALF + i * 128 : HALF + (i + 1) * 128] = block[...]
    product = contract(left[...], weights[...], NT)
    kept[...] = product[:OWN]
    sent[...] = product[OWN:].astype(BF16)


def down_first(left, part, low, early, late, full):
    features = full.shape[0]
    width = left.shape[1]
    tile = 2 * STEP
    shape = (OWN, features)
    parts = [
        pl.BlockSpec((tile // 2, half.shape[1]), lambda i: (i, 0)) for half in (low, early, late)
    ]
    column = pl.BlockSpec((OWN, tile), lambda i: (0, i))
    blocks = range((full.shape[1] + HALF - width) // 128, full.shape[1] // 128)
    return pl.pallas_call(
        down_first_kernel,
        grid=(features // tile,),
        out_shape=[
            jax.ShapeDtypeStruct(shape, F32),
            jax.ShapeDtypeStruct(shape, BF16),
            jax.ShapeDtypeStruct((features, width), BF16),
        ],
        in_specs=[pl.BlockSpec((2 * OWN, width), lambda i: (part, 0))]
        + parts
        + [pl.BlockSpec((tile, 128), partial(lambda b, i: (i, b), b)) for b in blocks],
        out_specs=[column, column, pl.BlockSpec((tile, width), lambda i: (i, 0))],
        compiler_params=LIMIT,
        cost_estimate=lasting(6),
        name="down_first",
    )(left, low, early, late, *[full] * len(blocks))


def act_back_kernel(x0, x1, weights, gate, up, grads, rows, steps, total, gates, ups):
    step = pl.program_id(0)

    for j, x in enumerate((x0, x1)):
        at = slice(j * OWN, (j + 1) * OWN)

        @pl.when(step == 0)
        def prepare():
            for s in range(steps.shape[0]):
                steps[s, at, :] = x[:, s * STEP : (s + 1) * STEP]

        @pl.when(step == j)
        def keep():
            rows[...] = x[...]
            gates[at] = gate[...]
            ups[at] = up[...]

    product = contract(steps[step], weights[...], NN)

    @pl.when(step == 0)
    def start():
        total[...] = product

    @pl.when(step > 0)
    def add():
        total[...] += product

    @pl.when(step == pl.num_programs(0) - 1)
    def finish():
        for b in range(total.shape[1] // 128):
            grad, gate_in, up_in = total[:, lanes(b)], gates[:, lanes(b)], ups[:, lanes(b)]
            s = jax.nn.sigmoid(gate_in)
            grads[:, lanes(2 * b)] = (grad * up_in * s * (1.0 + gate_in * (1.0 - s))).astype(BF16)
            grads[:, lanes(2 * b + 1)] = (grad * gate_in * s).astype(BF16)


def act_back(blocks, part, weights, block, gate, up):
    features = weights.shape[0]
    units = gate.shape[1]
    count = features // STEP
    rows = pl.BlockSpec((OWN, units), lambda i: (2 * part + jnp.minimum(i, 1), 0))
    return pl.pallas_call(
        act_back_kernel,
        grid=(count,),
        out_shape=[
            jax.ShapeDtypeStruct((2 * OWN, 2 * units), BF16),
            jax.ShapeDtypeStruct((2 * OWN, features), BF16),
        ],
        in_specs=[whole(OWN, features)] * 2
        + [pl.BlockSpec((STEP, units), lambda i: (i, block)), rows, rows],
        out_specs=[
            whole(2 * OWN, 2 * units),
            pl.BlockSpec((OWN, features), lambda i: (jnp.minimum(i, 1), 0)),
        ],
        scratch_shapes=[
            pltpu.VMEM((count, 2 * OWN, STEP), BF16),
            pltpu.VMEM((2 * OWN, units), F32),
            pltpu.VMEM((2 * OWN, units), F32),
            pltpu.VMEM((2 * OWN, units), F32),
        ],
        compiler_params=LIMIT,
        cost_estimate=lasting(8),
        name="act_back",
    )(*blocks, weights, gate, up)


def gated_back_kernel(
    places, x0, x1, x2, x3, weights, raw_gate, mixed, gain, grad_mixed, grad_gate, grad_gain, turned
):
    gain_sum = jnp.zeros((1, DV), F32)
    for j, x in enumerate((x0, x1, x2, x3)):
        turned[j * OWN : (j + 1) * OWN] = x[...]
        grads = contract(x[...], weights[...], NN)
        rows = place_rows(places, j)
        for h in range(HEADS):
            out = mixed[rows, lanes(h, DV)]
            gate = raw_gate[rows, lanes(h, DV)]
            grad = grads[:, lanes(h, DV)]
            scale = lax.rsqrt(jnp.mean(out * out, axis=1, keepdims=True) + MIXER_FLOOR)
            opened = grad * silu(gate)
            scaled = out * scale
            gain_sum = gain_sum + jnp.sum(opened * scaled, axis=0, keepdims=True)
            grad_gate[rows, lanes(h, DV)] = (
                grad * scaled * gain[...] * silu_slope(gate)
            ).astype(BF16)
            inward = opened * gain[...]
            along = jnp.mean(inward * out, axis=1, keepdims=True)
            grad_mixed[rows, lanes(h, DV)] = scale * inward - out * (
                (scale * scale * scale) * along
            )
    grad_gain[0:1] = gain_sum


def gated_back(places, blocks, weights, raw, mixed, gain):
    features = weights.shape[0]
    return pl.pallas_call(
        gated_back_kernel,
        grid=(1,),
        out_shape=[
            jax.ShapeDtypeStruct((ROWS, VW), F32),
            jax.ShapeDtypeStruct((ROWS, VW), BF16),
            jax.ShapeDtypeStruct((8, DV), F32),
            jax.ShapeDtypeStruct((ROWS, features), BF16),
        ],
        in_specs=[SMEM]
        + [whole(OWN, features)] * 4
        + [whole(features, VW), whole(ROWS, VW), whole(ROWS, VW), whole(1, DV)],
        out_specs=[whole(ROWS, VW), whole(ROWS, VW), whole(8, DV), whole(ROWS, features)],
        compiler_params=LIMIT,
        cost_estimate=lasting(6.5),
        name="gated_back",
    )(places, *blocks, weights, raw, mixed, gain)


def input_back_kernel(
    places, gate, conv, weights, kept_other, sent_other, kept_own, sent_own, turned
):
    @pl.when(pl.program_id(0) == 0)
    def prepare():
        for j in range(4):
            rows = place_rows(places, j)
            turned[j * OWN : (j + 1) * OWN, :VW] = gate[rows, :]
            turned[j * OWN : (j + 1) * OWN, VW:] = conv[rows, :]

    split_rows(
        contract(turned[...], weights[:, VW:], NT), kept_other, sent_other, kept_own, sent_own
    )


def input_back(places, gate, conv, weights):
    features = weights.shape[0]
    outs, specs = split_outs(features)
    return pl.pallas_call(
        input_back_kernel,
        grid=(features // TILE,),
        out_shape=outs,
        in_specs=[
            SMEM,
            whole(ROWS, VW),
            whole(ROWS, CONVW + SMALL),
            pl.BlockSpec((TILE, VW + PROJ), lambda i: (i, 0)),
        ],
        out_specs=specs,
        scratch_shapes=[pltpu.VMEM((ROWS, PROJ), BF16)],
        compiler_params=LIMIT,
        cost_estimate=lasting(8.5),
        name="input_back",
    )(places, gate, conv, weights)


def grads_kernel(counts, *refs):
    out = refs[-1]
    at, used = 0, 0
    for count in counts:
        total = contract(refs[used][...], refs[used + 1][...], TN)
        for i in range(1, count):
            total = total + contract(refs[used + 2 * i][...], refs[used + 2 * i + 1][...], TN)
        used += 2 * count
        width = total.shape[1]
        out[:, at : at + width] = total.astype(BF16)
        at += width


def weight_grads(groups, micros, name):
    operands, specs, counts, width = [], [], [], 0
    for group in groups:
        counts.append(len(group))
        for left, right in group:
            (left, part), (right, other) = left, right
            rows = min(left.shape[0], right.shape[0])
            operands += [left, right]
            specs += [
                pl.BlockSpec((rows, STEP), partial(lambda p, i: (p, i), part)),
                pl.BlockSpec((rows, right.shape[1]), partial(lambda p, i: (p, 0), other)),
            ]
        width += right.shape[1]
    features = groups[0][0][0][0].shape[1]
    return pl.pallas_call(
        partial(grads_kernel, counts),
        grid=(features // STEP,),
        out_shape=jax.ShapeDtypeStruct((features, width), BF16),
        in_specs=specs,
        out_specs=pl.BlockSpec((STEP, width), lambda i: (i, 0)),
        compiler_params=LIMIT,
        cost_estimate=lasting(micros),
        name=name,
    )(*operands)


def pack_kernel(*refs):
    out = refs[-1]
    at = 0
    for ref in refs[:-1]:
        out[:, at : at + ref.shape[1]] = ref[...]
        at += ref.shape[1]


def pack(*blocks):
    shape = (blocks[0].shape[0], sum(block.shape[1] for block in blocks))
    return pl.pallas_call(
        pack_kernel,
        out_shape=jax.ShapeDtypeStruct(shape, BF16),
        in_specs=vmem(len(blocks)),
        out_specs=pl.BlockSpec(memory_space=pltpu.VMEM),
        compiler_params=LIMIT,
        cost_estimate=lasting(1.7),
        name="pack",
    )(*blocks)


def pack_both_kernel(count, *refs):
    rows = refs[0].shape[0]
    out = refs[-1]
    at = 0
    for i in range(count):
        width = refs[2 * i].shape[1]
        out[:rows, at : at + width] = refs[2 * i][...]
        out[rows:, at : at + width] = refs[2 * i + 1][...]
        at += width
    for ref in refs[2 * count : -1]:
        half = ref.shape[1] // 2
        out[:rows, at : at + half] = ref[:, :half]
        out[rows:, at : at + half] = ref[:, half:]
        at += half


def pack_both(pairs, *halved):
    rows = pairs[0][0].shape[0]
    width = sum(own.shape[1] for own, other in pairs) + sum(b.shape[1] for b in halved) // 2
    operands = [block for pair in pairs for block in pair] + list(halved)
    return pl.pallas_call(
        partial(pack_both_kernel, len(pairs)),
        out_shape=jax.ShapeDtypeStruct((2 * rows, width), BF16),
        in_specs=vmem(len(operands)),
        out_specs=pl.BlockSpec(memory_space=pltpu.VMEM),
        compiler_params=LIMIT,
        cost_estimate=lasting(2),
        name="pack_both",
    )(*operands)


def down_part_kernel(left_a, right_a, left_b, right_b, own, other):
    product = contract(left_a[...], right_a[...], TN) + contract(left_b[...], right_b[...], TN)
    product = product.astype(BF16)
    for b in range(STEP // 128):
        own[b * 64 : b * 64 + 64] = product[b * 128 : b * 128 + 64]
        other[b * 64 : b * 64 + 64] = product[b * 128 + 64 : b * 128 + 128]


def down_part(near, far, act):
    features = near.shape[1]
    left = pl.BlockSpec((2 * OWN, STEP), lambda i: (0, i))
    return pl.pallas_call(
        down_part_kernel,
        grid=(features // STEP,),
        out_shape=[jax.ShapeDtypeStruct((features // 2, EARLY), BF16)] * 2,
        in_specs=[
            left,
            pl.BlockSpec((2 * OWN, EARLY), lambda i: (0, 0)),
            left,
            pl.BlockSpec((2 * OWN, EARLY), lambda i: (1, 0)),
        ],
        out_specs=[pl.BlockSpec((STEP // 2, EARLY), lambda i: (i, 0))] * 2,
        compiler_params=LIMIT,
        cost_estimate=lasting(3),
        name="down_part",
    )(near, act, far, act)


def last_grads_kernel(turned, gated, normed, gate, conv, near, far, act, own, other, out):
    here = normed[...]
    at = 0
    for left, right in ((turned[...], gated), (here, gate), (here, conv)):
        width = right.shape[1]
        out[:, at : at + width] = contract(left, right[...], TN).astype(BF16)
        at += width
    down = contract(near[...], act[: 2 * OWN, EARLY:], TN)
    down = down + contract(far[...], act[2 * OWN :, EARLY:], TN)
    out[:, at : at + down.shape[1]] = down.astype(BF16)
    at += down.shape[1]
    total = (own[...].astype(F32) + other[...].astype(F32)).astype(BF16)
    for b in range(STEP // 128):
        rows = slice(b * 64, b * 64 + 64)
        out[b * 128 : b * 128 + 64, at:] = total[rows, : EARLY // 2]
        out[b * 128 + 64 : b * 128 + 128, at:] = total[rows, EARLY // 2 :]


def last_grads(turned, gated, normed, gate, conv, near, far, act, own, other):
    features = normed.shape[1]
    width = VW + PROJ + act.shape[1] - EARLY // 2
    left = pl.BlockSpec((ROWS, STEP), lambda i: (0, i))
    half = pl.BlockSpec((2 * OWN, STEP), lambda i: (0, i))
    early = pl.BlockSpec((STEP // 2, EARLY), lambda i: (i, 0))
    return pl.pallas_call(
        last_grads_kernel,
        grid=(features // STEP,),
        out_shape=jax.ShapeDtypeStruct((features, width), BF16),
        in_specs=[
            left,
            whole(ROWS, VW),
            left,
            whole(ROWS, VW),
            whole(ROWS, CONVW + SMALL),
            half,
            half,
            whole(ROWS, act.shape[1]),
            early,
            early,
        ],
        out_specs=pl.BlockSpec((STEP, width), lambda i: (i, 0)),
        compiler_params=LIMIT,
        cost_estimate=lasting(13),
        name="last_grads",
    )(turned, gated, normed, gate, conv, near, far, act, own, other)


def finish_kernel(both, arrived, out, gate, value, query, key, beta, decay, down):
    rows = arrived.shape[0]

    def total(left, right):
        return both[:rows, left:right].astype(F32) + arrived[:, left:right].astype(F32)

    at = 0
    for ref in (out, gate, value, query, key):
        ref[...] = total(at, at + ref.shape[1])
        at += ref.shape[1]
    small = total(at, at + SMALL).T
    beta[...] = small[:HEADS]
    decay[...] = small[HEADS : 2 * HEADS]
    at += SMALL
    end = arrived.shape[1]
    down[:, : EARLY // 2] = both[:rows, end:].astype(F32)
    down[:, EARLY // 2 : EARLY] = both[rows:, end:].astype(F32)
    down[:, EARLY:] = total(at, end)


def finish(both, arrived, units):
    rows = arrived.shape[0]
    widths = (VW, VW, VW, QK, QK)
    return pl.pallas_call(
        finish_kernel,
        out_shape=[jax.ShapeDtypeStruct((rows, width), F32) for width in widths]
        + [jax.ShapeDtypeStruct((HEADS, rows), F32)] * 2
        + [jax.ShapeDtypeStruct((rows, units), F32)],
        in_specs=vmem(2),
        out_specs=vmem(8),
        compiler_params=LIMIT,
        cost_estimate=lasting(2),
        name="finish",
    )(both, arrived)


SWAP = [(0, 1), (1, 0)]
PLANE = ("z", "y")


def trade(values, axis):
    return lax.ppermute(values, axis, SWAP)


def gather_tokens(own):
    across = trade(own, "xh")
    return own, trade(own, "c"), across, trade(across, "c")


def scatter_tokens(kept_other, sent_other, kept_own, sent_own):
    other = kept_other + trade(sent_other, "c").astype(jnp.float32)
    own = kept_own + trade(sent_own, "c").astype(jnp.float32)
    return own + trade(other.astype(jnp.bfloat16), "xh").astype(jnp.float32)


def scatter_halves(far, near, operand):
    kept, sent = far
    low = (kept + trade(sent, "c").astype(jnp.float32)).astype(jnp.bfloat16)
    low, operand = lax.optimization_barrier((low, operand))
    kept, sent = near(operand)
    own = kept + trade(sent, "c").astype(jnp.float32)
    return own + trade(low, "xh").astype(jnp.float32)


def gather_plane(block):
    return lax.all_gather(block, PLANE, axis=0, tiled=False).reshape(-1, block.shape[1])


def scatter_grads(grads):
    both = lax.psum_scatter(grads, PLANE, scatter_dimension=0, tiled=True)
    both = both.reshape(2, -1, grads.shape[1])
    return both[0].astype(jnp.float32) + trade(both[1], "xl").astype(jnp.float32)


def features_in(rows):
    count = rows.shape[0]
    halves = rows.reshape(count, 2, -1)
    flip = lax.axis_index("xl") == 1
    first = jnp.where(flip, halves[:, 1], halves[:, 0]).reshape(count, 16, 64)
    second = jnp.where(flip, halves[:, 0], halves[:, 1]).reshape(count, 16, 64)
    return jnp.concatenate([first, second], axis=2).reshape(count, -1)


def features_out(rows):
    count = rows.shape[0]
    blocks = rows.reshape(count, 16, 2, 64)
    flip = lax.axis_index("xl") == 1
    first = blocks[:, :, 0].reshape(count, -1)
    second = blocks[:, :, 1].reshape(count, -1)
    low = jnp.where(flip, second, first)
    high = jnp.where(flip, first, second)
    return jnp.concatenate([low, high], axis=1)


def sum_over(values, axes):
    for axis in axes:
        size = lax.axis_size(axis)
        step = 1
        while step < size:
            values = values + lax.ppermute(values, axis, [(i, i ^ step) for i in range(size)])
            step *= 2
    return values


def shards(
    layer_input,
    teacher_out,
    lengths,
    norm1_gain,
    query_weight,
    key_weight,
    value_weight,
    output_gate,
    beta_weight,
    decay_weight,
    decay_log,
    step_bias,
    query_taps,
    key_taps,
    value_taps,
    mixer_gain,
    out_weight,
    norm2_gain,
    gate_weight,
    up_weight,
    down_weight,
):
    tok_rows = layer_input.shape[0]
    rows_dp = norm1_gain.shape[0]
    group_index = lax.axis_index("xl") * 16 + lax.axis_index("z") * 4 + lax.axis_index("y")
    half, core = lax.axis_index("xh"), lax.axis_index("c")
    tensor_index = half * 2 + core
    places = jnp.stack(
        [tensor_index, 2 * half + 1 - core, 2 - 2 * half + core, 3 - tensor_index]
    ).astype(jnp.int32)
    heads_here = decay_log.shape[0]
    own_lengths = lax.dynamic_index_in_dim(lengths, group_index, 0, keepdims=False)
    boundary = jnp.cumsum(own_lengths)
    own_rows = tensor_index * tok_rows + jnp.arange(tok_rows, dtype=jnp.int32)
    validity = (own_rows < boundary[-1]).astype(jnp.float32)[:, None]
    loss_scale = jnp.float32(128 * tok_rows) / jnp.sum(lengths).astype(jnp.float32)

    qk_width = query_taps.shape[1]
    v_width = value_taps.shape[1]
    f_width = gate_weight.shape[1]
    filler = jnp.zeros((rows_dp, SMALL - 2 * heads_here - 2), jnp.bfloat16)
    mixer_block = pack(out_weight, output_gate, value_weight, query_weight, key_weight)
    small_block = jnp.concatenate(
        [beta_weight, decay_weight, norm1_gain[:, None], norm2_gain[:, None], filler], axis=1
    )
    paired_units = jnp.stack(
        [gate_weight.reshape(rows_dp, -1, 128), up_weight.reshape(rows_dp, -1, 128)], axis=2
    ).reshape(rows_dp, 2 * f_width)
    mixer_full = gather_plane(
        pack_both(
            [(mixer_block, trade(mixer_block, "xl")), (small_block, trade(small_block, "xl"))],
            down_weight[:, :HALF],
        )
    )
    ffn_block = jnp.concatenate([paired_units, down_weight[:, HALF:]], axis=1)
    ffn_full = gather_plane(pack_both([(ffn_block, trade(ffn_block, "xl"))]))
    input_own = features_in(layer_input)
    teacher_own = features_in(teacher_out).astype(jnp.float32)
    conv_taps = jnp.concatenate([value_taps, query_taps, key_taps], axis=1).astype(jnp.float32)
    vectors = jnp.pad(
        jnp.stack([step_bias, jnp.exp(decay_log)]),
        ((0, 6), (heads_here, SMALL - 2 * heads_here)),
    )
    gain_mixer = mixer_gain.astype(jnp.float32)[None, :]

    mixer_full, *input_blocks = lax.optimization_barrier((mixer_full, *gather_tokens(input_own)))
    down_low = mixer_full[:, VW + PROJ :].reshape(16, 2, rows_dp, HALF // 2)
    down_low = down_low.swapaxes(1, 2).reshape(-1, HALF)
    low_first, low_last = down_low[:, :FIRST], down_low[:, FIRST:]
    low_first, mixer_full = lax.optimization_barrier((low_first, mixer_full))
    early = trade(low_first, "xl")
    raw, normed_one, gains = project(places, input_blocks, mixer_full)
    gain_first, gain_second = gains[0:1], gains[1:2]
    input_float = input_own.astype(jnp.float32)
    scale_one = lax.rsqrt(jnp.mean(input_float * input_float, axis=-1, keepdims=True) + EPSILON)
    gated_low, *saved, mixed = mixer_forward(boundary, raw, conv_taps, vectors, gain_mixer)
    gated_low, early = lax.optimization_barrier((gated_low, early))
    *terms, gated_turned = mix_out(places, gated_low, mixer_full)
    hidden = input_float + scatter_tokens(*terms)
    scale_two = lax.rsqrt(jnp.mean(hidden * hidden, axis=-1, keepdims=True) + EPSILON)
    normed_two = (hidden * scale_two * gain_second).astype(jnp.bfloat16)
    blocks = gather_tokens(normed_two)
    low_last, *blocks = lax.optimization_barrier((low_last, *blocks))
    late = trade(low_last, "xl")
    act_low, gate_in, up_in, normed_rows = gate_up(blocks, ffn_full, f_width)
    *far, down_full = down_first(act_low, 1, down_low, early, late, ffn_full)
    layer_out = hidden + scatter_halves(
        far, lambda act: half_back(act, 0, down_full, 0, 1024, 5, "down_near"), act_low
    )
    grad_layer = loss_scale * validity * (layer_out - teacher_own)
    grad_low = grad_layer.astype(jnp.bfloat16)
    across = trade(grad_low, "xh")
    grads_near, rows_near = act_back(
        (grad_low, trade(grad_low, "c")), 0, down_full, 0, gate_in, up_in
    )
    across, grads_near = lax.optimization_barrier((across, grads_near))
    grads_far, rows_far = act_back(
        (across, trade(across, "c")), 1, down_full, 0, gate_in, up_in
    )
    units_grad = weight_grads(
        [[((normed_rows, 0), (grads_near, 0)), ((normed_rows, 1), (grads_far, 0))]], 10.5, "units_grads"
    )
    units_grad, grads_far, grads_near = lax.optimization_barrier((units_grad, grads_far, grads_near))
    units_sum = scatter_grads(units_grad)
    far = half_back(grads_far, 0, ffn_full, 0, 512, 8, "normed_far")
    grad_normed_two = scatter_halves(
        far, lambda grads: half_back(grads, 0, ffn_full, 0, 512, 8, "normed_near"), grads_near
    )

    weighted_two = gain_second * grad_normed_two
    grad_gain_two = jnp.sum(grad_normed_two * hidden * scale_two, axis=0)
    grad_hidden = (
        grad_layer
        + scale_two * weighted_two
        - hidden
        * (scale_two * scale_two * scale_two)
        * jnp.mean(weighted_two * hidden, axis=-1, keepdims=True)
    )
    down_own, down_other = down_part(rows_near, rows_far, act_low)
    hidden_low = grad_hidden.astype(jnp.bfloat16)
    across = trade(hidden_low, "xh")
    across, down_other = lax.optimization_barrier((across, down_other))
    blocks = (hidden_low, trade(hidden_low, "c"), across, trade(across, "c"))
    down_across = trade(down_other, "xl")
    grad_mixed, gate_low, gain_grad, grad_turned = gated_back(
        places, blocks, mixer_full, raw, mixed, gain_mixer
    )
    raw_low, taps_grad, vectors_grad = mixer_backward(
        boundary, grad_mixed, raw, conv_taps, vectors, saved
    )
    last_grad = last_grads(
        grad_turned,
        gated_turned,
        normed_one,
        gate_low,
        raw_low,
        rows_near,
        rows_far,
        act_low,
        down_own,
        down_across,
    )
    last_grad, raw_low = lax.optimization_barrier((last_grad, raw_low))
    last_both = lax.psum_scatter(last_grad, PLANE, scatter_dimension=0, tiled=True)
    last_arrived = trade(last_both[rows_dp:, : last_grad.shape[1] - EARLY // 2], "xl")
    out_grad, gate_grad, value_grad, query_grad, key_grad, beta_grad, decay_grad, down_grad = finish(
        last_both, last_arrived, f_width
    )
    grad_normed_one = scatter_tokens(*input_back(places, gate_low, raw_low, mixer_full))
    weighted_one = gain_first * grad_normed_one
    grad_gain_one = jnp.sum(grad_normed_one * input_float * scale_one, axis=0)
    grad_input = (
        grad_hidden
        + scale_one * weighted_one
        - input_float
        * (scale_one * scale_one * scale_one)
        * jnp.mean(weighted_one * input_float, axis=-1, keepdims=True)
    )

    gain_pair = features_out(jnp.stack([grad_gain_one, grad_gain_two]))
    features = gain_pair.shape[1]
    taps = taps_grad[:CONV]
    n_all = 2 * features + DV
    flat = jnp.concatenate(
        [
            gain_pair.reshape(-1),
            gain_grad[0],
            taps.reshape(-1),
            vectors_grad[:2, heads_here : 2 * heads_here].reshape(-1),
        ]
    )
    flat = jnp.pad(flat, (0, -flat.shape[0] % 1024)).reshape(-1, 128)
    flat = sum_over(flat, ("xl", "z", "y"))
    shared = sum_over(flat[: n_all // 128], ("xh", "c")).reshape(-1)
    flat = flat.reshape(-1)
    taps_sum = flat[n_all : n_all + taps.size].reshape(CONV, -1)
    heads_at = n_all + taps.size
    norm1_grad = lax.dynamic_slice_in_dim(shared, group_index * rows_dp, rows_dp)
    norm2_grad = lax.dynamic_slice_in_dim(shared, features + group_index * rows_dp, rows_dp)
    units_sum = units_sum.reshape(rows_dp, -1, 2, 128)
    return (
        features_out(layer_out),
        features_out(grad_input),
        norm1_grad,
        query_grad,
        key_grad,
        value_grad,
        gate_grad,
        beta_grad.T,
        decay_grad.T,
        flat[heads_at : heads_at + heads_here],
        flat[heads_at + heads_here : heads_at + 2 * heads_here],
        taps_sum[:, v_width : v_width + qk_width],
        taps_sum[:, v_width + qk_width :],
        taps_sum[:, :v_width],
        shared[2 * features :],
        out_grad,
        norm2_grad,
        units_sum[:, :, 0].reshape(rows_dp, f_width),
        units_sum[:, :, 1].reshape(rows_dp, f_width),
        down_grad,
    )


def solution(mesh):
    fine = Mesh(mesh.devices.reshape(2, 4, 4, 2, 2), ("xl", "z", "y", "xh", "c"))
    dp = ("xl", "z", "y")
    tensor = ("xh", "c")
    tokens = P(dp + tensor, None)
    weight = P(dp, tensor)
    gain = P(dp)
    heads = P(tensor)
    taps = P(None, tensor)
    in_specs = (
        (tokens, tokens, P(), gain)
        + (weight,) * 6
        + (heads, heads, taps, taps, taps, P(), weight, gain)
        + (weight,) * 3
    )
    out_specs = (
        (tokens, tokens, gain)
        + (weight,) * 6
        + (heads, heads, taps, taps, taps, P(), weight, gain)
        + (weight,) * 3
    )
    return jax.shard_map(shards, mesh=fine, in_specs=in_specs, out_specs=out_specs, check_vma=False)
```
